32 devices in a mesh: seq: 8 (over z, y), mp: 4 (over x, core).
Axes of the slice: x: 2, y: 2, z: 4, core: 2. Of those that a mesh axis runs over, the one named last changes fastest.
Arguments:
- byte_hidden: bfloat16 [8192, 1024], P('seq', 'mp'), may hold values from -6 to 6
- patch_start: int32 [8192], P('seq'), may hold values from 0 to 1, as said below
- pool_query: bfloat16 [1024], P('mp'), may hold values from -4 to 4
- in_weight: bfloat16 [1024, 4096], P('seq', 'mp'), may hold values from -0.1875 to 0.1875
- latent_grad: bfloat16 [4096, 4096], P('seq', 'mp'), may hold values from -6 to 6
Outputs:
- latent: bfloat16 [4096, 4096], P('seq', 'mp')
- grad_weight: float32 [1024, 4096], P('seq', 'mp')
- grad_bytes: bfloat16 [8192, 1024], P('seq', 'mp')
The draws below stay inside these ranges and needn't reach their ends.
Inputs may be any that keep to these rules, and one draw needn't show every extreme that they name: `patch_start`: byte 0 begins a patch, and so does every byte whose position is 16 // 2 modulo 16; of the bytes 2k and 2k+1 at most one begins a patch. So no patch is longer than 16 bytes, and some patch is exactly 16 long. Each aligned block of 1024 bytes holds at most 512 patch starts, and one block holds exactly 512.
All inputs are finite; a program needn't handle non-finite values.
Results may differ from the reference program's by a relative error of at most 0.0049.
Values may be sent and summed in bfloat16 or wider, within the bound.
No kernel may reach another device: no remote copies, remote signals or barrier semaphores. Data moves between devices by JAX's collectives and lax.ppermute only.
A program may use at most 64 MiB of HBM per device.

```python
import math
import jax
import jax.numpy as jnp
from jax import lax

DL = 1024
DM = 4096
HEAD_DIM = 64
MAXLEN = 16
BYTE_DEV = 1024
PCAP = 512
BYTES = 8192
SLOTS = 4096
N_SEQ = 8
N_MP = 4


def draw_patch_start(key, part):
    key = jax.random.fold_in(key, 11)
    blocks = BYTES // BYTE_DEV
    pairs = BYTE_DEV // 2
    half_seg = MAXLEN // 2
    keys = jax.random.split(key, 6)
    rate = jax.random.randint(keys[0], (blocks, 1), 150, 600)
    dense = jax.random.randint(keys[1], (), 0, blocks)
    sparse = (dense + 1 + jax.random.randint(keys[2], (), 0, blocks - 1)) % blocks
    picked = jax.random.randint(keys[3], (blocks, pairs), 0, 1000) < rate
    odd_bit = jax.random.randint(keys[4], (blocks, pairs), 0, 2)
    window = jax.random.randint(keys[5], (), 0, BYTE_DEV // MAXLEN - 1)
    pair_index = jnp.arange(pairs)[None, :]
    block_index = jnp.arange(blocks)[:, None]
    forced = pair_index % half_seg == MAXLEN // 4
    first = (block_index == 0) & (pair_index == 0)
    window_pair = window * half_seg + MAXLEN // 4
    empty = (block_index == sparse) & (pair_index > window_pair) & (pair_index < window_pair + half_seg)
    present = (picked | (block_index == dense)) & jnp.logical_not(empty) | forced | first
    which = jnp.where(forced | first, 0, odd_bit)
    lower = present & (which == 0)
    upper = present & (which == 1)
    return jnp.stack([lower, upper], axis=-1).reshape(BYTES).astype(jnp.int32)


def raised(result, own_key, source, target, parts, factor):
    owner, partner = [(jnp.arange(result.shape[axis_at]) // (result.shape[axis_at] // parts)).reshape([-1 if axis == axis_at else 1 for axis in range(result.ndim)]) for axis_at in (source, target)]
    chosen = jax.random.permutation(own_key, parts)[partner]
    strong = (owner == chosen) | (owner == (partner + parts // 2) % parts)
    return jnp.where(strong, factor * result, result)


def levels(own_key, dims, cuts, smallest, high):
    def one(dim, shards_of):
        steps = jax.random.uniform(jax.random.fold_in(jax.random.fold_in(own_key, 6), dim), (shards_of,), jnp.float32, smallest / len(cuts), high / len(cuts))
        return jnp.repeat(jnp.exp(steps), dims[dim] // shards_of).reshape((-1,) + (1,) * (len(dims) - dim - 1))

    factor_of = one(*cuts[0])
    for cut in cuts[1:]:
        factor_of = factor_of * one(*cut)
    return factor_of


def noise(key, extent, scale, limit, cuts=(), kind=jnp.bfloat16):
    array = jax.random.normal(key, extent, jnp.float32) * scale
    if len(cuts) > 0:
        array = levels(key, extent, cuts, -0.22, 0.18) * array
    return jnp.clip(array, min=-limit, max=limit).astype(kind)


def heavy_noise(stream_key, extent, spread, limit, cuts, heavy, kind=jnp.bfloat16):
    array = spread * jax.random.normal(stream_key, extent, jnp.float32)
    if cuts:
        array = array * levels(stream_key, extent, cuts, -0.22, 0.18)
    return jnp.clip(raised(array, jax.random.fold_in(stream_key, 3), *heavy), -limit, limit).astype(kind)


def setup_inputs(seed: int = 0) -> dict:
    key_list = jax.random.split(jax.random.key(seed), 6)
    return {
        "byte_hidden": heavy_noise(key_list[0], (BYTES, DL), 1.0, 6.0, ((0, 8), (1, 4)), (0, 1, 8, 2.0)),
        "patch_start": draw_patch_start(jax.random.fold_in(key_list[5], 71), 0),
        "pool_query": noise(key_list[2], (DL,), 1.0, 4.0, ((0, 4),)),
        "in_weight": noise(key_list[3], (DL, DM), DL ** -0.5, 0.1875, ((0, 8), (1, 4))),
        "latent_grad": noise(key_list[4], (SLOTS, DM), 1.0, 6.0, ((0, 8), (1, 4))),
    }


soft_cap = 20.0

def reference(byte_hidden, patch_start, pool_query, in_weight, latent_grad):
    head_dim = HEAD_DIM
    heads = DL // head_dim
    slots = N_SEQ * PCAP
    inv_root = 1.0 / math.sqrt(head_dim)
    hidden_f = byte_hidden.astype(jnp.float32)
    query = pool_query.astype(jnp.float32)
    raw = (hidden_f * query).reshape(BYTES, heads, head_dim).sum(-1) * inv_root
    capped = soft_cap * jnp.tanh(raw / soft_cap)
    weight_exp = jnp.exp(capped)
    position = jnp.arange(BYTES, dtype=jnp.int32)
    patch_id = (jnp.cumsum(patch_start) - 1).astype(jnp.int32)
    start_pos = lax.cummax(jnp.where(patch_start > 0, position, 0).astype(jnp.int32), axis=0)
    owner = (start_pos // BYTE_DEV).astype(jnp.int32)
    counts = patch_start.reshape(N_SEQ, BYTE_DEV).sum(1).astype(jnp.int32)
    offsets = (jnp.cumsum(counts) - counts).astype(jnp.int32)
    slot = (owner * PCAP + patch_id - offsets[owner]).astype(jnp.int32)
    weighted = jnp.repeat(weight_exp, head_dim, axis=1) * hidden_f
    numer = jax.ops.segment_sum(weighted, slot, num_segments=slots)
    denom = jax.ops.segment_sum(weight_exp, slot, num_segments=slots)
    live = (jnp.arange(PCAP, dtype=jnp.int32)[None, :] < counts[:, None]).reshape(slots)
    safe = jnp.where(live[:, None], denom, jnp.float32(1.0))
    pooled = jnp.where(live[:, None], numer / jnp.repeat(safe, head_dim, axis=1), jnp.float32(0.0))
    pooled_low = pooled.astype(jnp.bfloat16)
    latent = jnp.dot(pooled_low, in_weight, preferred_element_type=jnp.float32).astype(jnp.bfloat16)
    quarter = DM // N_MP
    grad_pooled = jnp.zeros((slots, DL), jnp.float32)
    for index in range(N_MP):
        lower = index * quarter
        piece = lax.dot_general(latent_grad[:, lower:lower + quarter], in_weight[:, lower:lower + quarter], (((1,), (1,)), ((), ())), preferred_element_type=jnp.float32)
        piece = lax.optimization_barrier(piece.astype(jnp.bfloat16))
        grad_pooled = grad_pooled + piece.astype(jnp.float32)
    grad_weight = lax.dot_general(pooled_low, latent_grad, (((0,), (0,)), ((), ())), preferred_element_type=jnp.float32) * (1.0 / math.sqrt(slots))
    share = weight_exp / safe[slot]
    grad_rows = grad_pooled[slot]
    pooled_rows = pooled[slot]
    inner = (grad_rows * (hidden_f - pooled_rows)).reshape(BYTES, heads, head_dim).sum(-1)
    coeff = share * inner * (1.0 - (capped / soft_cap) ** 2) * inv_root
    grad_bytes = jnp.repeat(share, head_dim, axis=1) * grad_rows + jnp.repeat(coeff, head_dim, axis=1) * query
    return (latent, grad_weight, grad_bytes.astype(jnp.bfloat16))
```

```python
import functools
import math

import jax
import jax.numpy as jnp
from jax import lax
from jax.experimental import pallas as pl
from jax.experimental.pallas import tpu as pltpu
from jax.sharding import PartitionSpec as P

HEAD_DIM = 64
EDGE = 16
LANES = 128

soft_cap = 20.0
inv_root = 1.0 / math.sqrt(HEAD_DIM)
F32 = jnp.float32
BF16 = jnp.bfloat16
VMEM_LIMIT = 48 * 1024 * 1024
VMEM_MOST = 53 * 1024 * 1024


def iota(shape, dim):
    return lax.broadcasted_iota(jnp.int32, shape, dim)


def split(value):
    high = value.astype(BF16)
    return high, (value - high.astype(F32)).astype(BF16)


def dot(left, right, dims=((1,), (0,))):
    return lax.dot_general(left, right, (dims, ((), ())), preferred_element_type=F32)


def dot_split(left, value):
    high, low = split(value)
    return dot(left, high) + dot(left, low)


def head_sum(value):
    feats = value.shape[1]
    same = (iota((feats, feats), 0) // HEAD_DIM) == (iota((feats, feats), 1) // HEAD_DIM)
    block = jnp.where(same, 1.0, 0.0).astype(BF16)
    high, low = split(value)
    return dot(high, block) + dot(low, block)


def row_of(ref):
    value = ref[...].astype(F32)
    return jnp.concatenate([value[at : at + 1] for at in range(value.shape[0])], axis=1)


def scores(hidden, query):
    raw = head_sum(hidden * query) * inv_root
    bent = jnp.tanh(raw / soft_cap)
    return bent, jnp.exp(soft_cap * bent)


def segment_rows(start):
    upper = jnp.where(iota((LANES, LANES), 0) <= iota((LANES, LANES), 1), 1.0, 0.0).astype(BF16)
    count = dot(start.astype(F32).astype(BF16), upper)
    rows, total = [], jnp.full((1, 1), -1.0, F32)
    for index in range(start.shape[0]):
        row = count[index : index + 1]
        rows.append(row + total)
        total = total + row[:, LANES - 1 :]
    return rows, total


def lead_mask(start):
    first = jnp.broadcast_to(start[0:1].astype(F32), (EDGE, LANES))
    before = jnp.where(iota((EDGE, LANES), 1) <= iota((EDGE, LANES), 0), first, 0.0)
    return jnp.where(jnp.sum(before, axis=1, keepdims=True) > 0.0, 0.0, 1.0)


def tail_mask(start):
    rows = start.shape[0]
    last = jnp.broadcast_to(start[rows - 1 : rows].astype(F32), (EDGE, LANES))
    after = jnp.where(iota((EDGE, LANES), 1) > iota((EDGE, LANES), 0) + (LANES - EDGE), last, 0.0)
    return jnp.where(jnp.sum(after, axis=1, keepdims=True) > 0.0, 0.0, 1.0)


def load_kernel(hidden_hbm, start_hbm, grad_hbm,
                back_ref, ahead_ref, hidden_ref, start_ref, rows_v, sem):
    pairs = [(start_hbm, start_ref), (hidden_hbm, hidden_ref)]
    copies = [pltpu.make_async_copy(*pair, sem.at[at]) for at, pair in enumerate(pairs)]
    for copy in copies:
        copy.start()
    bytes_, feats = hidden_ref.shape
    width = grad_hbm.shape[1]
    copies[0].wait()
    start = start_ref[...]
    last = jnp.sum(start) - 1
    group = pl.multiple_of((last // EDGE) * EDGE, EDGE)
    rows = pltpu.make_async_copy(grad_hbm.at[pl.ds(group, EDGE), :], rows_v, sem.at[2])
    rows.start()
    back_ref[:, feats:] = jnp.broadcast_to(lead_mask(start), (EDGE, LANES)).astype(BF16)
    ahead_ref[:, width + feats :] = jnp.broadcast_to(tail_mask(start), (EDGE, LANES)).astype(BF16)
    copies[1].wait()
    back_ref[:, :feats] = hidden_ref[:EDGE]
    ahead_ref[:, width : width + feats] = hidden_ref[bytes_ - EDGE :]
    rows.wait()
    chosen = iota((EDGE, width), 0) == last - group
    ahead_ref[:, :width] = jnp.where(chosen, rows_v[...].astype(F32), 0.0).astype(BF16)


def pool_kernel(hidden_ref, next_ref, start_ref, query_ref, low_ref, pooled_ref, denom_ref):
    bytes_, feats = hidden_ref.shape
    slots = low_ref.shape[0]
    query = row_of(query_ref)
    rows, last = segment_rows(start_ref[...])
    segment = jnp.concatenate(rows, axis=1).astype(jnp.int32)
    onehot = jnp.where(iota((slots, bytes_), 0) == segment, 1.0, 0.0).astype(BF16)
    hidden = hidden_ref[...].astype(F32)
    _, weight = scores(hidden, query)
    numer = dot_split(onehot, weight * hidden)
    denom = dot_split(onehot, weight)
    following = next_ref[:, :feats].astype(F32)
    mask = next_ref[:, feats : feats + 1].astype(F32)
    extra = scores(following, query)[1] * mask
    is_last = iota((slots, feats), 0) == last.astype(jnp.int32)
    denom = denom + jnp.where(is_last, jnp.sum(extra, axis=0, keepdims=True), 0.0)
    numer = numer + jnp.where(is_last, jnp.sum(extra * following, axis=0, keepdims=True), 0.0)
    live = denom > 0.0
    pooled = jnp.where(live, numer / jnp.where(live, denom, 1.0), 0.0)
    low_ref[...] = pooled.astype(BF16)
    pooled_ref[...] = pooled
    denom_ref[...] = denom


def spread_kernel(hidden_ref, prev_ref, start_ref, query_ref, pooled_ref, denom_ref,
                  onehot_ref, share_ref, delta_ref, slope_ref):
    bytes_, feats = hidden_ref.shape
    slots = pooled_ref.shape[0]
    query = row_of(query_ref)
    rows, _ = segment_rows(start_ref[...])
    columns = [jnp.transpose(jnp.broadcast_to(row, (LANES, LANES))) for row in rows]
    segment = jnp.concatenate(columns, axis=0).astype(jnp.int32)
    onehot = jnp.concatenate(
        [
            jnp.where(segment == iota((bytes_, LANES), 1) + offset, 1.0, 0.0).astype(BF16)
            for offset in range(0, slots, LANES)
        ],
        axis=1,
    )
    onehot_ref[...] = onehot
    hidden = hidden_ref[...].astype(F32)
    bent, weight = scores(hidden, query)
    width = prev_ref.shape[1] - feats - LANES
    before = prev_ref[:, width : width + feats].astype(F32)
    part = scores(before, query)[1] * prev_ref[:, width + feats : width + feats + 1].astype(F32)
    lead = lead_mask(start_ref[...])
    own = weight[:EDGE] * lead
    first_denom = jnp.sum(part + own, axis=0, keepdims=True)
    first_numer = jnp.sum(part * before + own * hidden[:EDGE], axis=0, keepdims=True)
    full = first_denom > 0.0
    first_pooled = jnp.where(full, first_numer / jnp.where(full, first_denom, 1.0), 0.0)
    denom = dot_split(onehot, denom_ref[...])
    pooled = dot_split(onehot, pooled_ref[...])
    denom = jnp.concatenate([denom[:EDGE] + lead * first_denom, denom[EDGE:]], axis=0)
    pooled = jnp.concatenate([pooled[:EDGE] + lead * first_pooled, pooled[EDGE:]], axis=0)
    share = weight / denom
    share_ref[...] = share
    delta_ref[...] = hidden - pooled
    slope_ref[...] = share * (1.0 - bent * bent) * (inv_root * query)


def bytes_kernel(parts, *refs):
    recv_refs, (start_ref, onehot_ref, share_ref, delta_ref, slope_ref, out_ref) = (
        refs[:parts],
        refs[parts:],
    )
    slots = onehot_ref.shape[1]
    grad = recv_refs[0][...].astype(F32)
    for ref in recv_refs[1:]:
        grad = grad + ref[...].astype(F32)
    rows = dot_split(onehot_ref[...], grad[:slots])
    first = jnp.sum(grad[slots:], axis=0, keepdims=True)
    rows = jnp.concatenate([rows[:EDGE] + lead_mask(start_ref[...]) * first, rows[EDGE:]], axis=0)
    inner = head_sum(rows * delta_ref[...])
    out_ref[...] = (share_ref[...] * rows + slope_ref[...] * inner).astype(BF16)


def gather_parts(part_refs, full_ref):
    feats = part_refs[0].shape[1]
    place = lax.axis_index("mp")
    for index, ref in enumerate(part_refs):
        owner = pl.multiple_of((place ^ index) * feats, feats)
        full_ref[:, pl.ds(owner, feats)] = ref[...]


def outer_kernel(parts, scale, *refs):
    part_refs, grad_ref, out_refs = refs[:parts], refs[parts], refs[parts + 1 : -2]
    full_ref, terms_ref = refs[-2:]
    gather_parts(part_refs, full_ref)
    terms_ref[...] = dot(full_ref[...], grad_ref[...], ((0,), (0,))) * scale
    if len(out_refs) == 1:
        out_refs[0][...] = terms_ref[...].astype(out_refs[0].dtype)
        return
    place = lax.axis_index("seq")
    rows = out_refs[0].shape[0]
    for index, ref in enumerate(out_refs):
        owner = pl.multiple_of((place ^ index) * rows, rows)
        ref[...] = terms_ref[pl.ds(owner, rows), :].astype(ref.dtype)


def latent_kernel(parts, *refs):
    part_refs, (weight_ref, out_ref, full_ref) = refs[:parts], refs[parts:]
    gather_parts(part_refs, full_ref)
    out_ref[...] = dot(full_ref[...], weight_ref[...]).astype(BF16)


def partial_kernel(parts, grad_ref, prev_ref, *refs):
    piece_refs, out_refs, full_ref = refs[: -parts - 1], refs[-parts - 1 : -1], refs[-1]
    slots, width = grad_ref.shape
    feats = out_refs[0].shape[1]
    if len(piece_refs) == 1:
        full_ref[...] = piece_refs[0][...]
    else:
        rows = piece_refs[0].shape[0]
        spot = lax.axis_index("seq")
        for index, ref in enumerate(piece_refs):
            owner = pl.multiple_of((spot ^ index) * rows, rows)
            full_ref[pl.ds(owner, rows), :] = ref[...]
    place = lax.axis_index("mp")
    for index, ref in enumerate(out_refs):
        owner = pl.multiple_of((place ^ index) * feats, feats)
        block = full_ref[pl.ds(owner, feats), :]
        ref[:slots] = dot(grad_ref[...], block, ((1,), (1,))).astype(BF16)
        ref[slots:] = dot(prev_ref[:, :width], block, ((1,), (1,))).astype(BF16)


def call(kernel, out_shape, *args, flops=0, scratch=(), in_specs=None, limit=VMEM_LIMIT):
    if in_specs is None:
        in_specs = [pl.BlockSpec(memory_space=pltpu.VMEM)] * len(args)
    return pl.pallas_call(
        kernel,
        out_shape=out_shape,
        in_specs=in_specs,
        out_specs=jax.tree.map(lambda _: pl.BlockSpec(memory_space=pltpu.VMEM), out_shape),
        scratch_shapes=list(scratch),
        cost_estimate=pl.CostEstimate(flops=0, bytes_accessed=0, transcendentals=0),
        compiler_params=pltpu.CompilerParams(vmem_limit_bytes=limit),
    )(*args)


def shape(dims, dtype):
    return jax.ShapeDtypeStruct(dims, dtype)


VMEM = pl.BlockSpec(memory_space=pltpu.VMEM)
after = lax.optimization_barrier
HBM = pl.BlockSpec(memory_space=pltpu.HBM)


def shards(byte_hidden, patch_start, pool_query, in_weight, latent_grad):
    bytes_, feats = byte_hidden.shape
    slots, width = latent_grad.shape
    n_seq, n_mp = lax.axis_size("seq"), lax.axis_size("mp")
    latent_dim = feats * n_mp
    rows = latent_dim // n_seq
    staged = n_seq <= 8

    def swap(value, step):
        return lax.ppermute(value, "mp", [(i, i ^ step) for i in range(n_mp)])

    def trade(value, step):
        return lax.ppermute(value, "seq", [(i, i ^ step) for i in range(n_seq)])

    arguments = (
        byte_hidden,
        patch_start.reshape(bytes_ // LANES, LANES),
        latent_grad,
    )
    query = pool_query.reshape(feats // LANES, LANES)
    back, ahead, byte_hidden, start = call(
        load_kernel,
        (
            shape((EDGE, feats + LANES), BF16),
            shape((EDGE, width + feats + LANES), BF16),
            shape(byte_hidden.shape, BF16),
            shape(arguments[1].shape, jnp.int32),
        ),
        *arguments,
        in_specs=[HBM] * len(arguments),
        limit=VMEM_MOST,
        scratch=(
            pltpu.VMEM((EDGE, width), BF16),
            pltpu.SemaphoreType.DMA((len(arguments),)),
        ),
    )
    following = lax.ppermute(back, "seq", [(i, i - 1) for i in range(1, n_seq)])
    previous = lax.ppermute(ahead, "seq", [(i, i + 1) for i in range(n_seq - 1)])

    if staged:
        in_weight, _ = after((in_weight, back))
        pieces = [in_weight] + [None] * (n_seq - 1)
        pieces[1] = trade(in_weight, 1)
        for step in range(2, n_seq, 2):
            source = after((in_weight, pieces[2]))[0] if step == 4 else in_weight
            pieces[step] = trade(source, step)
    else:
        pieces = [lax.all_gather(in_weight, "seq", axis=0, tiled=True)]

    low, pooled, denom = call(
        pool_kernel,
        (shape((slots, feats), BF16), shape((slots, feats), F32), shape((slots, feats), F32)),
        byte_hidden,
        following,
        start,
        query,
        flops=8 * bytes_ * slots * feats,
    )

    if staged:
        low, previous, *pieces[1:3] = after((low, previous, *pieces[1:3]))
    parts = [low] + [swap(low, step) for step in range(1, n_mp)]
    if staged:
        latest = low
        for at, step in enumerate((2, *range(n_seq - 2, 2, -2))):
            wait = (latest, parts[at + 1]) if at else latest
            pieces[step], _ = after((pieces[step], wait))
            latest = pieces[step + 1] = trade(pieces[step], 1)
    onehot, share, delta, slope = call(
        spread_kernel,
        (shape((bytes_, slots), BF16),) + (shape((bytes_, feats), F32),) * 3,
        byte_hidden,
        previous,
        start,
        query,
        pooled,
        denom,
        flops=8 * bytes_ * slots * feats,
    )
    work = 2 * slots * width * latent_dim
    scale = 1.0 / math.sqrt(n_seq * slots)
    if staged:
        blocks = [shape((rows, width), BF16 if index % 2 else F32) for index in range(n_seq)]
    else:
        blocks = [shape((latent_dim, width), BF16)]
    if staged:
        parts, pieces[-1], share = after((parts, pieces[-1], share))
    terms = call(
        functools.partial(outer_kernel, n_mp, scale),
        tuple(blocks),
        *parts,
        latent_grad,
        flops=work,
        scratch=(pltpu.VMEM((slots, latent_dim), BF16), pltpu.VMEM((latent_dim, width), F32)),
    )
    if staged:
        fetched, pairs, sums = [], [], []
        for at, step in enumerate(reversed(range(0, n_seq, 2))):
            away = terms[step + 1]
            if at >= 2:
                away, _ = after((away, pairs[0] if at == 2 else fetched[1]))
            if at == 1:
                away, _ = after((away, latest))
            fetched.append(trade(away, 1))
            if at == 0:
                previous, _ = after((previous, fetched[0]))
            pairs.append(terms[step] + fetched[-1].astype(F32))
            if step:
                fetched.append(trade(pairs[-1].astype(BF16), step))
            sums.append(fetched[-1].astype(F32) if step else pairs[-1])
        grad_weight = sum(sums[1:], sums[0])
    else:
        received = lax.all_to_all(terms[0], "seq", split_axis=0, concat_axis=0, tiled=True)
        grad_weight = received.reshape(n_seq, rows, width).astype(F32).sum(0)

    *partials, weight_full = call(
        functools.partial(partial_kernel, n_mp),
        (shape((slots + EDGE, feats), BF16),) * n_mp + (shape((latent_dim, width), BF16),),
        latent_grad,
        previous,
        *pieces,
        flops=work,
    )
    grads = [partials[0]] + [swap(partials[step], step) for step in range(1, n_mp)]
    latent = call(
        functools.partial(latent_kernel, n_mp),
        shape((slots, width), BF16),
        *parts,
        weight_full,
        flops=work,
        scratch=(pltpu.VMEM((slots, latent_dim), BF16),),
    )
    grad_bytes = call(
        functools.partial(bytes_kernel, n_mp),
        shape((bytes_, feats), BF16),
        *grads,
        start,
        onehot,
        share,
        delta,
        slope,
        flops=4 * bytes_ * slots * feats,
    )
    return latent, grad_weight, grad_bytes


def solution(mesh):
    in_specs = (P("seq", "mp"), P("seq"), P("mp"), P("seq", "mp"), P("seq", "mp"))
    out_specs = (P("seq", "mp"), P("seq", "mp"), P("seq", "mp"))
    return jax.shard_map(shards, mesh=mesh, in_specs=in_specs, out_specs=out_specs, check_vma=False)
```

```python
import functools
import math

import jax
import jax.numpy as jnp
from jax import lax
from jax.experimental import pallas as pl
from jax.experimental.pallas import tpu as pltpu
from jax.sharding import PartitionSpec as P

HEAD_DIM = 64
EDGE = 16
LANES = 128

soft_cap = 20.0
inv_root = 1.0 / math.sqrt(HEAD_DIM)
F32 = jnp.float32
BF16 = jnp.bfloat16
VMEM_LIMIT = 48 * 1024 * 1024
VMEM_MOST = 53 * 1024 * 1024


def iota(shape, dim):
    return lax.broadcasted_iota(jnp.int32, shape, dim)


def split(value):
    high = value.astype(BF16)
    return high, (value - high.astype(F32)).astype(BF16)


def dot(left, right, dims=((1,), (0,))):
    return lax.dot_general(left, right, (dims, ((), ())), preferred_element_type=F32)


def dot_split(left, value):
    high, low = split(value)
    return dot(left, high) + dot(left, low)


def head_sum(value):
    feats = value.shape[1]
    same = (iota((feats, feats), 0) // HEAD_DIM) == (iota((feats, feats), 1) // HEAD_DIM)
    block = jnp.where(same, 1.0, 0.0).astype(BF16)
    high, low = split(value)
    return dot(high, block) + dot(low, block)


def row_of(ref):
    value = ref[...].astype(F32)
    return jnp.concatenate([value[at : at + 1] for at in range(value.shape[0])], axis=1)


def scores(hidden, query):
    raw = head_sum(hidden * query) * inv_root
    bent = jnp.tanh(raw / soft_cap)
    return bent, jnp.exp(soft_cap * bent)


def segment_rows(start):
    upper = jnp.where(iota((LANES, LANES), 0) <= iota((LANES, LANES), 1), 1.0, 0.0).astype(BF16)
    count = dot(start.astype(F32).astype(BF16), upper)
    rows, total = [], jnp.full((1, 1), -1.0, F32)
    for index in range(start.shape[0]):
        row = count[index : index + 1]
        rows.append(row + total)
        total = total + row[:, LANES - 1 :]
    return rows, total


def lead_mask(start):
    first = jnp.broadcast_to(start[0:1].astype(F32), (EDGE, LANES))
    before = jnp.where(iota((EDGE, LANES), 1) <= iota((EDGE, LANES), 0), first, 0.0)
    return jnp.where(jnp.sum(before, axis=1, keepdims=True) > 0.0, 0.0, 1.0)


def tail_mask(start):
    rows = start.shape[0]
    last = jnp.broadcast_to(start[rows - 1 : rows].astype(F32), (EDGE, LANES))
    after = jnp.where(iota((EDGE, LANES), 1) > iota((EDGE, LANES), 0) + (LANES - EDGE), last, 0.0)
    return jnp.where(jnp.sum(after, axis=1, keepdims=True) > 0.0, 0.0, 1.0)


def load_kernel(hidden_hbm, start_hbm, grad_hbm,
                back_ref, ahead_ref, hidden_ref, start_ref, rows_v, sem):
    pairs = [(start_hbm, start_ref), (hidden_hbm, hidden_ref)]
    copies = [pltpu.make_async_copy(*pair, sem.at[at]) for at, pair in enumerate(pairs)]
    for copy in copies:
        copy.start()
    bytes_, feats = hidden_ref.shape
    width = grad_hbm.shape[1]
    copies[0].wait()
    start = start_ref[...]
    last = jnp.sum(start) - 1
    group = pl.multiple_of((last // EDGE) * EDGE, EDGE)
    rows = pltpu.make_async_copy(grad_hbm.at[pl.ds(group, EDGE), :], rows_v, sem.at[2])
    rows.start()
    back_ref[:, feats:] = jnp.broadcast_to(lead_mask(start), (EDGE, LANES)).astype(BF16)
    ahead_ref[:EDGE, feats:] = jnp.broadcast_to(tail_mask(start), (EDGE, LANES)).astype(BF16)
    copies[1].wait()
    back_ref[:, :feats] = hidden_ref[:EDGE]
    ahead_ref[:EDGE, :feats] = hidden_ref[bytes_ - EDGE :]
    rows.wait()
    chosen = iota((EDGE, width), 0) == last - group
    row = jnp.sum(jnp.where(chosen, rows_v[...].astype(F32), 0.0), axis=0, keepdims=True)
    ahead_ref[EDGE:] = jnp.zeros((EDGE, feats + LANES), BF16)
    for at in range(width // feats):
        piece = row[:, at * feats : (at + 1) * feats]
        spread = jnp.where(iota((EDGE, feats), 0) == at, piece, 0.0)
        old = ahead_ref[EDGE:, :feats].astype(F32)
        ahead_ref[EDGE:, :feats] = (old + spread).astype(BF16)


def pool_kernel(hidden_ref, next_ref, start_ref, query_ref, low_ref, pooled_ref, denom_ref):
    bytes_, feats = hidden_ref.shape
    slots = low_ref.shape[0]
    query = row_of(query_ref)
    rows, last = segment_rows(start_ref[...])
    segment = jnp.concatenate(rows, axis=1).astype(jnp.int32)
    onehot = jnp.where(iota((slots, bytes_), 0) == segment, 1.0, 0.0).astype(BF16)
    hidden = hidden_ref[...].astype(F32)
    _, weight = scores(hidden, query)
    numer = dot_split(onehot, weight * hidden)
    denom = dot_split(onehot, weight)
    following = next_ref[:, :feats].astype(F32)
    mask = next_ref[:, feats : feats + 1].astype(F32)
    extra = scores(following, query)[1] * mask
    is_last = iota((slots, feats), 0) == last.astype(jnp.int32)
    denom = denom + jnp.where(is_last, jnp.sum(extra, axis=0, keepdims=True), 0.0)
    numer = numer + jnp.where(is_last, jnp.sum(extra * following, axis=0, keepdims=True), 0.0)
    live = denom > 0.0
    pooled = jnp.where(live, numer / jnp.where(live, denom, 1.0), 0.0)
    low_ref[...] = pooled.astype(BF16)
    pooled_ref[...] = pooled
    denom_ref[...] = denom


def spread_kernel(hidden_ref, prev_ref, start_ref, query_ref, pooled_ref, denom_ref,
                  onehot_ref, share_ref, delta_ref, slope_ref):
    bytes_, feats = hidden_ref.shape
    slots = pooled_ref.shape[0]
    query = row_of(query_ref)
    rows, _ = segment_rows(start_ref[...])
    columns = [jnp.transpose(jnp.broadcast_to(row, (LANES, LANES))) for row in rows]
    segment = jnp.concatenate(columns, axis=0).astype(jnp.int32)
    onehot = jnp.concatenate(
        [
            jnp.where(segment == iota((bytes_, LANES), 1) + offset, 1.0, 0.0).astype(BF16)
            for offset in range(0, slots, LANES)
        ],
        axis=1,
    )
    onehot_ref[...] = onehot
    hidden = hidden_ref[...].astype(F32)
    bent, weight = scores(hidden, query)
    before = prev_ref[:EDGE, :feats].astype(F32)
    part = scores(before, query)[1] * prev_ref[:EDGE, feats : feats + 1].astype(F32)
    lead = lead_mask(start_ref[...])
    own = weight[:EDGE] * lead
    first_denom = jnp.sum(part + own, axis=0, keepdims=True)
    first_numer = jnp.sum(part * before + own * hidden[:EDGE], axis=0, keepdims=True)
    full = first_denom > 0.0
    first_pooled = jnp.where(full, first_numer / jnp.where(full, first_denom, 1.0), 0.0)
    denom = dot_split(onehot, denom_ref[...])
    pooled = dot_split(onehot, pooled_ref[...])
    denom = jnp.concatenate([denom[:EDGE] + lead * first_denom, denom[EDGE:]], axis=0)
    pooled = jnp.concatenate([pooled[:EDGE] + lead * first_pooled, pooled[EDGE:]], axis=0)
    share = weight / denom
    share_ref[...] = share
    delta_ref[...] = hidden - pooled
    slope_ref[...] = share * (1.0 - bent * bent) * (inv_root * query)


def bytes_kernel(parts, *refs):
    recv_refs, (start_ref, onehot_ref, share_ref, delta_ref, slope_ref, out_ref) = (
        refs[:parts],
        refs[parts:],
    )
    slots = onehot_ref.shape[1]
    grad = recv_refs[0][...].astype(F32)
    for ref in recv_refs[1:]:
        grad = grad + ref[...].astype(F32)
    rows = dot_split(onehot_ref[...], grad[:slots])
    first = jnp.sum(grad[slots:], axis=0, keepdims=True)
    rows = jnp.concatenate([rows[:EDGE] + lead_mask(start_ref[...]) * first, rows[EDGE:]], axis=0)
    inner = head_sum(rows * delta_ref[...])
    out_ref[...] = (share_ref[...] * rows + slope_ref[...] * inner).astype(BF16)


def gather_parts(part_refs, full_ref):
    feats = part_refs[0].shape[1]
    place = lax.axis_index("mp")
    for index, ref in enumerate(part_refs):
        owner = pl.multiple_of((place ^ index) * feats, feats)
        full_ref[:, pl.ds(owner, feats)] = ref[...]


def outer_kernel(parts, scale, *refs):
    part_refs, grad_ref, out_refs = refs[:parts], refs[parts], refs[parts + 1 : -2]
    full_ref, terms_ref = refs[-2:]
    gather_parts(part_refs, full_ref)
    terms_ref[...] = dot(full_ref[...], grad_ref[...], ((0,), (0,))) * scale
    if len(out_refs) == 1:
        out_refs[0][...] = terms_ref[...].astype(out_refs[0].dtype)
        return
    place = lax.axis_index("seq")
    rows = out_refs[0].shape[0]
    for index, ref in enumerate(out_refs):
        owner = pl.multiple_of((place ^ index) * rows, rows)
        ref[...] = terms_ref[pl.ds(owner, rows), :].astype(ref.dtype)


def latent_kernel(parts, *refs):
    part_refs, (weight_ref, out_ref, full_ref) = refs[:parts], refs[parts:]
    gather_parts(part_refs, full_ref)
    out_ref[...] = dot(full_ref[...], weight_ref[...]).astype(BF16)


def partial_kernel(parts, grad_ref, prev_ref, *refs):
    piece_refs, out_refs, full_ref = refs[: -parts - 1], refs[-parts - 1 : -1], refs[-1]
    slots, width = grad_ref.shape
    feats = out_refs[0].shape[1]
    if len(piece_refs) == 1:
        full_ref[...] = piece_refs[0][...]
    else:
        rows = piece_refs[0].shape[0]
        spot = lax.axis_index("seq")
        for index, ref in enumerate(piece_refs):
            owner = pl.multiple_of((spot ^ index) * rows, rows)
            full_ref[pl.ds(owner, rows), :] = ref[...]
    last = prev_ref[EDGE:, :feats].astype(F32)
    row = jnp.concatenate([last[at : at + 1] for at in range(width // feats)], axis=1)
    row = jnp.where(iota((EDGE, width), 0) == 0, row, 0.0).astype(BF16)
    place = lax.axis_index("mp")
    for index, ref in enumerate(out_refs):
        owner = pl.multiple_of((place ^ index) * feats, feats)
        block = full_ref[pl.ds(owner, feats), :]
        ref[:slots] = dot(grad_ref[...], block, ((1,), (1,))).astype(BF16)
        ref[slots:] = dot(row, block, ((1,), (1,))).astype(BF16)


def call(kernel, out_shape, *args, flops=0, scratch=(), in_specs=None, limit=VMEM_LIMIT):
    if in_specs is None:
        in_specs = [pl.BlockSpec(memory_space=pltpu.VMEM)] * len(args)
    return pl.pallas_call(
        kernel,
        out_shape=out_shape,
        in_specs=in_specs,
        out_specs=jax.tree.map(lambda _: pl.BlockSpec(memory_space=pltpu.VMEM), out_shape),
        scratch_shapes=list(scratch),
        cost_estimate=pl.CostEstimate(flops=0, bytes_accessed=0, transcendentals=0),
        compiler_params=pltpu.CompilerParams(vmem_limit_bytes=limit),
    )(*args)


def shape(dims, dtype):
    return jax.ShapeDtypeStruct(dims, dtype)


VMEM = pl.BlockSpec(memory_space=pltpu.VMEM)
after = lax.optimization_barrier
HBM = pl.BlockSpec(memory_space=pltpu.HBM)


def shards(byte_hidden, patch_start, pool_query, in_weight, latent_grad):
    bytes_, feats = byte_hidden.shape
    slots, width = latent_grad.shape
    n_seq, n_mp = lax.axis_size("seq"), lax.axis_size("mp")
    latent_dim = feats * n_mp
    rows = latent_dim // n_seq
    staged = n_seq == 8

    def swap(value, step):
        return lax.ppermute(value, "mp", [(i, i ^ step) for i in range(n_mp)])

    def trade(value, step):
        return lax.ppermute(value, "seq", [(i, i ^ step) for i in range(n_seq)])

    arguments = (
        byte_hidden,
        patch_start.reshape(bytes_ // LANES, LANES),
        latent_grad,
    )
    query = pool_query.reshape(feats // LANES, LANES)
    back, ahead, byte_hidden, start = call(
        load_kernel,
        (
            shape((EDGE, feats + LANES), BF16),
            shape((2 * EDGE, feats + LANES), BF16),
            shape(byte_hidden.shape, BF16),
            shape(arguments[1].shape, jnp.int32),
        ),
        *arguments,
        in_specs=[HBM] * len(arguments),
        limit=VMEM_MOST,
        scratch=(
            pltpu.VMEM((EDGE, width), BF16),
            pltpu.SemaphoreType.DMA((len(arguments),)),
        ),
    )
    following = lax.ppermute(back, "seq", [(i, i - 1) for i in range(1, n_seq)])
    previous = lax.ppermute(ahead, "seq", [(i, i + 1) for i in range(n_seq - 1)])

    if staged:
        in_weight, _ = after((in_weight, back))
        pieces = [in_weight] + [None] * (n_seq - 1)
        pieces[1] = trade(in_weight, 1)
        for step in range(2, n_seq, 2):
            pieces[step] = trade(in_weight, step)
    else:
        pieces = [lax.all_gather(in_weight, "seq", axis=0, tiled=True)]

    low, pooled, denom = call(
        pool_kernel,
        (shape((slots, feats), BF16), shape((slots, feats), F32), shape((slots, feats), F32)),
        byte_hidden,
        following,
        start,
        query,
        flops=8 * bytes_ * slots * feats,
    )

    if staged:
        low, *pieces[1:3] = after((low, *pieces[1:3]))
        pieces[3] = trade(after((pieces[2], low))[0], 1)
    parts = [low]
    for step in reversed([1 << bit for bit in range(n_mp.bit_length() - 1)]):
        if staged and step == 1:
            parts[0], pieces[6], pieces[3] = after((parts[0], pieces[6], pieces[3]))
        parts = [part for held in parts for part in (held, swap(held, step))]
    onehot, share, delta, slope = call(
        spread_kernel,
        (shape((bytes_, slots), BF16),) + (shape((bytes_, feats), F32),) * 3,
        byte_hidden,
        previous,
        start,
        query,
        pooled,
        denom,
        flops=8 * bytes_ * slots * feats,
    )
    work = 2 * slots * width * latent_dim
    scale = 1.0 / math.sqrt(n_seq * slots)
    if staged:
        blocks = [shape((rows, width), BF16 if index % 2 else F32) for index in range(n_seq)]
    else:
        blocks = [shape((latent_dim, width), BF16)]
    terms = call(
        functools.partial(outer_kernel, n_mp, scale),
        tuple(blocks),
        *parts,
        latent_grad,
        flops=work,
        scratch=(pltpu.VMEM((slots, latent_dim), BF16), pltpu.VMEM((latent_dim, width), F32)),
    )
    if staged:
        fetched = {}
        fetched[7] = trade(terms[7], 1)
        pieces[7] = trade(after((pieces[6], terms[0]))[0], 1)
        pieces[5] = trade(after((pieces[4], fetched[7]))[0], 1)
        fetched[5] = trade(after((terms[5], pieces[7], previous))[0], 1)

    *partials, weight_full = call(
        functools.partial(partial_kernel, n_mp),
        (shape((slots + EDGE, feats), BF16),) * n_mp + (shape((latent_dim, width), BF16),),
        latent_grad,
        previous,
        *pieces,
        flops=work,
    )
    grads = [partials[0]] + [swap(partials[step], step) for step in range(1, n_mp)]

    if staged:
        fetched[6] = trade((terms[6] + fetched[7].astype(F32)).astype(BF16), 6)
        fetched[3] = trade(after((terms[3], weight_full, share, fetched[6]))[0], 1)
        fetched[4] = trade((terms[4] + fetched[5].astype(F32)).astype(BF16), 4)
        fetched[1] = trade(after((terms[1], fetched[5], grads[2]))[0], 1)
        fetched[2] = trade((terms[2] + fetched[3].astype(F32)).astype(BF16), 2)
        grad_weight = terms[0] + fetched[1].astype(F32)
        for step in (6, 4, 2):
            grad_weight = grad_weight + fetched[step].astype(F32)
    else:
        received = lax.all_to_all(terms[0], "seq", split_axis=0, concat_axis=0, tiled=True)
        grad_weight = received.reshape(n_seq, rows, width).astype(F32).sum(0)

    latent = call(
        functools.partial(latent_kernel, n_mp),
        shape((slots, width), BF16),
        *parts,
        weight_full,
        flops=work,
        scratch=(pltpu.VMEM((slots, latent_dim), BF16),),
    )
    grad_bytes = call(
        functools.partial(bytes_kernel, n_mp),
        shape((bytes_, feats), BF16),
        *grads,
        start,
        onehot,
        share,
        delta,
        slope,
        flops=4 * bytes_ * slots * feats,
    )
    return latent, grad_weight, grad_bytes


def solution(mesh):
    in_specs = (P("seq", "mp"), P("seq"), P("mp"), P("seq", "mp"), P("seq", "mp"))
    out_specs = (P("seq", "mp"), P("seq", "mp"), P("seq", "mp"))
    return jax.shard_map(shards, mesh=mesh, in_specs=in_specs, out_specs=out_specs, check_vma=False)
```

```python
import functools
import math

import jax
import jax.numpy as jnp
from jax import lax
from jax.experimental import pallas as pl
from jax.experimental.pallas import tpu as pltpu
from jax.sharding import PartitionSpec as P

HEAD_DIM = 64
EDGE = 16
LANES = 128

soft_cap = 20.0
inv_root = 1.0 / math.sqrt(HEAD_DIM)
F32 = jnp.float32
BF16 = jnp.bfloat16
VMEM_LIMIT = 48 * 1024 * 1024
VMEM_MOST = 53 * 1024 * 1024


def iota(shape, dim):
    return lax.broadcasted_iota(jnp.int32, shape, dim)


def split(value):
    high = value.astype(BF16)
    return high, (value - high.astype(F32)).astype(BF16)


def dot(left, right, dims=((1,), (0,))):
    return lax.dot_general(left, right, (dims, ((), ())), preferred_element_type=F32)


def dot_split(left, value):
    high, low = split(value)
    return dot(left, high) + dot(left, low)


def head_sum(value):
    feats = value.shape[1]
    same = (iota((feats, feats), 0) // HEAD_DIM) == (iota((feats, feats), 1) // HEAD_DIM)
    block = jnp.where(same, 1.0, 0.0).astype(BF16)
    high, low = split(value)
    return dot(high, block) + dot(low, block)


def row_of(ref):
    value = ref[...].astype(F32)
    return jnp.concatenate([value[at : at + 1] for at in range(value.shape[0])], axis=1)


def scores(hidden, query):
    raw = head_sum(hidden * query) * inv_root
    bent = jnp.tanh(raw / soft_cap)
    return bent, jnp.exp(soft_cap * bent)


def segment_rows(start):
    upper = jnp.where(iota((LANES, LANES), 0) <= iota((LANES, LANES), 1), 1.0, 0.0).astype(BF16)
    count = dot(start.astype(F32).astype(BF16), upper)
    rows, total = [], jnp.full((1, 1), -1.0, F32)
    for index in range(start.shape[0]):
        row = count[index : index + 1]
        rows.append(row + total)
        total = total + row[:, LANES - 1 :]
    return rows, total


def lead_mask(start):
    first = jnp.broadcast_to(start[0:1].astype(F32), (EDGE, LANES))
    before = jnp.where(iota((EDGE, LANES), 1) <= iota((EDGE, LANES), 0), first, 0.0)
    return jnp.where(jnp.sum(before, axis=1, keepdims=True) > 0.0, 0.0, 1.0)


def tail_mask(start):
    rows = start.shape[0]
    last = jnp.broadcast_to(start[rows - 1 : rows].astype(F32), (EDGE, LANES))
    after = jnp.where(iota((EDGE, LANES), 1) > iota((EDGE, LANES), 0) + (LANES - EDGE), last, 0.0)
    return jnp.where(jnp.sum(after, axis=1, keepdims=True) > 0.0, 0.0, 1.0)


def load_kernel(hidden_hbm, start_hbm, grad_hbm,
                even_ref, odd_ref, hidden_ref, start_ref, rows_v, sem):
    pairs = [(start_hbm, start_ref), (hidden_hbm, hidden_ref)]
    copies = [pltpu.make_async_copy(*pair, sem.at[at]) for at, pair in enumerate(pairs)]
    for copy in copies:
        copy.start()
    bytes_, feats = hidden_ref.shape
    width = grad_hbm.shape[1]
    is_odd = lax.rem(lax.axis_index("seq"), 2) == 1
    copies[0].wait()
    start = start_ref[...]
    last = jnp.sum(start) - 1
    group = pl.multiple_of((last // EDGE) * EDGE, EDGE)
    rows = pltpu.make_async_copy(grad_hbm.at[pl.ds(group, EDGE), :], rows_v, sem.at[2])
    rows.start()
    lead = jnp.broadcast_to(lead_mask(start), (EDGE, LANES))
    tail = jnp.broadcast_to(tail_mask(start), (EDGE, LANES))
    even_ref[:EDGE, feats:] = jnp.where(is_odd, lead, tail).astype(BF16)
    odd_ref[:EDGE, feats:] = jnp.where(is_odd, tail, lead).astype(BF16)
    copies[1].wait()
    head = hidden_ref[:EDGE].astype(F32)
    foot = hidden_ref[bytes_ - EDGE :].astype(F32)
    even_ref[:EDGE, :feats] = jnp.where(is_odd, head, foot).astype(BF16)
    odd_ref[:EDGE, :feats] = jnp.where(is_odd, foot, head).astype(BF16)
    rows.wait()
    chosen = iota((EDGE, width), 0) == last - group
    row = jnp.sum(jnp.where(chosen, rows_v[...].astype(F32), 0.0), axis=0, keepdims=True)
    spread = jnp.zeros((EDGE, feats), F32)
    for at in range(width // feats):
        piece = row[:, at * feats : (at + 1) * feats]
        spread = spread + jnp.where(iota((EDGE, feats), 0) == at, piece, 0.0)
    for ref in (even_ref, odd_ref):
        ref[EDGE:, :feats] = spread.astype(BF16)
        ref[EDGE:, feats:] = jnp.zeros((EDGE, LANES), BF16)


def halos(even_ref, odd_ref):
    is_odd = lax.rem(lax.axis_index("seq"), 2) == 1
    even, odd = even_ref[...].astype(F32), odd_ref[...].astype(F32)
    return jnp.where(is_odd, odd, even), jnp.where(is_odd, even, odd)


def pool_kernel(hidden_ref, even_ref, odd_ref, start_ref, query_ref, low_ref, pooled_ref, denom_ref):
    bytes_, feats = hidden_ref.shape
    slots = low_ref.shape[0]
    query = row_of(query_ref)
    rows, last = segment_rows(start_ref[...])
    segment = jnp.concatenate(rows, axis=1).astype(jnp.int32)
    onehot = jnp.where(iota((slots, bytes_), 0) == segment, 1.0, 0.0).astype(BF16)
    hidden = hidden_ref[...].astype(F32)
    _, weight = scores(hidden, query)
    numer = dot_split(onehot, weight * hidden)
    denom = dot_split(onehot, weight)
    halo, _ = halos(even_ref, odd_ref)
    following, mask = halo[:EDGE, :feats], halo[:EDGE, feats : feats + 1]
    extra = scores(following, query)[1] * mask
    is_last = iota((slots, feats), 0) == last.astype(jnp.int32)
    denom = denom + jnp.where(is_last, jnp.sum(extra, axis=0, keepdims=True), 0.0)
    numer = numer + jnp.where(is_last, jnp.sum(extra * following, axis=0, keepdims=True), 0.0)
    live = denom > 0.0
    pooled = jnp.where(live, numer / jnp.where(live, denom, 1.0), 0.0)
    low_ref[...] = pooled.astype(BF16)
    pooled_ref[...] = pooled
    denom_ref[...] = denom


def spread_kernel(hidden_ref, even_ref, odd_ref, start_ref, query_ref, pooled_ref, denom_ref,
                  onehot_ref, share_ref, delta_ref, slope_ref):
    bytes_, feats = hidden_ref.shape
    slots = pooled_ref.shape[0]
    query = row_of(query_ref)
    rows, _ = segment_rows(start_ref[...])
    columns = [jnp.transpose(jnp.broadcast_to(row, (LANES, LANES))) for row in rows]
    segment = jnp.concatenate(columns, axis=0).astype(jnp.int32)
    onehot = jnp.concatenate(
        [
            jnp.where(segment == iota((bytes_, LANES), 1) + offset, 1.0, 0.0).astype(BF16)
            for offset in range(0, slots, LANES)
        ],
        axis=1,
    )
    onehot_ref[...] = onehot
    hidden = hidden_ref[...].astype(F32)
    bent, weight = scores(hidden, query)
    _, halo = halos(even_ref, odd_ref)
    before = halo[:EDGE, :feats]
    part = scores(before, query)[1] * halo[:EDGE, feats : feats + 1]
    lead = lead_mask(start_ref[...])
    own = weight[:EDGE] * lead
    first_denom = jnp.sum(part + own, axis=0, keepdims=True)
    first_numer = jnp.sum(part * before + own * hidden[:EDGE], axis=0, keepdims=True)
    full = first_denom > 0.0
    first_pooled = jnp.where(full, first_numer / jnp.where(full, first_denom, 1.0), 0.0)
    denom = dot_split(onehot, denom_ref[...])
    pooled = dot_split(onehot, pooled_ref[...])
    denom = jnp.concatenate([denom[:EDGE] + lead * first_denom, denom[EDGE:]], axis=0)
    pooled = jnp.concatenate([pooled[:EDGE] + lead * first_pooled, pooled[EDGE:]], axis=0)
    share = weight / denom
    share_ref[...] = share
    delta_ref[...] = hidden - pooled
    slope_ref[...] = share * (1.0 - bent * bent) * (inv_root * query)


def bytes_kernel(parts, *refs):
    recv_refs, (start_ref, onehot_ref, share_ref, delta_ref, slope_ref, out_ref) = (
        refs[:parts],
        refs[parts:],
    )
    slots = onehot_ref.shape[1]
    grad = recv_refs[0][...].astype(F32)
    for ref in recv_refs[1:]:
        grad = grad + ref[...].astype(F32)
    rows = dot_split(onehot_ref[...], grad[:slots])
    first = jnp.sum(grad[slots:], axis=0, keepdims=True)
    rows = jnp.concatenate([rows[:EDGE] + lead_mask(start_ref[...]) * first, rows[EDGE:]], axis=0)
    inner = head_sum(rows * delta_ref[...])
    out_ref[...] = (share_ref[...] * rows + slope_ref[...] * inner).astype(BF16)


def gather_parts(part_refs, full_ref):
    feats = part_refs[0].shape[1]
    place = lax.axis_index("mp")
    for index, ref in enumerate(part_refs):
        owner = pl.multiple_of((place ^ index) * feats, feats)
        full_ref[:, pl.ds(owner, feats)] = ref[...]


def outer_kernel(parts, scale, *refs):
    part_refs, grad_ref, out_refs = refs[:parts], refs[parts], refs[parts + 1 : -2]
    full_ref, terms_ref = refs[-2:]
    gather_parts(part_refs, full_ref)
    terms_ref[...] = dot(full_ref[...], grad_ref[...], ((0,), (0,))) * scale
    if len(out_refs) == 1:
        out_refs[0][...] = terms_ref[...].astype(out_refs[0].dtype)
        return
    place = lax.axis_index("seq")
    rows = out_refs[0].shape[0]
    for index, ref in enumerate(out_refs):
        owner = pl.multiple_of((place ^ index) * rows, rows)
        ref[...] = terms_ref[pl.ds(owner, rows), :].astype(ref.dtype)


def latent_kernel(parts, *refs):
    part_refs, (weight_ref, out_ref, full_ref) = refs[:parts], refs[parts:]
    gather_parts(part_refs, full_ref)
    out_ref[...] = dot(full_ref[...], weight_ref[...]).astype(BF16)


def partial_kernel(parts, grad_ref, even_ref, odd_ref, *refs):
    piece_refs, out_refs, full_ref = refs[: -parts - 1], refs[-parts - 1 : -1], refs[-1]
    slots, width = grad_ref.shape
    feats = out_refs[0].shape[1]
    if len(piece_refs) == 1:
        full_ref[...] = piece_refs[0][...]
    else:
        rows = piece_refs[0].shape[0]
        spot = lax.axis_index("seq")
        for index, ref in enumerate(piece_refs):
            owner = pl.multiple_of((spot ^ index) * rows, rows)
            full_ref[pl.ds(owner, rows), :] = ref[...]
    last = halos(even_ref, odd_ref)[1][EDGE:, :feats]
    row = jnp.concatenate([last[at : at + 1] for at in range(width // feats)], axis=1)
    row = jnp.where(iota((EDGE, width), 0) == 0, row, 0.0).astype(BF16)
    place = lax.axis_index("mp")
    for index, ref in enumerate(out_refs):
        owner = pl.multiple_of((place ^ index) * feats, feats)
        block = full_ref[pl.ds(owner, feats), :]
        ref[:slots] = dot(grad_ref[...], block, ((1,), (1,))).astype(BF16)
        ref[slots:] = dot(row, block, ((1,), (1,))).astype(BF16)


def call(kernel, out_shape, *args, flops=0, scratch=(), in_specs=None, limit=VMEM_LIMIT):
    if in_specs is None:
        in_specs = [pl.BlockSpec(memory_space=pltpu.VMEM)] * len(args)
    return pl.pallas_call(
        kernel,
        out_shape=out_shape,
        in_specs=in_specs,
        out_specs=jax.tree.map(lambda _: pl.BlockSpec(memory_space=pltpu.VMEM), out_shape),
        scratch_shapes=list(scratch),
        cost_estimate=pl.CostEstimate(flops=0, bytes_accessed=0, transcendentals=0),
        compiler_params=pltpu.CompilerParams(vmem_limit_bytes=limit),
    )(*args)


def shape(dims, dtype):
    return jax.ShapeDtypeStruct(dims, dtype)


VMEM = pl.BlockSpec(memory_space=pltpu.VMEM)
after = lax.optimization_barrier
HBM = pl.BlockSpec(memory_space=pltpu.HBM)


def shards(byte_hidden, patch_start, pool_query, in_weight, latent_grad):
    bytes_, feats = byte_hidden.shape
    slots, width = latent_grad.shape
    n_seq, n_mp = lax.axis_size("seq"), lax.axis_size("mp")
    latent_dim = feats * n_mp
    rows = latent_dim // n_seq
    staged = n_seq == 8

    def swap(value, step):
        return lax.ppermute(value, "mp", [(i, i ^ step) for i in range(n_mp)])

    def trade(value, step):
        return lax.ppermute(value, "seq", [(i, i ^ step) for i in range(n_seq)])

    arguments = (
        byte_hidden,
        patch_start.reshape(bytes_ // LANES, LANES),
        latent_grad,
    )
    query = pool_query.reshape(feats // LANES, LANES)
    even, odd, byte_hidden, start = call(
        load_kernel,
        (
            shape((2 * EDGE, feats + LANES), BF16),
            shape((2 * EDGE, feats + LANES), BF16),
            shape(byte_hidden.shape, BF16),
            shape(arguments[1].shape, jnp.int32),
        ),
        *arguments,
        in_specs=[HBM] * len(arguments),
        limit=VMEM_MOST,
        scratch=(
            pltpu.VMEM((EDGE, width), BF16),
            pltpu.SemaphoreType.DMA((len(arguments),)),
        ),
    )
    in_weight, _ = after((in_weight, even))
    even = trade(even, 1)
    inner = [(i, i + 1) for i in range(1, n_seq - 1, 2)]
    odd = lax.ppermute(odd, "seq", inner + [(j, i) for i, j in inner])

    if staged:
        pieces = [in_weight] + [None] * (n_seq - 1)
        pieces[1] = trade(after((in_weight, even))[0], 1)
        for step in range(2, n_seq, 2):
            source = in_weight if step == 4 else after((in_weight, odd))[0]
            pieces[step] = trade(source, step)
    else:
        pieces = [lax.all_gather(in_weight, "seq", axis=0, tiled=True)]

    low, pooled, denom = call(
        pool_kernel,
        (shape((slots, feats), BF16), shape((slots, feats), F32), shape((slots, feats), F32)),
        byte_hidden,
        even,
        odd,
        start,
        query,
        flops=8 * bytes_ * slots * feats,
    )

    if staged:
        low, pieces[2] = after((low, pieces[2]))
        pieces[3] = trade(after((pieces[2], pieces[1]))[0], 1)
    parts = [low]
    for step in reversed([1 << bit for bit in range(n_mp.bit_length() - 1)]):
        if staged and step == 1:
            parts[0], pieces[6], pieces[3] = after((parts[0], pieces[6], pieces[3]))
        parts = [part for held in parts for part in (held, swap(held, step))]
    onehot, share, delta, slope = call(
        spread_kernel,
        (shape((bytes_, slots), BF16),) + (shape((bytes_, feats), F32),) * 3,
        byte_hidden,
        even,
        odd,
        start,
        query,
        pooled,
        denom,
        flops=8 * bytes_ * slots * feats,
    )
    work = 2 * slots * width * latent_dim
    scale = 1.0 / math.sqrt(n_seq * slots)
    if staged:
        blocks = [shape((rows, width), BF16 if index % 2 else F32) for index in range(n_seq)]
    else:
        blocks = [shape((latent_dim, width), BF16)]
    terms = call(
        functools.partial(outer_kernel, n_mp, scale),
        tuple(blocks),
        *parts,
        latent_grad,
        flops=work,
        scratch=(pltpu.VMEM((slots, latent_dim), BF16), pltpu.VMEM((latent_dim, width), F32)),
    )
    if staged:
        fetched = {}
        fetched[7] = trade(terms[7], 1)
        pieces[7] = trade(after((pieces[6], terms[0]))[0], 1)
        pieces[5] = trade(after((pieces[4], fetched[7]))[0], 1)
        fetched[5] = trade(after((terms[5], pieces[7]))[0], 1)

    *partials, weight_full = call(
        functools.partial(partial_kernel, n_mp),
        (shape((slots + EDGE, feats), BF16),) * n_mp + (shape((latent_dim, width), BF16),),
        latent_grad,
        even,
        odd,
        *pieces,
        flops=work,
    )
    grads = [partials[0]] + [swap(partials[step], step) for step in range(1, n_mp)]

    if staged:
        fetched[6] = trade((terms[6] + fetched[7].astype(F32)).astype(BF16), 6)
        fetched[3] = trade(after((terms[3], weight_full, share, fetched[6]))[0], 1)
        fetched[4] = trade((terms[4] + fetched[5].astype(F32)).astype(BF16), 4)
        fetched[1] = trade(after((terms[1], fetched[5], grads[2]))[0], 1)
        fetched[2] = trade((terms[2] + fetched[3].astype(F32)).astype(BF16), 2)
        grad_weight = terms[0] + fetched[1].astype(F32)
        for step in (6, 4, 2):
            grad_weight = grad_weight + fetched[step].astype(F32)
    else:
        received = lax.all_to_all(terms[0], "seq", split_axis=0, concat_axis=0, tiled=True)
        grad_weight = received.reshape(n_seq, rows, width).astype(F32).sum(0)

    latent = call(
        functools.partial(latent_kernel, n_mp),
        shape((slots, width), BF16),
        *parts,
        weight_full,
        flops=work,
        scratch=(pltpu.VMEM((slots, latent_dim), BF16),),
    )
    grad_bytes = call(
        functools.partial(bytes_kernel, n_mp),
        shape((bytes_, feats), BF16),
        *grads,
        start,
        onehot,
        share,
        delta,
        slope,
        flops=4 * bytes_ * slots * feats,
    )
    return latent, grad_weight, grad_bytes


def solution(mesh):
    in_specs = (P("seq", "mp"), P("seq"), P("mp"), P("seq", "mp"), P("seq", "mp"))
    out_specs = (P("seq", "mp"), P("seq", "mp"), P("seq", "mp"))
    return jax.shard_map(shards, mesh=mesh, in_specs=in_specs, out_specs=out_specs, check_vma=False)
```

```python
import functools
import math

import jax
import jax.numpy as jnp
from jax import lax
from jax.experimental import pallas as pl
from jax.experimental.pallas import tpu as pltpu
from jax.sharding import PartitionSpec as P

HEAD_DIM = 64
EDGE = 16
LANES = 128

soft_cap = 20.0
inv_root = 1.0 / math.sqrt(HEAD_DIM)
F32 = jnp.float32
BF16 = jnp.bfloat16
VMEM_LIMIT = 48 * 1024 * 1024
VMEM_MOST = 53 * 1024 * 1024


def iota(shape, dim):
    return lax.broadcasted_iota(jnp.int32, shape, dim)


def split(value):
    high = value.astype(BF16)
    return high, (value - high.astype(F32)).astype(BF16)


def dot(left, right, dims=((1,), (0,))):
    return lax.dot_general(left, right, (dims, ((), ())), preferred_element_type=F32)


def dot_split(left, value):
    high, low = split(value)
    return dot(left, high) + dot(left, low)


def head_sum(value):
    feats = value.shape[1]
    same = (iota((feats, feats), 0) // HEAD_DIM) == (iota((feats, feats), 1) // HEAD_DIM)
    block = jnp.where(same, 1.0, 0.0).astype(BF16)
    high, low = split(value)
    return dot(high, block) + dot(low, block)


def row_of(ref):
    value = ref[...].astype(F32)
    return jnp.concatenate([value[at : at + 1] for at in range(value.shape[0])], axis=1)


def scores(hidden, query):
    raw = head_sum(hidden * query) * inv_root
    bent = jnp.tanh(raw / soft_cap)
    return bent, jnp.exp(soft_cap * bent)


def segment_rows(start):
    upper = jnp.where(iota((LANES, LANES), 0) <= iota((LANES, LANES), 1), 1.0, 0.0).astype(BF16)
    count = dot(start.astype(F32).astype(BF16), upper)
    rows, total = [], jnp.full((1, 1), -1.0, F32)
    for index in range(start.shape[0]):
        row = count[index : index + 1]
        rows.append(row + total)
        total = total + row[:, LANES - 1 :]
    return rows, total


def lead_mask(start):
    first = jnp.broadcast_to(start[0:1].astype(F32), (EDGE, LANES))
    before = jnp.where(iota((EDGE, LANES), 1) <= iota((EDGE, LANES), 0), first, 0.0)
    return jnp.where(jnp.sum(before, axis=1, keepdims=True) > 0.0, 0.0, 1.0)


def tail_mask(start):
    rows = start.shape[0]
    last = jnp.broadcast_to(start[rows - 1 : rows].astype(F32), (EDGE, LANES))
    after = jnp.where(iota((EDGE, LANES), 1) > iota((EDGE, LANES), 0) + (LANES - EDGE), last, 0.0)
    return jnp.where(jnp.sum(after, axis=1, keepdims=True) > 0.0, 0.0, 1.0)


def load_kernel(hidden_hbm, start_hbm, grad_hbm,
                even_ref, odd_ref, hidden_ref, start_ref, rows_v, sem):
    pairs = [(start_hbm, start_ref), (hidden_hbm, hidden_ref)]
    copies = [pltpu.make_async_copy(*pair, sem.at[at]) for at, pair in enumerate(pairs)]
    for copy in copies:
        copy.start()
    bytes_, feats = hidden_ref.shape
    width = grad_hbm.shape[1]
    is_odd = lax.rem(lax.axis_index("seq"), 2) == 1
    copies[0].wait()
    start = start_ref[...]
    last = jnp.sum(start) - 1
    group = pl.multiple_of((last // EDGE) * EDGE, EDGE)
    rows = pltpu.make_async_copy(grad_hbm.at[pl.ds(group, EDGE), :], rows_v, sem.at[2])
    rows.start()
    lead = jnp.broadcast_to(lead_mask(start), (EDGE, LANES))
    tail = jnp.broadcast_to(tail_mask(start), (EDGE, LANES))
    even_ref[:EDGE, feats:] = jnp.where(is_odd, lead, tail).astype(BF16)
    odd_ref[:EDGE, feats:] = jnp.where(is_odd, tail, lead).astype(BF16)
    copies[1].wait()
    head = hidden_ref[:EDGE].astype(F32)
    foot = hidden_ref[bytes_ - EDGE :].astype(F32)
    even_ref[:EDGE, :feats] = jnp.where(is_odd, head, foot).astype(BF16)
    odd_ref[:EDGE, :feats] = jnp.where(is_odd, foot, head).astype(BF16)
    rows.wait()
    chosen = iota((EDGE, width), 0) == last - group
    row = jnp.sum(jnp.where(chosen, rows_v[...].astype(F32), 0.0), axis=0, keepdims=True)
    spread = jnp.zeros((EDGE, feats), F32)
    for at in range(width // feats):
        piece = row[:, at * feats : (at + 1) * feats]
        spread = spread + jnp.where(iota((EDGE, feats), 0) == at, piece, 0.0)
    for ref in (even_ref, odd_ref):
        ref[EDGE:, :feats] = spread.astype(BF16)
        ref[EDGE:, feats:] = jnp.zeros((EDGE, LANES), BF16)


def halos(even_ref, odd_ref):
    is_odd = lax.rem(lax.axis_index("seq"), 2) == 1
    even, odd = even_ref[...].astype(F32), odd_ref[...].astype(F32)
    return jnp.where(is_odd, odd, even), jnp.where(is_odd, even, odd)


def pool_kernel(hidden_ref, even_ref, odd_ref, start_ref, query_ref, low_ref, pooled_ref, denom_ref):
    bytes_, feats = hidden_ref.shape
    slots = low_ref.shape[0]
    query = row_of(query_ref)
    rows, last = segment_rows(start_ref[...])
    segment = jnp.concatenate(rows, axis=1).astype(jnp.int32)
    onehot = jnp.where(iota((slots, bytes_), 0) == segment, 1.0, 0.0).astype(BF16)
    hidden = hidden_ref[...].astype(F32)
    _, weight = scores(hidden, query)
    numer = dot_split(onehot, weight * hidden)
    denom = dot_split(onehot, weight)
    halo, _ = halos(even_ref, odd_ref)
    following, mask = halo[:EDGE, :feats], halo[:EDGE, feats : feats + 1]
    extra = scores(following, query)[1] * mask
    is_last = iota((slots, feats), 0) == last.astype(jnp.int32)
    denom = denom + jnp.where(is_last, jnp.sum(extra, axis=0, keepdims=True), 0.0)
    numer = numer + jnp.where(is_last, jnp.sum(extra * following, axis=0, keepdims=True), 0.0)
    live = denom > 0.0
    pooled = jnp.where(live, numer / jnp.where(live, denom, 1.0), 0.0)
    low_ref[...] = pooled.astype(BF16)
    pooled_ref[...] = pooled
    denom_ref[...] = denom


def spread_kernel(hidden_ref, even_ref, odd_ref, start_ref, query_ref, pooled_ref, denom_ref,
                  onehot_ref, share_ref, delta_ref, slope_ref):
    bytes_, feats = hidden_ref.shape
    slots = pooled_ref.shape[0]
    query = row_of(query_ref)
    rows, _ = segment_rows(start_ref[...])
    columns = [jnp.transpose(jnp.broadcast_to(row, (LANES, LANES))) for row in rows]
    segment = jnp.concatenate(columns, axis=0).astype(jnp.int32)
    onehot = jnp.concatenate(
        [
            jnp.where(segment == iota((bytes_, LANES), 1) + offset, 1.0, 0.0).astype(BF16)
            for offset in range(0, slots, LANES)
        ],
        axis=1,
    )
    onehot_ref[...] = onehot
    hidden = hidden_ref[...].astype(F32)
    bent, weight = scores(hidden, query)
    _, halo = halos(even_ref, odd_ref)
    before = halo[:EDGE, :feats]
    part = scores(before, query)[1] * halo[:EDGE, feats : feats + 1]
    lead = lead_mask(start_ref[...])
    own = weight[:EDGE] * lead
    first_denom = jnp.sum(part + own, axis=0, keepdims=True)
    first_numer = jnp.sum(part * before + own * hidden[:EDGE], axis=0, keepdims=True)
    full = first_denom > 0.0
    first_pooled = jnp.where(full, first_numer / jnp.where(full, first_denom, 1.0), 0.0)
    denom = dot_split(onehot, denom_ref[...])
    pooled = dot_split(onehot, pooled_ref[...])
    denom = jnp.concatenate([denom[:EDGE] + lead * first_denom, denom[EDGE:]], axis=0)
    pooled = jnp.concatenate([pooled[:EDGE] + lead * first_pooled, pooled[EDGE:]], axis=0)
    share = weight / denom
    share_ref[...] = share
    delta_ref[...] = hidden - pooled
    slope_ref[...] = share * (1.0 - bent * bent) * (inv_root * query)


def bytes_kernel(parts, *refs):
    recv_refs, (start_ref, onehot_ref, share_ref, delta_ref, slope_ref, out_ref) = (
        refs[:parts],
        refs[parts:],
    )
    slots = onehot_ref.shape[1]
    grad = recv_refs[0][...].astype(F32)
    for ref in recv_refs[1:]:
        grad = grad + ref[...].astype(F32)
    rows = dot_split(onehot_ref[...], grad[:slots])
    first = jnp.sum(grad[slots:], axis=0, keepdims=True)
    rows = jnp.concatenate([rows[:EDGE] + lead_mask(start_ref[...]) * first, rows[EDGE:]], axis=0)
    inner = head_sum(rows * delta_ref[...])
    out_ref[...] = (share_ref[...] * rows + slope_ref[...] * inner).astype(BF16)


def gather_parts(part_refs, full_ref):
    feats = part_refs[0].shape[1]
    place = lax.axis_index("mp")
    for index, ref in enumerate(part_refs):
        owner = pl.multiple_of((place ^ index) * feats, feats)
        full_ref[:, pl.ds(owner, feats)] = ref[...]


def outer_kernel(parts, scale, *refs):
    part_refs, grad_ref, out_refs = refs[:parts], refs[parts], refs[parts + 1 : -2]
    full_ref, terms_ref = refs[-2:]
    gather_parts(part_refs, full_ref)
    terms_ref[...] = dot(full_ref[...], grad_ref[...], ((0,), (0,))) * scale
    if len(out_refs) == 1:
        out_refs[0][...] = terms_ref[...].astype(out_refs[0].dtype)
        return
    place = lax.axis_index("seq")
    rows = out_refs[0].shape[0]
    for index, ref in enumerate(out_refs):
        owner = pl.multiple_of((place ^ index) * rows, rows)
        ref[...] = terms_ref[pl.ds(owner, rows), :].astype(ref.dtype)


def latent_kernel(parts, *refs):
    part_refs, (weight_ref, out_ref, full_ref) = refs[:parts], refs[parts:]
    gather_parts(part_refs, full_ref)
    out_ref[...] = dot(full_ref[...], weight_ref[...]).astype(BF16)


def partial_kernel(parts, grad_ref, even_ref, odd_ref, *refs):
    piece_refs, out_refs, full_ref = refs[: -parts - 1], refs[-parts - 1 : -1], refs[-1]
    slots, width = grad_ref.shape
    feats = out_refs[0].shape[1]
    if len(piece_refs) == 1:
        full_ref[...] = piece_refs[0][...]
    else:
        rows = piece_refs[0].shape[0]
        spot = lax.axis_index("seq")
        for index, ref in enumerate(piece_refs):
            owner = pl.multiple_of((spot ^ index) * rows, rows)
            full_ref[pl.ds(owner, rows), :] = ref[...]
    last = halos(even_ref, odd_ref)[1][EDGE:, :feats]
    row = jnp.concatenate([last[at : at + 1] for at in range(width // feats)], axis=1)
    row = jnp.where(iota((EDGE, width), 0) == 0, row, 0.0).astype(BF16)
    place = lax.axis_index("mp")
    for index, ref in enumerate(out_refs):
        owner = pl.multiple_of((place ^ index) * feats, feats)
        block = full_ref[pl.ds(owner, feats), :]
        ref[:slots] = dot(grad_ref[...], block, ((1,), (1,))).astype(BF16)
        ref[slots:] = dot(row, block, ((1,), (1,))).astype(BF16)


def call(kernel, out_shape, *args, flops=0, scratch=(), in_specs=None, limit=VMEM_LIMIT):
    if in_specs is None:
        in_specs = [pl.BlockSpec(memory_space=pltpu.VMEM)] * len(args)
    return pl.pallas_call(
        kernel,
        out_shape=out_shape,
        in_specs=in_specs,
        out_specs=jax.tree.map(lambda _: pl.BlockSpec(memory_space=pltpu.VMEM), out_shape),
        scratch_shapes=list(scratch),
        cost_estimate=pl.CostEstimate(flops=0, bytes_accessed=0, transcendentals=0),
        compiler_params=pltpu.CompilerParams(vmem_limit_bytes=limit),
    )(*args)


def shape(dims, dtype):
    return jax.ShapeDtypeStruct(dims, dtype)


VMEM = pl.BlockSpec(memory_space=pltpu.VMEM)
after = lax.optimization_barrier
HBM = pl.BlockSpec(memory_space=pltpu.HBM)


def shards(byte_hidden, patch_start, pool_query, in_weight, latent_grad):
    bytes_, feats = byte_hidden.shape
    slots, width = latent_grad.shape
    n_seq, n_mp = lax.axis_size("seq"), lax.axis_size("mp")
    latent_dim = feats * n_mp
    rows = latent_dim // n_seq
    staged = n_seq == 8

    def swap(value, step):
        return lax.ppermute(value, "mp", [(i, i ^ step) for i in range(n_mp)])

    def trade(value, step):
        return lax.ppermute(value, "seq", [(i, i ^ step) for i in range(n_seq)])

    arguments = (
        byte_hidden,
        patch_start.reshape(bytes_ // LANES, LANES),
        latent_grad,
    )
    query = pool_query.reshape(feats // LANES, LANES)
    even, odd, byte_hidden, start = call(
        load_kernel,
        (
            shape((2 * EDGE, feats + LANES), BF16),
            shape((2 * EDGE, feats + LANES), BF16),
            shape(byte_hidden.shape, BF16),
            shape(arguments[1].shape, jnp.int32),
        ),
        *arguments,
        in_specs=[HBM] * len(arguments),
        limit=VMEM_MOST,
        scratch=(
            pltpu.VMEM((EDGE, width), BF16),
            pltpu.SemaphoreType.DMA((len(arguments),)),
        ),
    )
    in_weight, _ = after((in_weight, even))
    even = trade(even, 1)
    inner = [(i, i + 1) for i in range(1, n_seq - 1, 2)]
    odd = lax.ppermute(odd, "seq", inner + [(j, i) for i, j in inner])

    if staged:
        pieces = [in_weight] + [None] * (n_seq - 1)
        pieces[1] = trade(in_weight, 1)
        for step in range(2, n_seq, 2):
            pieces[step] = trade(in_weight, step)
    else:
        pieces = [lax.all_gather(in_weight, "seq", axis=0, tiled=True)]

    low, pooled, denom = call(
        pool_kernel,
        (shape((slots, feats), BF16), shape((slots, feats), F32), shape((slots, feats), F32)),
        byte_hidden,
        even,
        odd,
        start,
        query,
        flops=8 * bytes_ * slots * feats,
    )

    if staged:
        low, pieces[1] = after((low, pieces[1]))
        pieces[3] = trade(after((pieces[2], low))[0], 1)
    parts = [low]
    for step in reversed([1 << bit for bit in range(n_mp.bit_length() - 1)]):
        if staged and step == 1:
            parts[0], pieces[6] = after((parts[0], pieces[6]))
        parts = [part for held in parts for part in (held, swap(held, step))]
    onehot, share, delta, slope = call(
        spread_kernel,
        (shape((bytes_, slots), BF16),) + (shape((bytes_, feats), F32),) * 3,
        byte_hidden,
        even,
        odd,
        start,
        query,
        pooled,
        denom,
        flops=8 * bytes_ * slots * feats,
    )
    work = 2 * slots * width * latent_dim
    scale = 1.0 / math.sqrt(n_seq * slots)
    if staged:
        blocks = [shape((rows, width), BF16 if index % 2 else F32) for index in range(n_seq)]
    else:
        blocks = [shape((latent_dim, width), BF16)]
    terms = call(
        functools.partial(outer_kernel, n_mp, scale),
        tuple(blocks),
        *parts,
        latent_grad,
        flops=work,
        scratch=(pltpu.VMEM((slots, latent_dim), BF16), pltpu.VMEM((latent_dim, width), F32)),
    )
    if staged:
        fetched = {}
        fetched[7] = trade(after((terms[7], pieces[3]))[0], 1)
        pieces[7] = trade(after((pieces[6], terms[0]))[0], 1)
        pieces[5] = trade(after((pieces[4], fetched[7]))[0], 1)
        fetched[5] = trade(after((terms[5], pieces[7]))[0], 1)

    *partials, weight_full = call(
        functools.partial(partial_kernel, n_mp),
        (shape((slots + EDGE, feats), BF16),) * n_mp + (shape((latent_dim, width), BF16),),
        latent_grad,
        even,
        odd,
        *pieces,
        flops=work,
    )
    grads = [partials[0]] + [swap(partials[step], step) for step in range(1, n_mp)]

    if staged:
        fetched[6] = trade((terms[6] + fetched[7].astype(F32)).astype(BF16), 6)
        fetched[3] = trade(after((terms[3], weight_full, share, fetched[6]))[0], 1)
        fetched[4] = trade((terms[4] + fetched[5].astype(F32)).astype(BF16), 4)
        fetched[1] = trade(after((terms[1], fetched[5], grads[2]))[0], 1)
        fetched[2] = trade((terms[2] + fetched[3].astype(F32)).astype(BF16), 2)
        grad_weight = terms[0] + fetched[1].astype(F32)
        for step in (6, 4, 2):
            grad_weight = grad_weight + fetched[step].astype(F32)
    else:
        received = lax.all_to_all(terms[0], "seq", split_axis=0, concat_axis=0, tiled=True)
        grad_weight = received.reshape(n_seq, rows, width).astype(F32).sum(0)

    latent = call(
        functools.partial(latent_kernel, n_mp),
        shape((slots, width), BF16),
        *parts,
        weight_full,
        flops=work,
        scratch=(pltpu.VMEM((slots, latent_dim), BF16),),
    )
    grad_bytes = call(
        functools.partial(bytes_kernel, n_mp),
        shape((bytes_, feats), BF16),
        *grads,
        start,
        onehot,
        share,
        delta,
        slope,
        flops=4 * bytes_ * slots * feats,
    )
    return latent, grad_weight, grad_bytes


def solution(mesh):
    in_specs = (P("seq", "mp"), P("seq"), P("mp"), P("seq", "mp"), P("seq", "mp"))
    out_specs = (P("seq", "mp"), P("seq", "mp"), P("seq", "mp"))
    return jax.shard_map(shards, mesh=mesh, in_specs=in_specs, out_specs=out_specs, check_vma=False)
```

```python
import functools
import math

import jax
import jax.numpy as jnp
from jax import lax
from jax.experimental import pallas as pl
from jax.experimental.pallas import tpu as pltpu
from jax.sharding import PartitionSpec as P

HEAD_DIM = 64
EDGE = 16
LANES = 128

soft_cap = 20.0
inv_root = 1.0 / math.sqrt(HEAD_DIM)
F32 = jnp.float32
BF16 = jnp.bfloat16
VMEM_LIMIT = 48 * 1024 * 1024
VMEM_MOST = 53 * 1024 * 1024


def iota(shape, dim):
    return lax.broadcasted_iota(jnp.int32, shape, dim)


def split(value):
    high = value.astype(BF16)
    return high, (value - high.astype(F32)).astype(BF16)


def dot(left, right, dims=((1,), (0,))):
    return lax.dot_general(left, right, (dims, ((), ())), preferred_element_type=F32)


def dot_split(left, value):
    high, low = split(value)
    return dot(left, high) + dot(left, low)


def head_sum(value):
    feats = value.shape[1]
    same = (iota((feats, feats), 0) // HEAD_DIM) == (iota((feats, feats), 1) // HEAD_DIM)
    block = jnp.where(same, 1.0, 0.0).astype(BF16)
    high, low = split(value)
    return dot(high, block) + dot(low, block)


def row_of(ref):
    value = ref[...].astype(F32)
    return jnp.concatenate([value[at : at + 1] for at in range(value.shape[0])], axis=1)


def scores(hidden, query):
    raw = head_sum(hidden * query) * inv_root
    bent = jnp.tanh(raw / soft_cap)
    return bent, jnp.exp(soft_cap * bent)


def segment_rows(start):
    upper = jnp.where(iota((LANES, LANES), 0) <= iota((LANES, LANES), 1), 1.0, 0.0).astype(BF16)
    count = dot(start.astype(F32).astype(BF16), upper)
    rows, total = [], jnp.full((1, 1), -1.0, F32)
    for index in range(start.shape[0]):
        row = count[index : index + 1]
        rows.append(row + total)
        total = total + row[:, LANES - 1 :]
    return rows, total


def lead_mask(start):
    first = jnp.broadcast_to(start[0:1].astype(F32), (EDGE, LANES))
    before = jnp.where(iota((EDGE, LANES), 1) <= iota((EDGE, LANES), 0), first, 0.0)
    return jnp.where(jnp.sum(before, axis=1, keepdims=True) > 0.0, 0.0, 1.0)


def tail_mask(start):
    rows = start.shape[0]
    last = jnp.broadcast_to(start[rows - 1 : rows].astype(F32), (EDGE, LANES))
    after = jnp.where(iota((EDGE, LANES), 1) > iota((EDGE, LANES), 0) + (LANES - EDGE), last, 0.0)
    return jnp.where(jnp.sum(after, axis=1, keepdims=True) > 0.0, 0.0, 1.0)


def load_kernel(hidden_hbm, start_hbm, grad_hbm,
                even_ref, odd_ref, hidden_ref, start_ref, rows_v, sem):
    pairs = [(start_hbm, start_ref), (hidden_hbm, hidden_ref)]
    copies = [pltpu.make_async_copy(*pair, sem.at[at]) for at, pair in enumerate(pairs)]
    for copy in copies:
        copy.start()
    bytes_, feats = hidden_ref.shape
    width = grad_hbm.shape[1]
    is_odd = lax.rem(lax.axis_index("seq"), 2) == 1
    copies[0].wait()
    start = start_ref[...]
    last = jnp.sum(start) - 1
    group = pl.multiple_of((last // EDGE) * EDGE, EDGE)
    rows = pltpu.make_async_copy(grad_hbm.at[pl.ds(group, EDGE), :], rows_v, sem.at[2])
    rows.start()
    lead = jnp.broadcast_to(lead_mask(start), (EDGE, LANES))
    tail = jnp.broadcast_to(tail_mask(start), (EDGE, LANES))
    even_ref[:EDGE, feats:] = jnp.where(is_odd, lead, tail).astype(BF16)
    odd_ref[:EDGE, feats:] = jnp.where(is_odd, tail, lead).astype(BF16)
    copies[1].wait()
    head = hidden_ref[:EDGE].astype(F32)
    foot = hidden_ref[bytes_ - EDGE :].astype(F32)
    even_ref[:EDGE, :feats] = jnp.where(is_odd, head, foot).astype(BF16)
    odd_ref[:EDGE, :feats] = jnp.where(is_odd, foot, head).astype(BF16)
    rows.wait()
    chosen = iota((EDGE, width), 0) == last - group
    row = jnp.sum(jnp.where(chosen, rows_v[...].astype(F32), 0.0), axis=0, keepdims=True)
    spread = jnp.zeros((EDGE, feats), F32)
    for at in range(width // feats):
        piece = row[:, at * feats : (at + 1) * feats]
        spread = spread + jnp.where(iota((EDGE, feats), 0) == at, piece, 0.0)
    for ref in (even_ref, odd_ref):
        ref[EDGE:, :feats] = spread.astype(BF16)
        ref[EDGE:, feats:] = jnp.zeros((EDGE, LANES), BF16)


def halos(even_ref, odd_ref):
    is_odd = lax.rem(lax.axis_index("seq"), 2) == 1
    even, odd = even_ref[...].astype(F32), odd_ref[...].astype(F32)
    return jnp.where(is_odd, odd, even), jnp.where(is_odd, even, odd)


def pool_kernel(hidden_ref, even_ref, odd_ref, start_ref, query_ref, low_ref, pooled_ref, denom_ref):
    bytes_, feats = hidden_ref.shape
    slots = low_ref.shape[0]
    query = row_of(query_ref)
    rows, last = segment_rows(start_ref[...])
    segment = jnp.concatenate(rows, axis=1).astype(jnp.int32)
    onehot = jnp.where(iota((slots, bytes_), 0) == segment, 1.0, 0.0).astype(BF16)
    hidden = hidden_ref[...].astype(F32)
    _, weight = scores(hidden, query)
    numer = dot_split(onehot, weight * hidden)
    denom = dot_split(onehot, weight)
    halo, _ = halos(even_ref, odd_ref)
    following, mask = halo[:EDGE, :feats], halo[:EDGE, feats : feats + 1]
    extra = scores(following, query)[1] * mask
    is_last = iota((slots, feats), 0) == last.astype(jnp.int32)
    denom = denom + jnp.where(is_last, jnp.sum(extra, axis=0, keepdims=True), 0.0)
    numer = numer + jnp.where(is_last, jnp.sum(extra * following, axis=0, keepdims=True), 0.0)
    live = denom > 0.0
    pooled = jnp.where(live, numer / jnp.where(live, denom, 1.0), 0.0)
    low_ref[...] = pooled.astype(BF16)
    pooled_ref[...] = pooled
    denom_ref[...] = denom


def spread_kernel(hidden_ref, even_ref, odd_ref, start_ref, query_ref, pooled_ref, denom_ref,
                  onehot_ref, share_ref, delta_ref, slope_ref):
    bytes_, feats = hidden_ref.shape
    slots = pooled_ref.shape[0]
    query = row_of(query_ref)
    rows, _ = segment_rows(start_ref[...])
    columns = [jnp.transpose(jnp.broadcast_to(row, (LANES, LANES))) for row in rows]
    segment = jnp.concatenate(columns, axis=0).astype(jnp.int32)
    onehot = jnp.concatenate(
        [
            jnp.where(segment == iota((bytes_, LANES), 1) + offset, 1.0, 0.0).astype(BF16)
            for offset in range(0, slots, LANES)
        ],
        axis=1,
    )
    onehot_ref[...] = onehot
    hidden = hidden_ref[...].astype(F32)
    bent, weight = scores(hidden, query)
    _, halo = halos(even_ref, odd_ref)
    before = halo[:EDGE, :feats]
    part = scores(before, query)[1] * halo[:EDGE, feats : feats + 1]
    lead = lead_mask(start_ref[...])
    own = weight[:EDGE] * lead
    first_denom = jnp.sum(part + own, axis=0, keepdims=True)
    first_numer = jnp.sum(part * before + own * hidden[:EDGE], axis=0, keepdims=True)
    full = first_denom > 0.0
    first_pooled = jnp.where(full, first_numer / jnp.where(full, first_denom, 1.0), 0.0)
    denom = dot_split(onehot, denom_ref[...])
    pooled = dot_split(onehot, pooled_ref[...])
    denom = jnp.concatenate([denom[:EDGE] + lead * first_denom, denom[EDGE:]], axis=0)
    pooled = jnp.concatenate([pooled[:EDGE] + lead * first_pooled, pooled[EDGE:]], axis=0)
    share = weight / denom
    share_ref[...] = share
    delta_ref[...] = hidden - pooled
    slope_ref[...] = share * (1.0 - bent * bent) * (inv_root * query)


def bytes_kernel(parts, *refs):
    recv_refs, (start_ref, onehot_ref, share_ref, delta_ref, slope_ref, out_ref) = (
        refs[:parts],
        refs[parts:],
    )
    slots = onehot_ref.shape[1]
    grad = recv_refs[0][...].astype(F32)
    for ref in recv_refs[1:]:
        grad = grad + ref[...].astype(F32)
    rows = dot_split(onehot_ref[...], grad[:slots])
    first = jnp.sum(grad[slots:], axis=0, keepdims=True)
    rows = jnp.concatenate([rows[:EDGE] + lead_mask(start_ref[...]) * first, rows[EDGE:]], axis=0)
    inner = head_sum(rows * delta_ref[...])
    out_ref[...] = (share_ref[...] * rows + slope_ref[...] * inner).astype(BF16)


def gather_parts(part_refs, full_ref):
    feats = part_refs[0].shape[1]
    place = lax.axis_index("mp")
    for index, ref in enumerate(part_refs):
        owner = pl.multiple_of((place ^ index) * feats, feats)
        full_ref[:, pl.ds(owner, feats)] = ref[...]


def outer_kernel(parts, scale, *refs):
    part_refs, grad_ref, out_refs = refs[:parts], refs[parts], refs[parts + 1 : -2]
    full_ref, terms_ref = refs[-2:]
    gather_parts(part_refs, full_ref)
    terms_ref[...] = dot(full_ref[...], grad_ref[...], ((0,), (0,))) * scale
    if len(out_refs) == 1:
        out_refs[0][...] = terms_ref[...].astype(out_refs[0].dtype)
        return
    place = lax.axis_index("seq")
    rows = out_refs[0].shape[0]
    for index, ref in enumerate(out_refs):
        owner = pl.multiple_of((place ^ index) * rows, rows)
        ref[...] = terms_ref[pl.ds(owner, rows), :].astype(ref.dtype)


def latent_kernel(parts, *refs):
    part_refs, (weight_ref, out_ref, full_ref) = refs[:parts], refs[parts:]
    gather_parts(part_refs, full_ref)
    out_ref[...] = dot(full_ref[...], weight_ref[...]).astype(BF16)


def partial_kernel(parts, grad_ref, even_ref, odd_ref, *refs):
    piece_refs, out_refs, full_ref = refs[: -parts - 1], refs[-parts - 1 : -1], refs[-1]
    slots, width = grad_ref.shape
    feats = out_refs[0].shape[1]
    if len(piece_refs) == 1:
        full_ref[...] = piece_refs[0][...]
    else:
        rows = piece_refs[0].shape[0]
        spot = lax.axis_index("seq")
        for index, ref in enumerate(piece_refs):
            owner = pl.multiple_of((spot ^ index) * rows, rows)
            full_ref[pl.ds(owner, rows), :] = ref[...]
    last = halos(even_ref, odd_ref)[1][EDGE:, :feats]
    row = jnp.concatenate([last[at : at + 1] for at in range(width // feats)], axis=1)
    row = jnp.where(iota((EDGE, width), 0) == 0, row, 0.0).astype(BF16)
    place = lax.axis_index("mp")
    for index, ref in enumerate(out_refs):
        owner = pl.multiple_of((place ^ index) * feats, feats)
        block = full_ref[pl.ds(owner, feats), :]
        ref[:slots] = dot(grad_ref[...], block, ((1,), (1,))).astype(BF16)
        ref[slots:] = dot(row, block, ((1,), (1,))).astype(BF16)


def call(kernel, out_shape, *args, weight=0, scratch=(), in_specs=None, limit=VMEM_LIMIT):
    if in_specs is None:
        in_specs = [pl.BlockSpec(memory_space=pltpu.VMEM)] * len(args)
    return pl.pallas_call(
        kernel,
        out_shape=out_shape,
        in_specs=in_specs,
        out_specs=jax.tree.map(lambda _: pl.BlockSpec(memory_space=pltpu.VMEM), out_shape),
        scratch_shapes=list(scratch),
        cost_estimate=pl.CostEstimate(flops=0, bytes_accessed=weight, transcendentals=0),
        compiler_params=pltpu.CompilerParams(vmem_limit_bytes=limit),
    )(*args)


def shape(dims, dtype):
    return jax.ShapeDtypeStruct(dims, dtype)


VMEM = pl.BlockSpec(memory_space=pltpu.VMEM)
after = lax.optimization_barrier
HBM = pl.BlockSpec(memory_space=pltpu.HBM)


def shards(byte_hidden, patch_start, pool_query, in_weight, latent_grad):
    bytes_, feats = byte_hidden.shape
    slots, width = latent_grad.shape
    n_seq, n_mp = lax.axis_size("seq"), lax.axis_size("mp")
    latent_dim = feats * n_mp
    rows = latent_dim // n_seq
    staged = n_seq == 8

    def swap(value, step):
        return lax.ppermute(value, "mp", [(i, i ^ step) for i in range(n_mp)])

    def trade(value, step):
        return lax.ppermute(value, "seq", [(i, i ^ step) for i in range(n_seq)])

    arguments = (
        byte_hidden,
        patch_start.reshape(bytes_ // LANES, LANES),
        latent_grad,
    )
    query = pool_query.reshape(feats // LANES, LANES)
    even, odd, byte_hidden, start = call(
        load_kernel,
        (
            shape((2 * EDGE, feats + LANES), BF16),
            shape((2 * EDGE, feats + LANES), BF16),
            shape(byte_hidden.shape, BF16),
            shape(arguments[1].shape, jnp.int32),
        ),
        *arguments,
        in_specs=[HBM] * len(arguments),
        limit=VMEM_MOST,
        scratch=(
            pltpu.VMEM((EDGE, width), BF16),
            pltpu.SemaphoreType.DMA((len(arguments),)),
        ),
    )
    in_weight, _ = after((in_weight, even))
    even = trade(even, 1)
    inner = [(i, i + 1) for i in range(1, n_seq - 1, 2)]
    odd = lax.ppermute(odd, "seq", inner + [(j, i) for i, j in inner])

    if staged:
        pieces = [in_weight] + [None] * (n_seq - 1)
        pieces[1] = trade(in_weight, 1)
        for step in range(2, n_seq, 2):
            pieces[step] = trade(in_weight, step)
    else:
        pieces = [lax.all_gather(in_weight, "seq", axis=0, tiled=True)]

    low, pooled, denom = call(
        pool_kernel,
        (shape((slots, feats), BF16), shape((slots, feats), F32), shape((slots, feats), F32)),
        byte_hidden,
        even,
        odd,
        start,
        query,
    )

    if staged:
        low = after((low, (pieces[1],)))[0]
        pieces[3] = trade(after((pieces[2], (low,)))[0], 1)
    parts = [low]
    for step in reversed([1 << bit for bit in range(n_mp.bit_length() - 1)]):
        if staged and step == 1:
            parts[0] = after((parts[0], (pieces[6], pieces[3],)))[0]
        parts = [part for held in parts for part in (held, swap(held, step))]
    onehot, share, delta, slope = call(
        spread_kernel,
        (shape((bytes_, slots), BF16),) + (shape((bytes_, feats), F32),) * 3,
        byte_hidden,
        even,
        odd,
        start,
        query,
        pooled,
        denom,
    )
    scale = 1.0 / math.sqrt(n_seq * slots)
    if staged:
        blocks = [shape((rows, width), BF16 if index % 2 else F32) for index in range(n_seq)]
    else:
        blocks = [shape((latent_dim, width), BF16)]
    terms = call(
        functools.partial(outer_kernel, n_mp, scale),
        tuple(blocks),
        *parts,
        latent_grad,
        scratch=(pltpu.VMEM((slots, latent_dim), BF16), pltpu.VMEM((latent_dim, width), F32)),
    )
    if staged:
        fetched = {}
        pieces[7] = trade(after((pieces[6], (pieces[3],)))[0], 1)
        fetched[7] = trade(terms[7], 1)
        fetched[5] = trade(terms[5], 1)
        pieces[5] = trade(after((pieces[4], (fetched[7], pieces[7],)))[0], 1)

    *partials, weight_full = call(
        functools.partial(partial_kernel, n_mp),
        (shape((slots + EDGE, feats), BF16),) * n_mp + (shape((latent_dim, width), BF16),),
        latent_grad,
        even,
        odd,
        *pieces,
    )
    grads = [partials[0]] + [swap(partials[step], step) for step in range(1, n_mp)]

    if staged:
        fetched[6] = trade((terms[6] + fetched[7].astype(F32)).astype(BF16), 6)
        fetched[3] = trade(after((terms[3], (fetched[6], weight_full, share,)))[0], 1)
        fetched[4] = trade((terms[4] + fetched[5].astype(F32)).astype(BF16), 4)
        fetched[1] = trade(after((terms[1], (grads[2], fetched[5],)))[0], 1)
        fetched[2] = trade((terms[2] + fetched[3].astype(F32)).astype(BF16), 2)
        grad_weight = terms[0] + fetched[1].astype(F32)
        for step in (6, 4, 2):
            grad_weight = grad_weight + fetched[step].astype(F32)
    else:
        received = lax.all_to_all(terms[0], "seq", split_axis=0, concat_axis=0, tiled=True)
        grad_weight = received.reshape(n_seq, rows, width).astype(F32).sum(0)

    latent = call(
        functools.partial(latent_kernel, n_mp),
        shape((slots, width), BF16),
        *parts,
        weight_full,
        scratch=(pltpu.VMEM((slots, latent_dim), BF16),),
    )
    grad_bytes = call(
        functools.partial(bytes_kernel, n_mp),
        shape((bytes_, feats), BF16),
        *grads,
        start,
        onehot,
        share,
        delta,
        slope,
    )
    return latent, grad_weight, grad_bytes


def solution(mesh):
    in_specs = (P("seq", "mp"), P("seq"), P("mp"), P("seq", "mp"), P("seq", "mp"))
    out_specs = (P("seq", "mp"), P("seq", "mp"), P("seq", "mp"))
    return jax.shard_map(shards, mesh=mesh, in_specs=in_specs, out_specs=out_specs, check_vma=False)
```

```python
import functools
import math

import jax
import jax.numpy as jnp
from jax import lax
from jax.experimental import pallas as pl
from jax.experimental.pallas import tpu as pltpu
from jax.sharding import PartitionSpec as P

HEAD_DIM = 64
EDGE = 16
LANES = 128

soft_cap = 20.0
inv_root = 1.0 / math.sqrt(HEAD_DIM)
F32 = jnp.float32
BF16 = jnp.bfloat16
VMEM_LIMIT = 48 * 1024 * 1024
VMEM_MOST = 53 * 1024 * 1024


def iota(shape, dim):
    return lax.broadcasted_iota(jnp.int32, shape, dim)


def split(value):
    high = value.astype(BF16)
    return high, (value - high.astype(F32)).astype(BF16)


def dot(left, right, dims=((1,), (0,))):
    return lax.dot_general(left, right, (dims, ((), ())), preferred_element_type=F32)


def dot_split(left, value):
    high, low = split(value)
    return dot(left, high) + dot(left, low)


def head_sum(value):
    feats = value.shape[1]
    same = (iota((feats, feats), 0) // HEAD_DIM) == (iota((feats, feats), 1) // HEAD_DIM)
    block = jnp.where(same, 1.0, 0.0).astype(BF16)
    high, low = split(value)
    return dot(high, block) + dot(low, block)


def row_of(ref):
    value = ref[...].astype(F32)
    return jnp.concatenate([value[at : at + 1] for at in range(value.shape[0])], axis=1)


def scores(hidden, query):
    raw = head_sum(hidden * query) * inv_root
    bent = jnp.tanh(raw / soft_cap)
    return bent, jnp.exp(soft_cap * bent)


def segment_rows(start):
    upper = jnp.where(iota((LANES, LANES), 0) <= iota((LANES, LANES), 1), 1.0, 0.0).astype(BF16)
    count = dot(start.astype(F32).astype(BF16), upper)
    rows, total = [], jnp.full((1, 1), -1.0, F32)
    for index in range(start.shape[0]):
        row = count[index : index + 1]
        rows.append(row + total)
        total = total + row[:, LANES - 1 :]
    return rows, total


def lead_mask(start):
    first = jnp.broadcast_to(start[0:1].astype(F32), (EDGE, LANES))
    before = jnp.where(iota((EDGE, LANES), 1) <= iota((EDGE, LANES), 0), first, 0.0)
    return jnp.where(jnp.sum(before, axis=1, keepdims=True) > 0.0, 0.0, 1.0)


def tail_mask(start):
    rows = start.shape[0]
    last = jnp.broadcast_to(start[rows - 1 : rows].astype(F32), (EDGE, LANES))
    after = jnp.where(iota((EDGE, LANES), 1) > iota((EDGE, LANES), 0) + (LANES - EDGE), last, 0.0)
    return jnp.where(jnp.sum(after, axis=1, keepdims=True) > 0.0, 0.0, 1.0)


def load_kernel(hidden_hbm, start_hbm, grad_hbm,
                even_ref, odd_ref, hidden_ref, start_ref, rows_v, sem):
    pairs = [(start_hbm, start_ref), (hidden_hbm, hidden_ref)]
    copies = [pltpu.make_async_copy(*pair, sem.at[at]) for at, pair in enumerate(pairs)]
    for copy in copies:
        copy.start()
    bytes_, feats = hidden_ref.shape
    width = grad_hbm.shape[1]
    is_odd = lax.rem(lax.axis_index("seq"), 2) == 1
    copies[0].wait()
    start = start_ref[...]
    last = jnp.sum(start) - 1
    group = pl.multiple_of((last // EDGE) * EDGE, EDGE)
    rows = pltpu.make_async_copy(grad_hbm.at[pl.ds(group, EDGE), :], rows_v, sem.at[2])
    rows.start()
    lead = jnp.broadcast_to(lead_mask(start), (EDGE, LANES))
    tail = jnp.broadcast_to(tail_mask(start), (EDGE, LANES))
    even_ref[:EDGE, feats:] = jnp.where(is_odd, lead, tail).astype(BF16)
    odd_ref[:EDGE, feats:] = jnp.where(is_odd, tail, lead).astype(BF16)
    copies[1].wait()
    head = hidden_ref[:EDGE].astype(F32)
    foot = hidden_ref[bytes_ - EDGE :].astype(F32)
    even_ref[:EDGE, :feats] = jnp.where(is_odd, head, foot).astype(BF16)
    odd_ref[:EDGE, :feats] = jnp.where(is_odd, foot, head).astype(BF16)
    rows.wait()
    chosen = iota((EDGE, width), 0) == last - group
    row = jnp.sum(jnp.where(chosen, rows_v[...].astype(F32), 0.0), axis=0, keepdims=True)
    spread = jnp.zeros((EDGE, feats), F32)
    for at in range(width // feats):
        piece = row[:, at * feats : (at + 1) * feats]
        spread = spread + jnp.where(iota((EDGE, feats), 0) == at, piece, 0.0)
    for ref in (even_ref, odd_ref):
        ref[EDGE:, :feats] = spread.astype(BF16)
        ref[EDGE:, feats:] = jnp.zeros((EDGE, LANES), BF16)


def halos(even_ref, odd_ref):
    is_odd = lax.rem(lax.axis_index("seq"), 2) == 1
    even, odd = even_ref[...].astype(F32), odd_ref[...].astype(F32)
    return jnp.where(is_odd, odd, even), jnp.where(is_odd, even, odd)


def pool_kernel(hidden_ref, even_ref, odd_ref, start_ref, query_ref, low_ref, pooled_ref, denom_ref):
    bytes_, feats = hidden_ref.shape
    slots = low_ref.shape[0]
    query = row_of(query_ref)
    rows, last = segment_rows(start_ref[...])
    segment = jnp.concatenate(rows, axis=1).astype(jnp.int32)
    onehot = jnp.where(iota((slots, bytes_), 0) == segment, 1.0, 0.0).astype(BF16)
    hidden = hidden_ref[...].astype(F32)
    _, weight = scores(hidden, query)
    numer = dot_split(onehot, weight * hidden)
    denom = dot_split(onehot, weight)
    halo, _ = halos(even_ref, odd_ref)
    following, mask = halo[:EDGE, :feats], halo[:EDGE, feats : feats + 1]
    extra = scores(following, query)[1] * mask
    is_last = iota((slots, feats), 0) == last.astype(jnp.int32)
    denom = denom + jnp.where(is_last, jnp.sum(extra, axis=0, keepdims=True), 0.0)
    numer = numer + jnp.where(is_last, jnp.sum(extra * following, axis=0, keepdims=True), 0.0)
    live = denom > 0.0
    pooled = jnp.where(live, numer / jnp.where(live, denom, 1.0), 0.0)
    low_ref[...] = pooled.astype(BF16)
    pooled_ref[...] = pooled
    denom_ref[...] = denom


def spread_kernel(hidden_ref, even_ref, odd_ref, start_ref, query_ref, pooled_ref, denom_ref,
                  onehot_ref, share_ref, delta_ref, slope_ref):
    bytes_, feats = hidden_ref.shape
    slots = pooled_ref.shape[0]
    query = row_of(query_ref)
    rows, _ = segment_rows(start_ref[...])
    columns = [jnp.transpose(jnp.broadcast_to(row, (LANES, LANES))) for row in rows]
    segment = jnp.concatenate(columns, axis=0).astype(jnp.int32)
    onehot = jnp.concatenate(
        [
            jnp.where(segment == iota((bytes_, LANES), 1) + offset, 1.0, 0.0).astype(BF16)
            for offset in range(0, slots, LANES)
        ],
        axis=1,
    )
    onehot_ref[...] = onehot
    hidden = hidden_ref[...].astype(F32)
    bent, weight = scores(hidden, query)
    _, halo = halos(even_ref, odd_ref)
    before = halo[:EDGE, :feats]
    part = scores(before, query)[1] * halo[:EDGE, feats : feats + 1]
    lead = lead_mask(start_ref[...])
    own = weight[:EDGE] * lead
    first_denom = jnp.sum(part + own, axis=0, keepdims=True)
    first_numer = jnp.sum(part * before + own * hidden[:EDGE], axis=0, keepdims=True)
    full = first_denom > 0.0
    first_pooled = jnp.where(full, first_numer / jnp.where(full, first_denom, 1.0), 0.0)
    denom = dot_split(onehot, denom_ref[...])
    pooled = dot_split(onehot, pooled_ref[...])
    denom = jnp.concatenate([denom[:EDGE] + lead * first_denom, denom[EDGE:]], axis=0)
    pooled = jnp.concatenate([pooled[:EDGE] + lead * first_pooled, pooled[EDGE:]], axis=0)
    share = weight / denom
    share_ref[...] = share
    delta_ref[...] = hidden - pooled
    slope_ref[...] = share * (1.0 - bent * bent) * (inv_root * query)


def bytes_kernel(parts, *refs):
    recv_refs, (start_ref, onehot_ref, share_ref, delta_ref, slope_ref, out_ref) = (
        refs[:parts],
        refs[parts:],
    )
    slots = onehot_ref.shape[1]
    grad = recv_refs[0][...].astype(F32)
    for ref in recv_refs[1:]:
        grad = grad + ref[...].astype(F32)
    rows = dot_split(onehot_ref[...], grad[:slots])
    first = jnp.sum(grad[slots:], axis=0, keepdims=True)
    rows = jnp.concatenate([rows[:EDGE] + lead_mask(start_ref[...]) * first, rows[EDGE:]], axis=0)
    inner = head_sum(rows * delta_ref[...])
    out_ref[...] = (share_ref[...] * rows + slope_ref[...] * inner).astype(BF16)


def gather_parts(part_refs, full_ref):
    feats = part_refs[0].shape[1]
    place = lax.axis_index("mp")
    for index, ref in enumerate(part_refs):
        owner = pl.multiple_of((place ^ index) * feats, feats)
        full_ref[:, pl.ds(owner, feats)] = ref[...]


def outer_kernel(parts, scale, *refs):
    part_refs, grad_ref, out_refs = refs[:parts], refs[parts], refs[parts + 1 : -2]
    full_ref, terms_ref = refs[-2:]
    gather_parts(part_refs, full_ref)
    terms_ref[...] = dot(full_ref[...], grad_ref[...], ((0,), (0,))) * scale
    if len(out_refs) == 1:
        out_refs[0][...] = terms_ref[...].astype(out_refs[0].dtype)
        return
    place = lax.axis_index("seq")
    rows = out_refs[0].shape[0]
    for index, ref in enumerate(out_refs):
        owner = pl.multiple_of((place ^ index) * rows, rows)
        ref[...] = terms_ref[pl.ds(owner, rows), :].astype(ref.dtype)


def latent_kernel(parts, *refs):
    part_refs, (weight_ref, out_ref, full_ref) = refs[:parts], refs[parts:]
    gather_parts(part_refs, full_ref)
    out_ref[...] = dot(full_ref[...], weight_ref[...]).astype(BF16)


def partial_kernel(parts, grad_ref, even_ref, odd_ref, *refs):
    piece_refs, out_refs, full_ref = refs[: -parts - 1], refs[-parts - 1 : -1], refs[-1]
    slots, width = grad_ref.shape
    feats = out_refs[0].shape[1]
    if len(piece_refs) == 1:
        full_ref[...] = piece_refs[0][...]
    else:
        rows = piece_refs[0].shape[0]
        spot = lax.axis_index("seq")
        for index, ref in enumerate(piece_refs):
            owner = pl.multiple_of((spot ^ index) * rows, rows)
            full_ref[pl.ds(owner, rows), :] = ref[...]
    last = halos(even_ref, odd_ref)[1][EDGE:, :feats]
    row = jnp.concatenate([last[at : at + 1] for at in range(width // feats)], axis=1)
    row = jnp.where(iota((EDGE, width), 0) == 0, row, 0.0).astype(BF16)
    place = lax.axis_index("mp")
    for index, ref in enumerate(out_refs):
        owner = pl.multiple_of((place ^ index) * feats, feats)
        block = full_ref[pl.ds(owner, feats), :]
        ref[:slots] = dot(grad_ref[...], block, ((1,), (1,))).astype(BF16)
        ref[slots:] = dot(row, block, ((1,), (1,))).astype(BF16)


def call(kernel, out_shape, *args, weight=0, scratch=(), in_specs=None, limit=VMEM_LIMIT):
    if in_specs is None:
        in_specs = [pl.BlockSpec(memory_space=pltpu.VMEM)] * len(args)
    return pl.pallas_call(
        kernel,
        out_shape=out_shape,
        in_specs=in_specs,
        out_specs=jax.tree.map(lambda _: pl.BlockSpec(memory_space=pltpu.VMEM), out_shape),
        scratch_shapes=list(scratch),
        cost_estimate=pl.CostEstimate(flops=0, bytes_accessed=weight, transcendentals=0),
        compiler_params=pltpu.CompilerParams(vmem_limit_bytes=limit),
    )(*args)


def shape(dims, dtype):
    return jax.ShapeDtypeStruct(dims, dtype)


VMEM = pl.BlockSpec(memory_space=pltpu.VMEM)
after = lax.optimization_barrier
HBM = pl.BlockSpec(memory_space=pltpu.HBM)


def shards(byte_hidden, patch_start, pool_query, in_weight, latent_grad):
    bytes_, feats = byte_hidden.shape
    slots, width = latent_grad.shape
    n_seq, n_mp = lax.axis_size("seq"), lax.axis_size("mp")
    latent_dim = feats * n_mp
    rows = latent_dim // n_seq
    staged = n_seq == 8

    def swap(value, step):
        return lax.ppermute(value, "mp", [(i, i ^ step) for i in range(n_mp)])

    def trade(value, step):
        return lax.ppermute(value, "seq", [(i, i ^ step) for i in range(n_seq)])

    arguments = (
        byte_hidden,
        patch_start.reshape(bytes_ // LANES, LANES),
        latent_grad,
    )
    query = pool_query.reshape(feats // LANES, LANES)
    even, odd, byte_hidden, start = call(
        load_kernel,
        (
            shape((2 * EDGE, feats + LANES), BF16),
            shape((2 * EDGE, feats + LANES), BF16),
            shape(byte_hidden.shape, BF16),
            shape(arguments[1].shape, jnp.int32),
        ),
        *arguments,
        in_specs=[HBM] * len(arguments),
        limit=VMEM_MOST,
        scratch=(
            pltpu.VMEM((EDGE, width), BF16),
            pltpu.SemaphoreType.DMA((len(arguments),)),
        ),
    )
    in_weight, _ = after((in_weight, even))
    even = trade(even, 1)
    inner = [(i, i + 1) for i in range(1, n_seq - 1, 2)]
    odd = lax.ppermute(odd, "seq", inner + [(j, i) for i, j in inner])

    if staged:
        pieces = [in_weight] + [None] * (n_seq - 1)
        for step in (1, 2, 4):
            first = even if step == 1 else odd
            pieces[step] = trade(after((in_weight, first))[0], step)
    else:
        pieces = [lax.all_gather(in_weight, "seq", axis=0, tiled=True)]

    low, pooled, denom = call(
        pool_kernel,
        (shape((slots, feats), BF16), shape((slots, feats), F32), shape((slots, feats), F32)),
        byte_hidden,
        even,
        odd,
        start,
        query,
    )

    if staged:
        pieces[3] = trade(after((pieces[2], (low, pieces[1],)))[0], 1)
    parts = [low]
    for step in reversed([1 << bit for bit in range(n_mp.bit_length() - 1)]):
        if staged and step == 1:
            parts[0] = after((parts[0], (pieces[4], pieces[3],)))[0]
        parts = [part for held in parts for part in (held, swap(held, step))]
    onehot, share, delta, slope = call(
        spread_kernel,
        (shape((bytes_, slots), BF16),) + (shape((bytes_, feats), F32),) * 3,
        byte_hidden,
        even,
        odd,
        start,
        query,
        pooled,
        denom,
    )
    scale = 1.0 / math.sqrt(n_seq * slots)
    if staged:
        blocks = [shape((rows, width), BF16 if index % 2 else F32) for index in range(n_seq)]
    else:
        blocks = [shape((latent_dim, width), BF16)]
    terms = call(
        functools.partial(outer_kernel, n_mp, scale),
        tuple(blocks),
        *parts,
        latent_grad,
        scratch=(pltpu.VMEM((slots, latent_dim), BF16), pltpu.VMEM((latent_dim, width), F32)),
    )
    if staged:
        fetched = {}
        pieces[7] = trade(after((pieces[6], (pieces[3],)))[0], 1)
        pieces[5] = trade(pieces[4], 1)
        pieces[6] = trade(pieces[4], 2)
        pieces[7] = trade(after((pieces[6], (pieces[5],)))[0], 1)
        fetched[7] = trade(terms[7], 1)
        fetched[6] = trade((terms[6] + fetched[7].astype(F32)).astype(BF16), 2)
        fetched[5] = trade(after((terms[5], (pieces[7],)))[0], 1)

    if staged:
        latent_grad, _ = after((latent_grad, (fetched[7],)))
    *partials, weight_full = call(
        functools.partial(partial_kernel, n_mp),
        (shape((slots + EDGE, feats), BF16),) * n_mp + (shape((latent_dim, width), BF16),),
        latent_grad,
        even,
        odd,
        *pieces,
    )
    grads = [partials[0]] + [swap(partials[step], step) for step in range(1, n_mp)]

    if staged:
        fetched[3] = trade(after((terms[3], (fetched[5], fetched[6], weight_full, share,)))[0], 1)
        pair = terms[4] + fetched[5].astype(F32) + fetched[6].astype(F32)
        fetched[4] = trade(pair.astype(BF16), 4)
        fetched[1] = trade(after((terms[1], (grads[2],)))[0], 1)
        fetched[2] = trade((terms[2] + fetched[3].astype(F32)).astype(BF16), 2)
        grad_weight = terms[0] + fetched[1].astype(F32)
        for step in (4, 2):
            grad_weight = grad_weight + fetched[step].astype(F32)
    else:
        received = lax.all_to_all(terms[0], "seq", split_axis=0, concat_axis=0, tiled=True)
        grad_weight = received.reshape(n_seq, rows, width).astype(F32).sum(0)

    latent = call(
        functools.partial(latent_kernel, n_mp),
        shape((slots, width), BF16),
        *parts,
        weight_full,
        scratch=(pltpu.VMEM((slots, latent_dim), BF16),),
    )
    grad_bytes = call(
        functools.partial(bytes_kernel, n_mp),
        shape((bytes_, feats), BF16),
        *grads,
        start,
        onehot,
        share,
        delta,
        slope,
    )
    return latent, grad_weight, grad_bytes


def solution(mesh):
    in_specs = (P("seq", "mp"), P("seq"), P("mp"), P("seq", "mp"), P("seq", "mp"))
    out_specs = (P("seq", "mp"), P("seq", "mp"), P("seq", "mp"))
    return jax.shard_map(shards, mesh=mesh, in_specs=in_specs, out_specs=out_specs, check_vma=False)
```

```python
import functools
import math

import jax
import jax.numpy as jnp
from jax import lax
from jax.experimental import pallas as pl
from jax.experimental.pallas import tpu as pltpu
from jax.sharding import PartitionSpec as P

HEAD_DIM = 64
EDGE = 16
LANES = 128

soft_cap = 20.0
inv_root = 1.0 / math.sqrt(HEAD_DIM)
F32 = jnp.float32
BF16 = jnp.bfloat16
VMEM_LIMIT = 48 * 1024 * 1024
VMEM_MOST = 53 * 1024 * 1024


def iota(shape, dim):
    return lax.broadcasted_iota(jnp.int32, shape, dim)


def split(value):
    high = value.astype(BF16)
    return high, (value - high.astype(F32)).astype(BF16)


def dot(left, right, dims=((1,), (0,))):
    return lax.dot_general(left, right, (dims, ((), ())), preferred_element_type=F32)


def dot_split(left, value):
    high, low = split(value)
    return dot(left, high) + dot(left, low)


def head_sum(value):
    feats = value.shape[1]
    same = (iota((feats, feats), 0) // HEAD_DIM) == (iota((feats, feats), 1) // HEAD_DIM)
    block = jnp.where(same, 1.0, 0.0).astype(BF16)
    high, low = split(value)
    return dot(high, block) + dot(low, block)


def row_of(ref):
    value = ref[...].astype(F32)
    return jnp.concatenate([value[at : at + 1] for at in range(value.shape[0])], axis=1)


def scores(hidden, query):
    raw = head_sum(hidden * query) * inv_root
    bent = jnp.tanh(raw / soft_cap)
    return bent, jnp.exp(soft_cap * bent)


def segment_rows(start):
    upper = jnp.where(iota((LANES, LANES), 0) <= iota((LANES, LANES), 1), 1.0, 0.0).astype(BF16)
    count = dot(start.astype(F32).astype(BF16), upper)
    rows, total = [], jnp.full((1, 1), -1.0, F32)
    for index in range(start.shape[0]):
        row = count[index : index + 1]
        rows.append(row + total)
        total = total + row[:, LANES - 1 :]
    return rows, total


def lead_mask(start):
    first = jnp.broadcast_to(start[0:1].astype(F32), (EDGE, LANES))
    before = jnp.where(iota((EDGE, LANES), 1) <= iota((EDGE, LANES), 0), first, 0.0)
    return jnp.where(jnp.sum(before, axis=1, keepdims=True) > 0.0, 0.0, 1.0)


def tail_mask(start):
    rows = start.shape[0]
    last = jnp.broadcast_to(start[rows - 1 : rows].astype(F32), (EDGE, LANES))
    after = jnp.where(iota((EDGE, LANES), 1) > iota((EDGE, LANES), 0) + (LANES - EDGE), last, 0.0)
    return jnp.where(jnp.sum(after, axis=1, keepdims=True) > 0.0, 0.0, 1.0)


def load_kernel(hidden_hbm, start_hbm, grad_hbm,
                even_ref, odd_ref, hidden_ref, start_ref, rows_v, sem):
    pairs = [(start_hbm, start_ref), (hidden_hbm, hidden_ref)]
    copies = [pltpu.make_async_copy(*pair, sem.at[at]) for at, pair in enumerate(pairs)]
    for copy in copies:
        copy.start()
    bytes_, feats = hidden_ref.shape
    width = grad_hbm.shape[1]
    is_odd = lax.rem(lax.axis_index("seq"), 2) == 1
    copies[0].wait()
    start = start_ref[...]
    last = jnp.sum(start) - 1
    group = pl.multiple_of((last // EDGE) * EDGE, EDGE)
    rows = pltpu.make_async_copy(grad_hbm.at[pl.ds(group, EDGE), :], rows_v, sem.at[2])
    rows.start()
    lead = jnp.broadcast_to(lead_mask(start), (EDGE, LANES))
    tail = jnp.broadcast_to(tail_mask(start), (EDGE, LANES))
    even_ref[:EDGE, feats:] = jnp.where(is_odd, lead, tail).astype(BF16)
    odd_ref[:EDGE, feats:] = jnp.where(is_odd, tail, lead).astype(BF16)
    copies[1].wait()
    head = hidden_ref[:EDGE].astype(F32)
    foot = hidden_ref[bytes_ - EDGE :].astype(F32)
    even_ref[:EDGE, :feats] = jnp.where(is_odd, head, foot).astype(BF16)
    odd_ref[:EDGE, :feats] = jnp.where(is_odd, foot, head).astype(BF16)
    rows.wait()
    chosen = iota((EDGE, width), 0) == last - group
    row = jnp.sum(jnp.where(chosen, rows_v[...].astype(F32), 0.0), axis=0, keepdims=True)
    spread = jnp.zeros((EDGE, feats), F32)
    for at in range(width // feats):
        piece = row[:, at * feats : (at + 1) * feats]
        spread = spread + jnp.where(iota((EDGE, feats), 0) == at, piece, 0.0)
    for ref in (even_ref, odd_ref):
        ref[EDGE:, :feats] = spread.astype(BF16)
        ref[EDGE:, feats:] = jnp.zeros((EDGE, LANES), BF16)


def halos(even_ref, odd_ref):
    is_odd = lax.rem(lax.axis_index("seq"), 2) == 1
    even, odd = even_ref[...].astype(F32), odd_ref[...].astype(F32)
    return jnp.where(is_odd, odd, even), jnp.where(is_odd, even, odd)


def pool_kernel(hidden_ref, even_ref, odd_ref, start_ref, query_ref, low_ref, pooled_ref, denom_ref):
    bytes_, feats = hidden_ref.shape
    slots = low_ref.shape[0]
    query = row_of(query_ref)
    rows, last = segment_rows(start_ref[...])
    segment = jnp.concatenate(rows, axis=1).astype(jnp.int32)
    onehot = jnp.where(iota((slots, bytes_), 0) == segment, 1.0, 0.0).astype(BF16)
    hidden = hidden_ref[...].astype(F32)
    _, weight = scores(hidden, query)
    numer = dot_split(onehot, weight * hidden)
    denom = dot_split(onehot, weight)
    halo, _ = halos(even_ref, odd_ref)
    following, mask = halo[:EDGE, :feats], halo[:EDGE, feats : feats + 1]
    extra = scores(following, query)[1] * mask
    is_last = iota((slots, feats), 0) == last.astype(jnp.int32)
    denom = denom + jnp.where(is_last, jnp.sum(extra, axis=0, keepdims=True), 0.0)
    numer = numer + jnp.where(is_last, jnp.sum(extra * following, axis=0, keepdims=True), 0.0)
    live = denom > 0.0
    pooled = jnp.where(live, numer / jnp.where(live, denom, 1.0), 0.0)
    low_ref[...] = pooled.astype(BF16)
    pooled_ref[...] = pooled
    denom_ref[...] = denom


def spread_kernel(hidden_ref, even_ref, odd_ref, start_ref, query_ref, pooled_ref, denom_ref,
                  onehot_ref, share_ref, delta_ref, slope_ref):
    bytes_, feats = hidden_ref.shape
    slots = pooled_ref.shape[0]
    query = row_of(query_ref)
    rows, _ = segment_rows(start_ref[...])
    columns = [jnp.transpose(jnp.broadcast_to(row, (LANES, LANES))) for row in rows]
    segment = jnp.concatenate(columns, axis=0).astype(jnp.int32)
    onehot = jnp.concatenate(
        [
            jnp.where(segment == iota((bytes_, LANES), 1) + offset, 1.0, 0.0).astype(BF16)
            for offset in range(0, slots, LANES)
        ],
        axis=1,
    )
    onehot_ref[...] = onehot
    hidden = hidden_ref[...].astype(F32)
    bent, weight = scores(hidden, query)
    _, halo = halos(even_ref, odd_ref)
    before = halo[:EDGE, :feats]
    part = scores(before, query)[1] * halo[:EDGE, feats : feats + 1]
    lead = lead_mask(start_ref[...])
    own = weight[:EDGE] * lead
    first_denom = jnp.sum(part + own, axis=0, keepdims=True)
    first_numer = jnp.sum(part * before + own * hidden[:EDGE], axis=0, keepdims=True)
    full = first_denom > 0.0
    first_pooled = jnp.where(full, first_numer / jnp.where(full, first_denom, 1.0), 0.0)
    denom = dot_split(onehot, denom_ref[...])
    pooled = dot_split(onehot, pooled_ref[...])
    denom = jnp.concatenate([denom[:EDGE] + lead * first_denom, denom[EDGE:]], axis=0)
    pooled = jnp.concatenate([pooled[:EDGE] + lead * first_pooled, pooled[EDGE:]], axis=0)
    share = weight / denom
    share_ref[...] = share
    delta_ref[...] = hidden - pooled
    slope_ref[...] = share * (1.0 - bent * bent) * (inv_root * query)


def bytes_kernel(parts, *refs):
    recv_refs, (start_ref, onehot_ref, share_ref, delta_ref, slope_ref, out_ref) = (
        refs[:parts],
        refs[parts:],
    )
    slots = onehot_ref.shape[1]
    grad = recv_refs[0][...].astype(F32)
    for ref in recv_refs[1:]:
        grad = grad + ref[...].astype(F32)
    rows = dot_split(onehot_ref[...], grad[:slots])
    first = jnp.sum(grad[slots:], axis=0, keepdims=True)
    rows = jnp.concatenate([rows[:EDGE] + lead_mask(start_ref[...]) * first, rows[EDGE:]], axis=0)
    inner = head_sum(rows * delta_ref[...])
    out_ref[...] = (share_ref[...] * rows + slope_ref[...] * inner).astype(BF16)


def gather_parts(part_refs, full_ref):
    feats = part_refs[0].shape[1]
    place = lax.axis_index("mp")
    for index, ref in enumerate(part_refs):
        owner = pl.multiple_of((place ^ index) * feats, feats)
        full_ref[:, pl.ds(owner, feats)] = ref[...]


def outer_kernel(parts, scale, *refs):
    part_refs, grad_ref, out_refs = refs[:parts], refs[parts], refs[parts + 1 : -2]
    full_ref, terms_ref = refs[-2:]
    gather_parts(part_refs, full_ref)
    terms_ref[...] = dot(full_ref[...], grad_ref[...], ((0,), (0,))) * scale
    if len(out_refs) == 1:
        out_refs[0][...] = terms_ref[...].astype(out_refs[0].dtype)
        return
    place = lax.axis_index("seq")
    rows = out_refs[0].shape[0]
    for index, ref in enumerate(out_refs):
        owner = pl.multiple_of((place ^ index) * rows, rows)
        ref[...] = terms_ref[pl.ds(owner, rows), :].astype(ref.dtype)


def latent_kernel(parts, *refs):
    part_refs, (weight_ref, out_ref, full_ref) = refs[:parts], refs[parts:]
    gather_parts(part_refs, full_ref)
    out_ref[...] = dot(full_ref[...], weight_ref[...]).astype(BF16)


def partial_kernel(parts, grad_ref, even_ref, odd_ref, *refs):
    piece_refs, out_refs, full_ref = refs[: -parts - 1], refs[-parts - 1 : -1], refs[-1]
    slots, width = grad_ref.shape
    feats = out_refs[0].shape[1]
    if len(piece_refs) == 1:
        full_ref[...] = piece_refs[0][...]
    else:
        rows = piece_refs[0].shape[0]
        spot = lax.axis_index("seq")
        for index, ref in enumerate(piece_refs):
            owner = pl.multiple_of((spot ^ index) * rows, rows)
            full_ref[pl.ds(owner, rows), :] = ref[...]
    last = halos(even_ref, odd_ref)[1][EDGE:, :feats]
    row = jnp.concatenate([last[at : at + 1] for at in range(width // feats)], axis=1)
    row = jnp.where(iota((EDGE, width), 0) == 0, row, 0.0).astype(BF16)
    place = lax.axis_index("mp")
    for index, ref in enumerate(out_refs):
        owner = pl.multiple_of((place ^ index) * feats, feats)
        block = full_ref[pl.ds(owner, feats), :]
        ref[:slots] = dot(grad_ref[...], block, ((1,), (1,))).astype(BF16)
        ref[slots:] = dot(row, block, ((1,), (1,))).astype(BF16)


def call(kernel, out_shape, *args, weight=0, scratch=(), in_specs=None, limit=VMEM_LIMIT):
    if in_specs is None:
        in_specs = [pl.BlockSpec(memory_space=pltpu.VMEM)] * len(args)
    return pl.pallas_call(
        kernel,
        out_shape=out_shape,
        in_specs=in_specs,
        out_specs=jax.tree.map(lambda _: pl.BlockSpec(memory_space=pltpu.VMEM), out_shape),
        scratch_shapes=list(scratch),
        cost_estimate=pl.CostEstimate(flops=0, bytes_accessed=weight, transcendentals=0),
        compiler_params=pltpu.CompilerParams(vmem_limit_bytes=limit),
    )(*args)


def shape(dims, dtype):
    return jax.ShapeDtypeStruct(dims, dtype)


VMEM = pl.BlockSpec(memory_space=pltpu.VMEM)
after = lax.optimization_barrier
HBM = pl.BlockSpec(memory_space=pltpu.HBM)


def shards(byte_hidden, patch_start, pool_query, in_weight, latent_grad):
    bytes_, feats = byte_hidden.shape
    slots, width = latent_grad.shape
    n_seq, n_mp = lax.axis_size("seq"), lax.axis_size("mp")
    latent_dim = feats * n_mp
    rows = latent_dim // n_seq
    staged = n_seq == 8

    def swap(value, step):
        return lax.ppermute(value, "mp", [(i, i ^ step) for i in range(n_mp)])

    def trade(value, step):
        return lax.ppermute(value, "seq", [(i, i ^ step) for i in range(n_seq)])

    arguments = (
        byte_hidden,
        patch_start.reshape(bytes_ // LANES, LANES),
        latent_grad,
    )
    query = pool_query.reshape(feats // LANES, LANES)
    even, odd, byte_hidden, start = call(
        load_kernel,
        (
            shape((2 * EDGE, feats + LANES), BF16),
            shape((2 * EDGE, feats + LANES), BF16),
            shape(byte_hidden.shape, BF16),
            shape(arguments[1].shape, jnp.int32),
        ),
        *arguments,
        in_specs=[HBM] * len(arguments),
        limit=VMEM_MOST,
        scratch=(
            pltpu.VMEM((EDGE, width), BF16),
            pltpu.SemaphoreType.DMA((len(arguments),)),
        ),
    )
    in_weight, _ = after((in_weight, even))
    even = trade(even, 1)
    inner = [(i, i + 1) for i in range(1, n_seq - 1, 2)]
    odd = lax.ppermute(odd, "seq", inner + [(j, i) for i, j in inner])

    if staged:
        pieces = [in_weight] + [None] * (n_seq - 1)
        for step in (1, 2, 4):
            pieces[step] = trade(in_weight, step)
    else:
        pieces = [lax.all_gather(in_weight, "seq", axis=0, tiled=True)]

    low, pooled, denom = call(
        pool_kernel,
        (shape((slots, feats), BF16), shape((slots, feats), F32), shape((slots, feats), F32)),
        byte_hidden,
        even,
        odd,
        start,
        query,
    )

    if staged:
        low = after((low, (pieces[1],)))[0]
        pieces[3] = trade(after((pieces[2], (low,)))[0], 1)
    parts = [low]
    for step in reversed([1 << bit for bit in range(n_mp.bit_length() - 1)]):
        if staged and step == 1:
            parts = [after((parts[0], (pieces[4],)))[0], parts[1]]
        parts = [part for held in parts for part in (held, swap(held, step))]
    onehot, share, delta, slope = call(
        spread_kernel,
        (shape((bytes_, slots), BF16),) + (shape((bytes_, feats), F32),) * 3,
        byte_hidden,
        even,
        odd,
        start,
        query,
        pooled,
        denom,
    )
    scale = 1.0 / math.sqrt(n_seq * slots)
    if staged:
        blocks = [shape((rows, width), BF16 if index % 2 else F32) for index in range(n_seq)]
    else:
        blocks = [shape((latent_dim, width), BF16)]
    terms = call(
        functools.partial(outer_kernel, n_mp, scale),
        tuple(blocks),
        *parts,
        latent_grad,
        scratch=(pltpu.VMEM((slots, latent_dim), BF16), pltpu.VMEM((latent_dim, width), F32)),
    )
    if staged:
        fetched = {}
        pieces[7] = trade(after((pieces[6], (pieces[3],)))[0], 1)
        pieces[5] = trade(after((pieces[4], (terms[0],)))[0], 1)
        pieces[6] = trade(pieces[4], 2)
        pieces[7] = trade(after((pieces[6], (pieces[5],)))[0], 1)
        fetched[7] = trade(after((terms[7], (pieces[3],)))[0], 1)
        fetched[6] = trade((terms[6] + fetched[7].astype(F32)).astype(BF16), 2)
        fetched[5] = trade(after((terms[5], (pieces[7],)))[0], 1)

    if staged:
        latent_grad, _ = after((latent_grad, (fetched[7],)))
    *partials, weight_full = call(
        functools.partial(partial_kernel, n_mp),
        (shape((slots + EDGE, feats), BF16),) * n_mp + (shape((latent_dim, width), BF16),),
        latent_grad,
        even,
        odd,
        *pieces,
    )
    grads = [partials[0]] + [swap(partials[step], step) for step in range(1, n_mp)]

    if staged:
        fetched[3] = trade(after((terms[3], (fetched[5], fetched[6], weight_full, share,)))[0], 1)
        pair = terms[4] + fetched[5].astype(F32) + fetched[6].astype(F32)
        fetched[4] = trade(pair.astype(BF16), 4)
        fetched[1] = trade(after((terms[1], (grads[2],)))[0], 1)
        fetched[2] = trade((terms[2] + fetched[3].astype(F32)).astype(BF16), 2)
        grad_weight = terms[0] + fetched[1].astype(F32)
        for step in (4, 2):
            grad_weight = grad_weight + fetched[step].astype(F32)
    else:
        received = lax.all_to_all(terms[0], "seq", split_axis=0, concat_axis=0, tiled=True)
        grad_weight = received.reshape(n_seq, rows, width).astype(F32).sum(0)

    latent = call(
        functools.partial(latent_kernel, n_mp),
        shape((slots, width), BF16),
        *parts,
        weight_full,
        scratch=(pltpu.VMEM((slots, latent_dim), BF16),),
    )
    grad_bytes = call(
        functools.partial(bytes_kernel, n_mp),
        shape((bytes_, feats), BF16),
        *grads,
        start,
        onehot,
        share,
        delta,
        slope,
    )
    return latent, grad_weight, grad_bytes


def solution(mesh):
    in_specs = (P("seq", "mp"), P("seq"), P("mp"), P("seq", "mp"), P("seq", "mp"))
    out_specs = (P("seq", "mp"), P("seq", "mp"), P("seq", "mp"))
    return jax.shard_map(shards, mesh=mesh, in_specs=in_specs, out_specs=out_specs, check_vma=False)
```

```python
import functools
import math

import jax
import jax.numpy as jnp
from jax import lax
from jax.experimental import pallas as pl
from jax.experimental.pallas import tpu as pltpu
from jax.sharding import PartitionSpec as P

HEAD_DIM = 64
EDGE = 16
LANES = 128

soft_cap = 20.0
inv_root = 1.0 / math.sqrt(HEAD_DIM)
F32 = jnp.float32
BF16 = jnp.bfloat16
VMEM_LIMIT = 48 * 1024 * 1024
VMEM_MOST = 53 * 1024 * 1024


def iota(shape, dim):
    return lax.broadcasted_iota(jnp.int32, shape, dim)


def split(value):
    high = value.astype(BF16)
    return high, (value - high.astype(F32)).astype(BF16)


def dot(left, right, dims=((1,), (0,))):
    return lax.dot_general(left, right, (dims, ((), ())), preferred_element_type=F32)


def dot_split(left, value):
    high, low = split(value)
    return dot(left, high) + dot(left, low)


def head_sum(value):
    feats = value.shape[1]
    same = (iota((feats, feats), 0) // HEAD_DIM) == (iota((feats, feats), 1) // HEAD_DIM)
    block = jnp.where(same, 1.0, 0.0).astype(BF16)
    high, low = split(value)
    return dot(high, block) + dot(low, block)


def row_of(ref):
    value = ref[...].astype(F32)
    return jnp.concatenate([value[at : at + 1] for at in range(value.shape[0])], axis=1)


def scores(hidden, query):
    raw = head_sum(hidden * query) * inv_root
    bent = jnp.tanh(raw / soft_cap)
    return bent, jnp.exp(soft_cap * bent)


def segment_rows(start):
    upper = jnp.where(iota((LANES, LANES), 0) <= iota((LANES, LANES), 1), 1.0, 0.0).astype(BF16)
    count = dot(start.astype(F32).astype(BF16), upper)
    rows, total = [], jnp.full((1, 1), -1.0, F32)
    for index in range(start.shape[0]):
        row = count[index : index + 1]
        rows.append(row + total)
        total = total + row[:, LANES - 1 :]
    return rows, total


def lead_mask(start):
    first = jnp.broadcast_to(start[0:1].astype(F32), (EDGE, LANES))
    before = jnp.where(iota((EDGE, LANES), 1) <= iota((EDGE, LANES), 0), first, 0.0)
    return jnp.where(jnp.sum(before, axis=1, keepdims=True) > 0.0, 0.0, 1.0)


def tail_mask(start):
    rows = start.shape[0]
    last = jnp.broadcast_to(start[rows - 1 : rows].astype(F32), (EDGE, LANES))
    after = jnp.where(iota((EDGE, LANES), 1) > iota((EDGE, LANES), 0) + (LANES - EDGE), last, 0.0)
    return jnp.where(jnp.sum(after, axis=1, keepdims=True) > 0.0, 0.0, 1.0)


def load_kernel(hidden_hbm, start_hbm, grad_hbm,
                back_ref, ahead_ref, hidden_ref, start_ref, rows_v, sem):
    pairs = [(start_hbm, start_ref), (hidden_hbm, hidden_ref)]
    copies = [pltpu.make_async_copy(*pair, sem.at[at]) for at, pair in enumerate(pairs)]
    for copy in copies:
        copy.start()
    bytes_, feats = hidden_ref.shape
    width = grad_hbm.shape[1]
    copies[0].wait()
    start = start_ref[...]
    last = jnp.sum(start) - 1
    group = pl.multiple_of((last // EDGE) * EDGE, EDGE)
    rows = pltpu.make_async_copy(grad_hbm.at[pl.ds(group, EDGE), :], rows_v, sem.at[2])
    rows.start()
    back_ref[:, feats:] = jnp.broadcast_to(lead_mask(start), (EDGE, LANES)).astype(BF16)
    ahead_ref[:EDGE, feats:] = jnp.broadcast_to(tail_mask(start), (EDGE, LANES)).astype(BF16)
    copies[1].wait()
    back_ref[:, :feats] = hidden_ref[:EDGE]
    ahead_ref[:EDGE, :feats] = hidden_ref[bytes_ - EDGE :]
    rows.wait()
    chosen = iota((EDGE, width), 0) == last - group
    row = jnp.sum(jnp.where(chosen, rows_v[...].astype(F32), 0.0), axis=0, keepdims=True)
    ahead_ref[EDGE:] = jnp.zeros((EDGE, feats + LANES), BF16)
    for at in range(width // feats):
        piece = row[:, at * feats : (at + 1) * feats]
        spread = jnp.where(iota((EDGE, feats), 0) == at, piece, 0.0)
        old = ahead_ref[EDGE:, :feats].astype(F32)
        ahead_ref[EDGE:, :feats] = (old + spread).astype(BF16)


def pool_kernel(hidden_ref, next_ref, start_ref, query_ref, low_ref, pooled_ref, denom_ref):
    bytes_, feats = hidden_ref.shape
    slots = low_ref.shape[0]
    query = row_of(query_ref)
    rows, last = segment_rows(start_ref[...])
    segment = jnp.concatenate(rows, axis=1).astype(jnp.int32)
    onehot = jnp.where(iota((slots, bytes_), 0) == segment, 1.0, 0.0).astype(BF16)
    hidden = hidden_ref[...].astype(F32)
    _, weight = scores(hidden, query)
    numer = dot_split(onehot, weight * hidden)
    denom = dot_split(onehot, weight)
    following = next_ref[:, :feats].astype(F32)
    mask = next_ref[:, feats : feats + 1].astype(F32)
    extra = scores(following, query)[1] * mask
    is_last = iota((slots, feats), 0) == last.astype(jnp.int32)
    denom = denom + jnp.where(is_last, jnp.sum(extra, axis=0, keepdims=True), 0.0)
    numer = numer + jnp.where(is_last, jnp.sum(extra * following, axis=0, keepdims=True), 0.0)
    live = denom > 0.0
    pooled = jnp.where(live, numer / jnp.where(live, denom, 1.0), 0.0)
    low_ref[...] = pooled.astype(BF16)
    pooled_ref[...] = pooled
    denom_ref[...] = denom


def spread_kernel(hidden_ref, prev_ref, start_ref, query_ref, pooled_ref, denom_ref,
                  onehot_ref, share_ref, delta_ref, slope_ref):
    bytes_, feats = hidden_ref.shape
    slots = pooled_ref.shape[0]
    query = row_of(query_ref)
    rows, _ = segment_rows(start_ref[...])
    columns = [jnp.transpose(jnp.broadcast_to(row, (LANES, LANES))) for row in rows]
    segment = jnp.concatenate(columns, axis=0).astype(jnp.int32)
    onehot = jnp.concatenate(
        [
            jnp.where(segment == iota((bytes_, LANES), 1) + offset, 1.0, 0.0).astype(BF16)
            for offset in range(0, slots, LANES)
        ],
        axis=1,
    )
    onehot_ref[...] = onehot
    hidden = hidden_ref[...].astype(F32)
    bent, weight = scores(hidden, query)
    before = prev_ref[:EDGE, :feats].astype(F32)
    part = scores(before, query)[1] * prev_ref[:EDGE, feats : feats + 1].astype(F32)
    lead = lead_mask(start_ref[...])
    own = weight[:EDGE] * lead
    first_denom = jnp.sum(part + own, axis=0, keepdims=True)
    first_numer = jnp.sum(part * before + own * hidden[:EDGE], axis=0, keepdims=True)
    full = first_denom > 0.0
    first_pooled = jnp.where(full, first_numer / jnp.where(full, first_denom, 1.0), 0.0)
    denom = dot_split(onehot, denom_ref[...])
    pooled = dot_split(onehot, pooled_ref[...])
    denom = jnp.concatenate([denom[:EDGE] + lead * first_denom, denom[EDGE:]], axis=0)
    pooled = jnp.concatenate([pooled[:EDGE] + lead * first_pooled, pooled[EDGE:]], axis=0)
    share = weight / denom
    share_ref[...] = share
    delta_ref[...] = hidden - pooled
    slope_ref[...] = share * (1.0 - bent * bent) * (inv_root * query)


def bytes_kernel(parts, *refs):
    recv_refs, (start_ref, onehot_ref, share_ref, delta_ref, slope_ref, out_ref) = (
        refs[:parts],
        refs[parts:],
    )
    slots = onehot_ref.shape[1]
    grad = recv_refs[0][...].astype(F32)
    for ref in recv_refs[1:]:
        grad = grad + ref[...].astype(F32)
    rows = dot_split(onehot_ref[...], grad[:slots])
    first = jnp.sum(grad[slots:], axis=0, keepdims=True)
    rows = jnp.concatenate([rows[:EDGE] + lead_mask(start_ref[...]) * first, rows[EDGE:]], axis=0)
    inner = head_sum(rows * delta_ref[...])
    out_ref[...] = (share_ref[...] * rows + slope_ref[...] * inner).astype(BF16)


def gather_parts(part_refs, full_ref):
    feats = part_refs[0].shape[1]
    place = lax.axis_index("mp")
    for index, ref in enumerate(part_refs):
        owner = pl.multiple_of((place ^ index) * feats, feats)
        full_ref[:, pl.ds(owner, feats)] = ref[...]


def outer_kernel(parts, scale, *refs):
    part_refs, grad_ref, out_refs = refs[:parts], refs[parts], refs[parts + 1 : -2]
    full_ref, terms_ref = refs[-2:]
    gather_parts(part_refs, full_ref)
    terms_ref[...] = dot(full_ref[...], grad_ref[...], ((0,), (0,))) * scale
    if len(out_refs) == 1:
        out_refs[0][...] = terms_ref[...].astype(out_refs[0].dtype)
        return
    place = lax.axis_index("seq")
    rows = out_refs[0].shape[0]
    for index, ref in enumerate(out_refs):
        owner = pl.multiple_of((place ^ index) * rows, rows)
        ref[...] = terms_ref[pl.ds(owner, rows), :].astype(ref.dtype)


def latent_kernel(parts, *refs):
    part_refs, (weight_ref, out_ref, full_ref) = refs[:parts], refs[parts:]
    gather_parts(part_refs, full_ref)
    out_ref[...] = dot(full_ref[...], weight_ref[...]).astype(BF16)


def partial_kernel(parts, grad_ref, prev_ref, *refs):
    piece_refs, out_refs, full_ref = refs[: -parts - 1], refs[-parts - 1 : -1], refs[-1]
    slots, width = grad_ref.shape
    feats = out_refs[0].shape[1]
    if len(piece_refs) == 1:
        full_ref[...] = piece_refs[0][...]
    else:
        rows = piece_refs[0].shape[0]
        spot = lax.axis_index("seq")
        for index, ref in enumerate(piece_refs):
            owner = pl.multiple_of((spot ^ index) * rows, rows)
            full_ref[pl.ds(owner, rows), :] = ref[...]
    last = prev_ref[EDGE:, :feats].astype(F32)
    row = jnp.concatenate([last[at : at + 1] for at in range(width // feats)], axis=1)
    row = jnp.where(iota((EDGE, width), 0) == 0, row, 0.0).astype(BF16)
    place = lax.axis_index("mp")
    for index, ref in enumerate(out_refs):
        owner = pl.multiple_of((place ^ index) * feats, feats)
        block = full_ref[pl.ds(owner, feats), :]
        ref[:slots] = dot(grad_ref[...], block, ((1,), (1,))).astype(BF16)
        ref[slots:] = dot(row, block, ((1,), (1,))).astype(BF16)


def call(kernel, out_shape, *args, flops=0, scratch=(), in_specs=None, limit=VMEM_LIMIT):
    if in_specs is None:
        in_specs = [pl.BlockSpec(memory_space=pltpu.VMEM)] * len(args)
    return pl.pallas_call(
        kernel,
        out_shape=out_shape,
        in_specs=in_specs,
        out_specs=jax.tree.map(lambda _: pl.BlockSpec(memory_space=pltpu.VMEM), out_shape),
        scratch_shapes=list(scratch),
        cost_estimate=pl.CostEstimate(flops=0, bytes_accessed=0, transcendentals=0),
        compiler_params=pltpu.CompilerParams(vmem_limit_bytes=limit),
    )(*args)


def shape(dims, dtype):
    return jax.ShapeDtypeStruct(dims, dtype)


VMEM = pl.BlockSpec(memory_space=pltpu.VMEM)
after = lax.optimization_barrier
HBM = pl.BlockSpec(memory_space=pltpu.HBM)


def shards(byte_hidden, patch_start, pool_query, in_weight, latent_grad):
    bytes_, feats = byte_hidden.shape
    slots, width = latent_grad.shape
    n_seq, n_mp = lax.axis_size("seq"), lax.axis_size("mp")
    latent_dim = feats * n_mp
    rows = latent_dim // n_seq
    staged = n_seq == 8

    def swap(value, step):
        return lax.ppermute(value, "mp", [(i, i ^ step) for i in range(n_mp)])

    def trade(value, step):
        return lax.ppermute(value, "seq", [(i, i ^ step) for i in range(n_seq)])

    arguments = (
        byte_hidden,
        patch_start.reshape(bytes_ // LANES, LANES),
        latent_grad,
    )
    query = pool_query.reshape(feats // LANES, LANES)
    back, ahead, byte_hidden, start = call(
        load_kernel,
        (
            shape((EDGE, feats + LANES), BF16),
            shape((2 * EDGE, feats + LANES), BF16),
            shape(byte_hidden.shape, BF16),
            shape(arguments[1].shape, jnp.int32),
        ),
        *arguments,
        in_specs=[HBM] * len(arguments),
        limit=VMEM_MOST,
        scratch=(
            pltpu.VMEM((EDGE, width), BF16),
            pltpu.SemaphoreType.DMA((len(arguments),)),
        ),
    )
    following = lax.ppermute(back, "seq", [(i, i - 1) for i in range(1, n_seq)])
    previous = lax.ppermute(ahead, "seq", [(i, i + 1) for i in range(n_seq - 1)])

    if staged:
        in_weight, _ = after((in_weight, back))
        pieces = [in_weight] + [None] * (n_seq - 1)
        for step in (1, 2, 4):
            pieces[step] = trade(in_weight, step)
        pieces[6] = trade(pieces[4], 2)
    else:
        pieces = [lax.all_gather(in_weight, "seq", axis=0, tiled=True)]

    low, pooled, denom = call(
        pool_kernel,
        (shape((slots, feats), BF16), shape((slots, feats), F32), shape((slots, feats), F32)),
        byte_hidden,
        following,
        start,
        query,
        flops=8 * bytes_ * slots * feats,
    )

    if staged:
        low, *pieces[1:3] = after((low, *pieces[1:3]))
        pieces[3] = trade(after((pieces[2], low))[0], 1)
    parts = [low]
    for step in reversed([1 << bit for bit in range(n_mp.bit_length() - 1)]):
        if staged and step == 1:
            parts[0], _ = after((parts[0], (pieces[4], pieces[3])))
        parts = [part for held in parts for part in (held, swap(held, step))]
    onehot, share, delta, slope = call(
        spread_kernel,
        (shape((bytes_, slots), BF16),) + (shape((bytes_, feats), F32),) * 3,
        byte_hidden,
        previous,
        start,
        query,
        pooled,
        denom,
        flops=8 * bytes_ * slots * feats,
    )
    work = 2 * slots * width * latent_dim
    scale = 1.0 / math.sqrt(n_seq * slots)
    if staged:
        blocks = [shape((rows, width), BF16 if index % 2 else F32) for index in range(n_seq)]
    else:
        blocks = [shape((latent_dim, width), BF16)]
    terms = call(
        functools.partial(outer_kernel, n_mp, scale),
        tuple(blocks),
        *parts,
        latent_grad,
        flops=work,
        scratch=(pltpu.VMEM((slots, latent_dim), BF16), pltpu.VMEM((latent_dim, width), F32)),
    )
    if staged:
        fetched = {}
        fetched[7] = trade(terms[7], 1)
        pieces[5] = trade(after((pieces[4], terms[0]))[0], 1)
        pieces[7] = trade(after((pieces[6], fetched[7]))[0], 1)
        fetched[5] = trade(after((terms[5], pieces[5], previous))[0], 1)

    *partials, weight_full = call(
        functools.partial(partial_kernel, n_mp),
        (shape((slots + EDGE, feats), BF16),) * n_mp + (shape((latent_dim, width), BF16),),
        latent_grad,
        previous,
        *pieces,
        flops=work,
    )
    grads = [partials[0]] + [swap(partials[step], step) for step in range(1, n_mp)]

    if staged:
        fetched[6] = trade((terms[6] + fetched[7].astype(F32)).astype(BF16), 2)
        fetched[3] = trade(after((terms[3], weight_full, share, fetched[6]))[0], 1)
        pair = terms[4] + fetched[5].astype(F32) + fetched[6].astype(F32)
        fetched[4] = trade(pair.astype(BF16), 4)
        fetched[1] = trade(after((terms[1], fetched[5], grads[2]))[0], 1)
        fetched[2] = trade((terms[2] + fetched[3].astype(F32)).astype(BF16), 2)
        grad_weight = terms[0] + fetched[1].astype(F32)
        for step in (4, 2):
            grad_weight = grad_weight + fetched[step].astype(F32)
    else:
        received = lax.all_to_all(terms[0], "seq", split_axis=0, concat_axis=0, tiled=True)
        grad_weight = received.reshape(n_seq, rows, width).astype(F32).sum(0)

    latent = call(
        functools.partial(latent_kernel, n_mp),
        shape((slots, width), BF16),
        *parts,
        weight_full,
        flops=work,
        scratch=(pltpu.VMEM((slots, latent_dim), BF16),),
    )
    grad_bytes = call(
        functools.partial(bytes_kernel, n_mp),
        shape((bytes_, feats), BF16),
        *grads,
        start,
        onehot,
        share,
        delta,
        slope,
        flops=4 * bytes_ * slots * feats,
    )
    return latent, grad_weight, grad_bytes


def solution(mesh):
    in_specs = (P("seq", "mp"), P("seq"), P("mp"), P("seq", "mp"), P("seq", "mp"))
    out_specs = (P("seq", "mp"), P("seq", "mp"), P("seq", "mp"))
    return jax.shard_map(shards, mesh=mesh, in_specs=in_specs, out_specs=out_specs, check_vma=False)
```

```python
import functools
import math

import jax
import jax.numpy as jnp
from jax import lax
from jax.experimental import pallas as pl
from jax.experimental.pallas import tpu as pltpu
from jax.sharding import PartitionSpec as P

HEAD_DIM = 64
EDGE = 16
LANES = 128

soft_cap = 20.0
inv_root = 1.0 / math.sqrt(HEAD_DIM)
F32 = jnp.float32
BF16 = jnp.bfloat16
VMEM_LIMIT = 48 * 1024 * 1024
VMEM_MOST = 53 * 1024 * 1024


def iota(shape, dim):
    return lax.broadcasted_iota(jnp.int32, shape, dim)


def split(value):
    high = value.astype(BF16)
    return high, (value - high.astype(F32)).astype(BF16)


def dot(left, right, dims=((1,), (0,))):
    return lax.dot_general(left, right, (dims, ((), ())), preferred_element_type=F32)


def dot_split(left, value):
    high, low = split(value)
    return dot(left, high) + dot(left, low)


def head_sum(value):
    feats = value.shape[1]
    same = (iota((feats, feats), 0) // HEAD_DIM) == (iota((feats, feats), 1) // HEAD_DIM)
    block = jnp.where(same, 1.0, 0.0).astype(BF16)
    high, low = split(value)
    return dot(high, block) + dot(low, block)


def row_of(ref):
    value = ref[...].astype(F32)
    return jnp.concatenate([value[at : at + 1] for at in range(value.shape[0])], axis=1)


def scores(hidden, query):
    raw = head_sum(hidden * query) * inv_root
    bent = jnp.tanh(raw / soft_cap)
    return bent, jnp.exp(soft_cap * bent)


def segment_rows(start):
    upper = jnp.where(iota((LANES, LANES), 0) <= iota((LANES, LANES), 1), 1.0, 0.0).astype(BF16)
    count = dot(start.astype(F32).astype(BF16), upper)
    rows, total = [], jnp.full((1, 1), -1.0, F32)
    for index in range(start.shape[0]):
        row = count[index : index + 1]
        rows.append(row + total)
        total = total + row[:, LANES - 1 :]
    return rows, total


def lead_mask(start):
    first = jnp.broadcast_to(start[0:1].astype(F32), (EDGE, LANES))
    before = jnp.where(iota((EDGE, LANES), 1) <= iota((EDGE, LANES), 0), first, 0.0)
    return jnp.where(jnp.sum(before, axis=1, keepdims=True) > 0.0, 0.0, 1.0)


def tail_mask(start):
    rows = start.shape[0]
    last = jnp.broadcast_to(start[rows - 1 : rows].astype(F32), (EDGE, LANES))
    after = jnp.where(iota((EDGE, LANES), 1) > iota((EDGE, LANES), 0) + (LANES - EDGE), last, 0.0)
    return jnp.where(jnp.sum(after, axis=1, keepdims=True) > 0.0, 0.0, 1.0)


def load_kernel(hidden_hbm, start_hbm, grad_hbm,
                back_ref, ahead_ref, hidden_ref, start_ref, rows_v, sem):
    pairs = [(start_hbm, start_ref), (hidden_hbm, hidden_ref)]
    copies = [pltpu.make_async_copy(*pair, sem.at[at]) for at, pair in enumerate(pairs)]
    for copy in copies:
        copy.start()
    bytes_, feats = hidden_ref.shape
    width = grad_hbm.shape[1]
    copies[0].wait()
    start = start_ref[...]
    last = jnp.sum(start) - 1
    group = pl.multiple_of((last // EDGE) * EDGE, EDGE)
    rows = pltpu.make_async_copy(grad_hbm.at[pl.ds(group, EDGE), :], rows_v, sem.at[2])
    rows.start()
    back_ref[:, feats:] = jnp.broadcast_to(lead_mask(start), (EDGE, LANES)).astype(BF16)
    ahead_ref[:EDGE, feats:] = jnp.broadcast_to(tail_mask(start), (EDGE, LANES)).astype(BF16)
    copies[1].wait()
    back_ref[:, :feats] = hidden_ref[:EDGE]
    ahead_ref[:EDGE, :feats] = hidden_ref[bytes_ - EDGE :]
    rows.wait()
    chosen = iota((EDGE, width), 0) == last - group
    row = jnp.sum(jnp.where(chosen, rows_v[...].astype(F32), 0.0), axis=0, keepdims=True)
    ahead_ref[EDGE:] = jnp.zeros((EDGE, feats + LANES), BF16)
    for at in range(width // feats):
        piece = row[:, at * feats : (at + 1) * feats]
        spread = jnp.where(iota((EDGE, feats), 0) == at, piece, 0.0)
        old = ahead_ref[EDGE:, :feats].astype(F32)
        ahead_ref[EDGE:, :feats] = (old + spread).astype(BF16)


def pool_kernel(hidden_ref, next_ref, start_ref, query_ref, low_ref, pooled_ref, denom_ref):
    bytes_, feats = hidden_ref.shape
    slots = low_ref.shape[0]
    query = row_of(query_ref)
    rows, last = segment_rows(start_ref[...])
    segment = jnp.concatenate(rows, axis=1).astype(jnp.int32)
    onehot = jnp.where(iota((slots, bytes_), 0) == segment, 1.0, 0.0).astype(BF16)
    hidden = hidden_ref[...].astype(F32)
    _, weight = scores(hidden, query)
    numer = dot_split(onehot, weight * hidden)
    denom = dot_split(onehot, weight)
    following = next_ref[:, :feats].astype(F32)
    mask = next_ref[:, feats : feats + 1].astype(F32)
    extra = scores(following, query)[1] * mask
    is_last = iota((slots, feats), 0) == last.astype(jnp.int32)
    denom = denom + jnp.where(is_last, jnp.sum(extra, axis=0, keepdims=True), 0.0)
    numer = numer + jnp.where(is_last, jnp.sum(extra * following, axis=0, keepdims=True), 0.0)
    live = denom > 0.0
    pooled = jnp.where(live, numer / jnp.where(live, denom, 1.0), 0.0)
    low_ref[...] = pooled.astype(BF16)
    pooled_ref[...] = pooled
    denom_ref[...] = denom


def spread_kernel(hidden_ref, prev_ref, start_ref, query_ref, pooled_ref, denom_ref,
                  onehot_ref, share_ref, delta_ref, slope_ref):
    bytes_, feats = hidden_ref.shape
    slots = pooled_ref.shape[0]
    query = row_of(query_ref)
    rows, _ = segment_rows(start_ref[...])
    columns = [jnp.transpose(jnp.broadcast_to(row, (LANES, LANES))) for row in rows]
    segment = jnp.concatenate(columns, axis=0).astype(jnp.int32)
    onehot = jnp.concatenate(
        [
            jnp.where(segment == iota((bytes_, LANES), 1) + offset, 1.0, 0.0).astype(BF16)
            for offset in range(0, slots, LANES)
        ],
        axis=1,
    )
    onehot_ref[...] = onehot
    hidden = hidden_ref[...].astype(F32)
    bent, weight = scores(hidden, query)
    before = prev_ref[:EDGE, :feats].astype(F32)
    part = scores(before, query)[1] * prev_ref[:EDGE, feats : feats + 1].astype(F32)
    lead = lead_mask(start_ref[...])
    own = weight[:EDGE] * lead
    first_denom = jnp.sum(part + own, axis=0, keepdims=True)
    first_numer = jnp.sum(part * before + own * hidden[:EDGE], axis=0, keepdims=True)
    full = first_denom > 0.0
    first_pooled = jnp.where(full, first_numer / jnp.where(full, first_denom, 1.0), 0.0)
    denom = dot_split(onehot, denom_ref[...])
    pooled = dot_split(onehot, pooled_ref[...])
    denom = jnp.concatenate([denom[:EDGE] + lead * first_denom, denom[EDGE:]], axis=0)
    pooled = jnp.concatenate([pooled[:EDGE] + lead * first_pooled, pooled[EDGE:]], axis=0)
    share = weight / denom
    share_ref[...] = share
    delta_ref[...] = hidden - pooled
    slope_ref[...] = share * (1.0 - bent * bent) * (inv_root * query)


def bytes_kernel(parts, *refs):
    recv_refs, (start_ref, onehot_ref, share_ref, delta_ref, slope_ref, out_ref) = (
        refs[:parts],
        refs[parts:],
    )
    slots = onehot_ref.shape[1]
    grad = recv_refs[0][...].astype(F32)
    for ref in recv_refs[1:]:
        grad = grad + ref[...].astype(F32)
    rows = dot_split(onehot_ref[...], grad[:slots])
    first = jnp.sum(grad[slots:], axis=0, keepdims=True)
    rows = jnp.concatenate([rows[:EDGE] + lead_mask(start_ref[...]) * first, rows[EDGE:]], axis=0)
    inner = head_sum(rows * delta_ref[...])
    out_ref[...] = (share_ref[...] * rows + slope_ref[...] * inner).astype(BF16)


def gather_parts(part_refs, full_ref):
    feats = part_refs[0].shape[1]
    place = lax.axis_index("mp")
    for index, ref in enumerate(part_refs):
        owner = pl.multiple_of((place ^ index) * feats, feats)
        full_ref[:, pl.ds(owner, feats)] = ref[...]


def outer_kernel(parts, scale, *refs):
    part_refs, grad_ref, out_refs = refs[:parts], refs[parts], refs[parts + 1 : -2]
    full_ref, terms_ref = refs[-2:]
    gather_parts(part_refs, full_ref)
    terms_ref[...] = dot(full_ref[...], grad_ref[...], ((0,), (0,))) * scale
    if len(out_refs) == 1:
        out_refs[0][...] = terms_ref[...].astype(out_refs[0].dtype)
        return
    place = lax.axis_index("seq")
    rows = out_refs[0].shape[0]
    for index, ref in enumerate(out_refs):
        owner = pl.multiple_of((place ^ index) * rows, rows)
        ref[...] = terms_ref[pl.ds(owner, rows), :].astype(ref.dtype)


def latent_kernel(parts, *refs):
    part_refs, (weight_ref, out_ref, full_ref) = refs[:parts], refs[parts:]
    gather_parts(part_refs, full_ref)
    out_ref[...] = dot(full_ref[...], weight_ref[...]).astype(BF16)


def partial_kernel(parts, grad_ref, prev_ref, *refs):
    piece_refs, out_refs, full_ref = refs[: -parts - 1], refs[-parts - 1 : -1], refs[-1]
    slots, width = grad_ref.shape
    feats = out_refs[0].shape[1]
    if len(piece_refs) == 1:
        full_ref[...] = piece_refs[0][...]
    else:
        rows = piece_refs[0].shape[0]
        spot = lax.axis_index("seq")
        for index, ref in enumerate(piece_refs):
            owner = pl.multiple_of((spot ^ index) * rows, rows)
            full_ref[pl.ds(owner, rows), :] = ref[...]
    last = prev_ref[EDGE:, :feats].astype(F32)
    row = jnp.concatenate([last[at : at + 1] for at in range(width // feats)], axis=1)
    row = jnp.where(iota((EDGE, width), 0) == 0, row, 0.0).astype(BF16)
    place = lax.axis_index("mp")
    for index, ref in enumerate(out_refs):
        owner = pl.multiple_of((place ^ index) * feats, feats)
        block = full_ref[pl.ds(owner, feats), :]
        ref[:slots] = dot(grad_ref[...], block, ((1,), (1,))).astype(BF16)
        ref[slots:] = dot(row, block, ((1,), (1,))).astype(BF16)


def call(kernel, out_shape, *args, flops=0, scratch=(), in_specs=None, limit=VMEM_LIMIT):
    if in_specs is None:
        in_specs = [pl.BlockSpec(memory_space=pltpu.VMEM)] * len(args)
    return pl.pallas_call(
        kernel,
        out_shape=out_shape,
        in_specs=in_specs,
        out_specs=jax.tree.map(lambda _: pl.BlockSpec(memory_space=pltpu.VMEM), out_shape),
        scratch_shapes=list(scratch),
        cost_estimate=pl.CostEstimate(flops=0, bytes_accessed=0, transcendentals=0),
        compiler_params=pltpu.CompilerParams(vmem_limit_bytes=limit),
    )(*args)


def shape(dims, dtype):
    return jax.ShapeDtypeStruct(dims, dtype)


VMEM = pl.BlockSpec(memory_space=pltpu.VMEM)
after = lax.optimization_barrier
HBM = pl.BlockSpec(memory_space=pltpu.HBM)


def shards(byte_hidden, patch_start, pool_query, in_weight, latent_grad):
    bytes_, feats = byte_hidden.shape
    slots, width = latent_grad.shape
    n_seq, n_mp = lax.axis_size("seq"), lax.axis_size("mp")
    latent_dim = feats * n_mp
    rows = latent_dim // n_seq
    staged = n_seq == 8

    def swap(value, step):
        return lax.ppermute(value, "mp", [(i, i ^ step) for i in range(n_mp)])

    def trade(value, step):
        return lax.ppermute(value, "seq", [(i, i ^ step) for i in range(n_seq)])

    arguments = (
        byte_hidden,
        patch_start.reshape(bytes_ // LANES, LANES),
        latent_grad,
    )
    query = pool_query.reshape(feats // LANES, LANES)
    back, ahead, byte_hidden, start = call(
        load_kernel,
        (
            shape((EDGE, feats + LANES), BF16),
            shape((2 * EDGE, feats + LANES), BF16),
            shape(byte_hidden.shape, BF16),
            shape(arguments[1].shape, jnp.int32),
        ),
        *arguments,
        in_specs=[HBM] * len(arguments),
        limit=VMEM_MOST,
        scratch=(
            pltpu.VMEM((EDGE, width), BF16),
            pltpu.SemaphoreType.DMA((len(arguments),)),
        ),
    )
    following = lax.ppermute(back, "seq", [(i, i - 1) for i in range(1, n_seq)])
    previous = lax.ppermute(ahead, "seq", [(i, i + 1) for i in range(n_seq - 1)])

    if staged:
        in_weight, _ = after((in_weight, back))
        pieces = [in_weight] + [None] * (n_seq - 1)
        for step in (1, 2, 4):
            pieces[step] = trade(in_weight, step)
        pieces[6] = trade(pieces[4], 2)
    else:
        pieces = [lax.all_gather(in_weight, "seq", axis=0, tiled=True)]

    low, pooled, denom = call(
        pool_kernel,
        (shape((slots, feats), BF16), shape((slots, feats), F32), shape((slots, feats), F32)),
        byte_hidden,
        following,
        start,
        query,
        flops=8 * bytes_ * slots * feats,
    )

    if staged:
        low, *pieces[1:3] = after((low, *pieces[1:3]))
        pieces[3] = trade(after((pieces[2], low))[0], 1)
    parts = [low]
    for step in reversed([1 << bit for bit in range(n_mp.bit_length() - 1)]):
        if staged and step == 1:
            parts[0], _ = after((parts[0], (pieces[4], pieces[3], previous)))
        parts = [part for held in parts for part in (held, swap(held, step))]
    onehot, share, delta, slope = call(
        spread_kernel,
        (shape((bytes_, slots), BF16),) + (shape((bytes_, feats), F32),) * 3,
        byte_hidden,
        previous,
        start,
        query,
        pooled,
        denom,
        flops=8 * bytes_ * slots * feats,
    )
    work = 2 * slots * width * latent_dim
    scale = 1.0 / math.sqrt(n_seq * slots)
    if staged:
        blocks = [shape((rows, width), BF16 if index % 2 else F32) for index in range(n_seq)]
    else:
        blocks = [shape((latent_dim, width), BF16)]
    terms = call(
        functools.partial(outer_kernel, n_mp, scale),
        tuple(blocks),
        *parts,
        latent_grad,
        flops=work,
        scratch=(pltpu.VMEM((slots, latent_dim), BF16), pltpu.VMEM((latent_dim, width), F32)),
    )
    if staged:
        fetched = {}
        fetched[7] = trade(terms[7], 1)
        pieces[5] = trade(pieces[4], 1)
        pieces[7] = trade(after((pieces[6], fetched[7], pieces[5]))[0], 1)
        fetched[5] = trade(after((terms[5], pieces[5]))[0], 1)

    *partials, weight_full = call(
        functools.partial(partial_kernel, n_mp),
        (shape((slots + EDGE, feats), BF16),) * n_mp + (shape((latent_dim, width), BF16),),
        latent_grad,
        previous,
        *pieces,
        flops=work,
    )
    grads = [partials[0]] + [swap(partials[step], step) for step in range(1, n_mp)]

    if staged:
        fetched[6] = trade((terms[6] + fetched[7].astype(F32)).astype(BF16), 2)
        fetched[3] = trade(after((terms[3], weight_full, share, fetched[6]))[0], 1)
        pair = terms[4] + fetched[5].astype(F32) + fetched[6].astype(F32)
        fetched[4] = trade(pair.astype(BF16), 4)
        fetched[1] = trade(after((terms[1], fetched[5], grads[2]))[0], 1)
        fetched[2] = trade((terms[2] + fetched[3].astype(F32)).astype(BF16), 2)
        grad_weight = terms[0] + fetched[1].astype(F32)
        for step in (4, 2):
            grad_weight = grad_weight + fetched[step].astype(F32)
    else:
        received = lax.all_to_all(terms[0], "seq", split_axis=0, concat_axis=0, tiled=True)
        grad_weight = received.reshape(n_seq, rows, width).astype(F32).sum(0)

    latent = call(
        functools.partial(latent_kernel, n_mp),
        shape((slots, width), BF16),
        *parts,
        weight_full,
        flops=work,
        scratch=(pltpu.VMEM((slots, latent_dim), BF16),),
    )
    grad_bytes = call(
        functools.partial(bytes_kernel, n_mp),
        shape((bytes_, feats), BF16),
        *grads,
        start,
        onehot,
        share,
        delta,
        slope,
        flops=4 * bytes_ * slots * feats,
    )
    return latent, grad_weight, grad_bytes


def solution(mesh):
    in_specs = (P("seq", "mp"), P("seq"), P("mp"), P("seq", "mp"), P("seq", "mp"))
    out_specs = (P("seq", "mp"), P("seq", "mp"), P("seq", "mp"))
    return jax.shard_map(shards, mesh=mesh, in_specs=in_specs, out_specs=out_specs, check_vma=False)
```

```python
import functools
import math

import jax
import jax.numpy as jnp
from jax import lax
from jax.experimental import pallas as pl
from jax.experimental.pallas import tpu as pltpu
from jax.sharding import PartitionSpec as P

HEAD_DIM = 64
EDGE = 16
LANES = 128

soft_cap = 20.0
inv_root = 1.0 / math.sqrt(HEAD_DIM)
F32 = jnp.float32
BF16 = jnp.bfloat16
VMEM_LIMIT = 48 * 1024 * 1024
VMEM_MOST = 53 * 1024 * 1024


def iota(shape, dim):
    return lax.broadcasted_iota(jnp.int32, shape, dim)


def split(value):
    high = value.astype(BF16)
    return high, (value - high.astype(F32)).astype(BF16)


def dot(left, right, dims=((1,), (0,))):
    return lax.dot_general(left, right, (dims, ((), ())), preferred_element_type=F32)


def dot_split(left, value):
    high, low = split(value)
    return dot(left, high) + dot(left, low)


def head_sum(value):
    feats = value.shape[1]
    same = (iota((feats, feats), 0) // HEAD_DIM) == (iota((feats, feats), 1) // HEAD_DIM)
    block = jnp.where(same, 1.0, 0.0).astype(BF16)
    high, low = split(value)
    return dot(high, block) + dot(low, block)


def row_of(ref):
    value = ref[...].astype(F32)
    return jnp.concatenate([value[at : at + 1] for at in range(value.shape[0])], axis=1)


def scores(hidden, query):
    raw = head_sum(hidden * query) * inv_root
    bent = jnp.tanh(raw / soft_cap)
    return bent, jnp.exp(soft_cap * bent)


def segment_rows(start):
    upper = jnp.where(iota((LANES, LANES), 0) <= iota((LANES, LANES), 1), 1.0, 0.0).astype(BF16)
    count = dot(start.astype(F32).astype(BF16), upper)
    rows, total = [], jnp.full((1, 1), -1.0, F32)
    for index in range(start.shape[0]):
        row = count[index : index + 1]
        rows.append(row + total)
        total = total + row[:, LANES - 1 :]
    return rows, total


def lead_mask(start):
    first = jnp.broadcast_to(start[0:1].astype(F32), (EDGE, LANES))
    before = jnp.where(iota((EDGE, LANES), 1) <= iota((EDGE, LANES), 0), first, 0.0)
    return jnp.where(jnp.sum(before, axis=1, keepdims=True) > 0.0, 0.0, 1.0)


def tail_mask(start):
    rows = start.shape[0]
    last = jnp.broadcast_to(start[rows - 1 : rows].astype(F32), (EDGE, LANES))
    after = jnp.where(iota((EDGE, LANES), 1) > iota((EDGE, LANES), 0) + (LANES - EDGE), last, 0.0)
    return jnp.where(jnp.sum(after, axis=1, keepdims=True) > 0.0, 0.0, 1.0)


def load_kernel(hidden_hbm, start_hbm, grad_hbm,
                back_ref, ahead_ref, hidden_ref, start_ref, rows_v, sem):
    pairs = [(start_hbm, start_ref), (hidden_hbm, hidden_ref)]
    copies = [pltpu.make_async_copy(*pair, sem.at[at]) for at, pair in enumerate(pairs)]
    for copy in copies:
        copy.start()
    bytes_, feats = hidden_ref.shape
    width = grad_hbm.shape[1]
    copies[0].wait()
    start = start_ref[...]
    last = jnp.sum(start) - 1
    group = pl.multiple_of((last // EDGE) * EDGE, EDGE)
    rows = pltpu.make_async_copy(grad_hbm.at[pl.ds(group, EDGE), :], rows_v, sem.at[2])
    rows.start()
    back_ref[:, feats:] = jnp.broadcast_to(lead_mask(start), (EDGE, LANES)).astype(BF16)
    ahead_ref[:EDGE, feats:] = jnp.broadcast_to(tail_mask(start), (EDGE, LANES)).astype(BF16)
    copies[1].wait()
    back_ref[:, :feats] = hidden_ref[:EDGE]
    ahead_ref[:EDGE, :feats] = hidden_ref[bytes_ - EDGE :]
    rows.wait()
    chosen = iota((EDGE, width), 0) == last - group
    row = jnp.sum(jnp.where(chosen, rows_v[...].astype(F32), 0.0), axis=0, keepdims=True)
    ahead_ref[EDGE:] = jnp.zeros((EDGE, feats + LANES), BF16)
    for at in range(width // feats):
        piece = row[:, at * feats : (at + 1) * feats]
        spread = jnp.where(iota((EDGE, feats), 0) == at, piece, 0.0)
        old = ahead_ref[EDGE:, :feats].astype(F32)
        ahead_ref[EDGE:, :feats] = (old + spread).astype(BF16)


def pool_kernel(hidden_ref, next_ref, start_ref, query_ref, low_ref, pooled_ref, denom_ref):
    bytes_, feats = hidden_ref.shape
    slots = low_ref.shape[0]
    query = row_of(query_ref)
    rows, last = segment_rows(start_ref[...])
    segment = jnp.concatenate(rows, axis=1).astype(jnp.int32)
    onehot = jnp.where(iota((slots, bytes_), 0) == segment, 1.0, 0.0).astype(BF16)
    hidden = hidden_ref[...].astype(F32)
    _, weight = scores(hidden, query)
    numer = dot_split(onehot, weight * hidden)
    denom = dot_split(onehot, weight)
    following = next_ref[:, :feats].astype(F32)
    mask = next_ref[:, feats : feats + 1].astype(F32)
    extra = scores(following, query)[1] * mask
    is_last = iota((slots, feats), 0) == last.astype(jnp.int32)
    denom = denom + jnp.where(is_last, jnp.sum(extra, axis=0, keepdims=True), 0.0)
    numer = numer + jnp.where(is_last, jnp.sum(extra * following, axis=0, keepdims=True), 0.0)
    live = denom > 0.0
    pooled = jnp.where(live, numer / jnp.where(live, denom, 1.0), 0.0)
    low_ref[...] = pooled.astype(BF16)
    pooled_ref[...] = pooled
    denom_ref[...] = denom


def spread_kernel(hidden_ref, prev_ref, start_ref, query_ref, pooled_ref, denom_ref,
                  onehot_ref, share_ref, delta_ref, slope_ref):
    bytes_, feats = hidden_ref.shape
    slots = pooled_ref.shape[0]
    query = row_of(query_ref)
    rows, _ = segment_rows(start_ref[...])
    columns = [jnp.transpose(jnp.broadcast_to(row, (LANES, LANES))) for row in rows]
    segment = jnp.concatenate(columns, axis=0).astype(jnp.int32)
    onehot = jnp.concatenate(
        [
            jnp.where(segment == iota((bytes_, LANES), 1) + offset, 1.0, 0.0).astype(BF16)
            for offset in range(0, slots, LANES)
        ],
        axis=1,
    )
    onehot_ref[...] = onehot
    hidden = hidden_ref[...].astype(F32)
    bent, weight = scores(hidden, query)
    before = prev_ref[:EDGE, :feats].astype(F32)
    part = scores(before, query)[1] * prev_ref[:EDGE, feats : feats + 1].astype(F32)
    lead = lead_mask(start_ref[...])
    own = weight[:EDGE] * lead
    first_denom = jnp.sum(part + own, axis=0, keepdims=True)
    first_numer = jnp.sum(part * before + own * hidden[:EDGE], axis=0, keepdims=True)
    full = first_denom > 0.0
    first_pooled = jnp.where(full, first_numer / jnp.where(full, first_denom, 1.0), 0.0)
    denom = dot_split(onehot, denom_ref[...])
    pooled = dot_split(onehot, pooled_ref[...])
    denom = jnp.concatenate([denom[:EDGE] + lead * first_denom, denom[EDGE:]], axis=0)
    pooled = jnp.concatenate([pooled[:EDGE] + lead * first_pooled, pooled[EDGE:]], axis=0)
    share = weight / denom
    share_ref[...] = share
    delta_ref[...] = hidden - pooled
    slope_ref[...] = share * (1.0 - bent * bent) * (inv_root * query)


def bytes_kernel(parts, *refs):
    recv_refs, (start_ref, onehot_ref, share_ref, delta_ref, slope_ref, out_ref) = (
        refs[:parts],
        refs[parts:],
    )
    slots = onehot_ref.shape[1]
    grad = recv_refs[0][...].astype(F32)
    for ref in recv_refs[1:]:
        grad = grad + ref[...].astype(F32)
    rows = dot_split(onehot_ref[...], grad[:slots])
    first = jnp.sum(grad[slots:], axis=0, keepdims=True)
    rows = jnp.concatenate([rows[:EDGE] + lead_mask(start_ref[...]) * first, rows[EDGE:]], axis=0)
    inner = head_sum(rows * delta_ref[...])
    out_ref[...] = (share_ref[...] * rows + slope_ref[...] * inner).astype(BF16)


def gather_parts(part_refs, full_ref):
    feats = part_refs[0].shape[1]
    place = lax.axis_index("mp")
    for index, ref in enumerate(part_refs):
        owner = pl.multiple_of((place ^ index) * feats, feats)
        full_ref[:, pl.ds(owner, feats)] = ref[...]


def outer_kernel(parts, scale, *refs):
    part_refs, grad_ref, out_refs = refs[:parts], refs[parts], refs[parts + 1 : -2]
    full_ref, terms_ref = refs[-2:]
    gather_parts(part_refs, full_ref)
    terms_ref[...] = dot(full_ref[...], grad_ref[...], ((0,), (0,))) * scale
    if len(out_refs) == 1:
        out_refs[0][...] = terms_ref[...].astype(out_refs[0].dtype)
        return
    place = lax.axis_index("seq")
    rows = out_refs[0].shape[0]
    for index, ref in enumerate(out_refs):
        owner = pl.multiple_of((place ^ index) * rows, rows)
        ref[...] = terms_ref[pl.ds(owner, rows), :].astype(ref.dtype)


def latent_kernel(parts, *refs):
    part_refs, (weight_ref, out_ref, full_ref) = refs[:parts], refs[parts:]
    gather_parts(part_refs, full_ref)
    out_ref[...] = dot(full_ref[...], weight_ref[...]).astype(BF16)


def partial_kernel(parts, grad_ref, prev_ref, *refs):
    piece_refs, out_refs, full_ref = refs[: -parts - 1], refs[-parts - 1 : -1], refs[-1]
    slots, width = grad_ref.shape
    feats = out_refs[0].shape[1]
    if len(piece_refs) == 1:
        full_ref[...] = piece_refs[0][...]
    else:
        rows = piece_refs[0].shape[0]
        spot = lax.axis_index("seq")
        for index, ref in enumerate(piece_refs):
            owner = pl.multiple_of((spot ^ index) * rows, rows)
            full_ref[pl.ds(owner, rows), :] = ref[...]
    last = prev_ref[EDGE:, :feats].astype(F32)
    row = jnp.concatenate([last[at : at + 1] for at in range(width // feats)], axis=1)
    row = jnp.where(iota((EDGE, width), 0) == 0, row, 0.0).astype(BF16)
    place = lax.axis_index("mp")
    for index, ref in enumerate(out_refs):
        owner = pl.multiple_of((place ^ index) * feats, feats)
        block = full_ref[pl.ds(owner, feats), :]
        ref[:slots] = dot(grad_ref[...], block, ((1,), (1,))).astype(BF16)
        ref[slots:] = dot(row, block, ((1,), (1,))).astype(BF16)


def call(kernel, out_shape, *args, flops=0, scratch=(), in_specs=None, limit=VMEM_LIMIT):
    if in_specs is None:
        in_specs = [pl.BlockSpec(memory_space=pltpu.VMEM)] * len(args)
    return pl.pallas_call(
        kernel,
        out_shape=out_shape,
        in_specs=in_specs,
        out_specs=jax.tree.map(lambda _: pl.BlockSpec(memory_space=pltpu.VMEM), out_shape),
        scratch_shapes=list(scratch),
        cost_estimate=pl.CostEstimate(flops=0, bytes_accessed=0, transcendentals=0),
        compiler_params=pltpu.CompilerParams(vmem_limit_bytes=limit),
    )(*args)


def shape(dims, dtype):
    return jax.ShapeDtypeStruct(dims, dtype)


VMEM = pl.BlockSpec(memory_space=pltpu.VMEM)
after = lax.optimization_barrier
HBM = pl.BlockSpec(memory_space=pltpu.HBM)


def shards(byte_hidden, patch_start, pool_query, in_weight, latent_grad):
    bytes_, feats = byte_hidden.shape
    slots, width = latent_grad.shape
    n_seq, n_mp = lax.axis_size("seq"), lax.axis_size("mp")
    latent_dim = feats * n_mp
    rows = latent_dim // n_seq
    staged = n_seq == 8

    def swap(value, step):
        return lax.ppermute(value, "mp", [(i, i ^ step) for i in range(n_mp)])

    def trade(value, step):
        return lax.ppermute(value, "seq", [(i, i ^ step) for i in range(n_seq)])

    arguments = (
        byte_hidden,
        patch_start.reshape(bytes_ // LANES, LANES),
        latent_grad,
    )
    query = pool_query.reshape(feats // LANES, LANES)
    back, ahead, byte_hidden, start = call(
        load_kernel,
        (
            shape((EDGE, feats + LANES), BF16),
            shape((2 * EDGE, feats + LANES), BF16),
            shape(byte_hidden.shape, BF16),
            shape(arguments[1].shape, jnp.int32),
        ),
        *arguments,
        in_specs=[HBM] * len(arguments),
        limit=VMEM_MOST,
        scratch=(
            pltpu.VMEM((EDGE, width), BF16),
            pltpu.SemaphoreType.DMA((len(arguments),)),
        ),
    )
    following = lax.ppermute(back, "seq", [(i, i - 1) for i in range(1, n_seq)])
    previous = lax.ppermute(ahead, "seq", [(i, i + 1) for i in range(n_seq - 1)])

    if staged:
        in_weight, _ = after((in_weight, back))
        pieces = [in_weight] + [None] * (n_seq - 1)
        for step in (1, 2, 4):
            pieces[step] = trade(in_weight, step)
        pieces[6] = trade(pieces[4], 2)
    else:
        pieces = [lax.all_gather(in_weight, "seq", axis=0, tiled=True)]

    low, pooled, denom = call(
        pool_kernel,
        (shape((slots, feats), BF16), shape((slots, feats), F32), shape((slots, feats), F32)),
        byte_hidden,
        following,
        start,
        query,
        flops=8 * bytes_ * slots * feats,
    )

    if staged:
        low, *pieces[1:3] = after((low, *pieces[1:3]))
        pieces[3] = trade(after((pieces[2], low))[0], 1)
    parts = [low]
    for step in reversed([1 << bit for bit in range(n_mp.bit_length() - 1)]):
        if staged and step == 1:
            parts[0], _ = after((parts[0], (pieces[4], pieces[3], previous)))
        parts = [part for held in parts for part in (held, swap(held, step))]
    onehot, share, delta, slope = call(
        spread_kernel,
        (shape((bytes_, slots), BF16),) + (shape((bytes_, feats), F32),) * 3,
        byte_hidden,
        previous,
        start,
        query,
        pooled,
        denom,
        flops=8 * bytes_ * slots * feats,
    )
    work = 2 * slots * width * latent_dim
    scale = 1.0 / math.sqrt(n_seq * slots)
    if staged:
        blocks = [shape((rows, width), BF16 if index % 2 else F32) for index in range(n_seq)]
    else:
        blocks = [shape((latent_dim, width), BF16)]
    terms = call(
        functools.partial(outer_kernel, n_mp, scale),
        tuple(blocks),
        *parts,
        latent_grad,
        flops=work,
        scratch=(pltpu.VMEM((slots, latent_dim), BF16), pltpu.VMEM((latent_dim, width), F32)),
    )
    if staged:
        fetched = {}
        pieces[5] = trade(pieces[4], 1)
        fetched[7] = trade(after((terms[7], pieces[5]))[0], 1)
        pieces[7] = trade(after((pieces[6], terms[0]))[0], 1)
        fetched[5] = trade(after((terms[5], fetched[7]))[0], 1)

    *partials, weight_full = call(
        functools.partial(partial_kernel, n_mp),
        (shape((slots + EDGE, feats), BF16),) * n_mp + (shape((latent_dim, width), BF16),),
        latent_grad,
        previous,
        *pieces,
        flops=work,
    )
    if n_mp == 4:
        near = swap(partials[3], 1)
        pair = partials[2].astype(F32) + near.astype(F32)
        grads = [partials[0], swap(partials[1], 1), swap(pair.astype(BF16), 2)]
    else:
        near, grads = None, [swap(partials[step], step) for step in range(n_mp)]

    if staged:
        fetched[6] = trade((terms[6] + fetched[7].astype(F32)).astype(BF16), 2)
        fetched[3] = trade(after((terms[3], weight_full, share, fetched[6]))[0], 1)
        pair = terms[4] + fetched[5].astype(F32) + fetched[6].astype(F32)
        fetched[4] = trade(pair.astype(BF16), 4)
        fetched[1] = trade(after((terms[1], fetched[3], near))[0], 1)
        fetched[2] = trade((terms[2] + fetched[3].astype(F32)).astype(BF16), 2)
        grad_weight = terms[0] + fetched[1].astype(F32)
        for step in (4, 2):
            grad_weight = grad_weight + fetched[step].astype(F32)
    else:
        received = lax.all_to_all(terms[0], "seq", split_axis=0, concat_axis=0, tiled=True)
        grad_weight = received.reshape(n_seq, rows, width).astype(F32).sum(0)

    latent = call(
        functools.partial(latent_kernel, n_mp),
        shape((slots, width), BF16),
        *parts,
        weight_full,
        flops=work,
        scratch=(pltpu.VMEM((slots, latent_dim), BF16),),
    )
    grad_bytes = call(
        functools.partial(bytes_kernel, len(grads)),
        shape((bytes_, feats), BF16),
        *grads,
        start,
        onehot,
        share,
        delta,
        slope,
        flops=4 * bytes_ * slots * feats,
    )
    return latent, grad_weight, grad_bytes


def solution(mesh):
    in_specs = (P("seq", "mp"), P("seq"), P("mp"), P("seq", "mp"), P("seq", "mp"))
    out_specs = (P("seq", "mp"), P("seq", "mp"), P("seq", "mp"))
    return jax.shard_map(shards, mesh=mesh, in_specs=in_specs, out_specs=out_specs, check_vma=False)
```

```python
import functools
import math

import jax
import jax.numpy as jnp
from jax import lax
from jax.experimental import pallas as pl
from jax.experimental.pallas import tpu as pltpu
from jax.sharding import PartitionSpec as P

HEAD_DIM = 64
EDGE = 16
LANES = 128

soft_cap = 20.0
inv_root = 1.0 / math.sqrt(HEAD_DIM)
F32 = jnp.float32
BF16 = jnp.bfloat16
VMEM_LIMIT = 48 * 1024 * 1024
VMEM_MOST = 53 * 1024 * 1024


def iota(shape, dim):
    return lax.broadcasted_iota(jnp.int32, shape, dim)


def split(value):
    high = value.astype(BF16)
    return high, (value - high.astype(F32)).astype(BF16)


def dot(left, right, dims=((1,), (0,))):
    return lax.dot_general(left, right, (dims, ((), ())), preferred_element_type=F32)


def dot_split(left, value):
    high, low = split(value)
    return dot(left, high) + dot(left, low)


def head_sum(value):
    feats = value.shape[1]
    same = (iota((feats, feats), 0) // HEAD_DIM) == (iota((feats, feats), 1) // HEAD_DIM)
    block = jnp.where(same, 1.0, 0.0).astype(BF16)
    high, low = split(value)
    return dot(high, block) + dot(low, block)


def row_of(ref):
    value = ref[...].astype(F32)
    return jnp.concatenate([value[at : at + 1] for at in range(value.shape[0])], axis=1)


def scores(hidden, query):
    raw = head_sum(hidden * query) * inv_root
    bent = jnp.tanh(raw / soft_cap)
    return bent, jnp.exp(soft_cap * bent)


def segment_rows(start):
    upper = jnp.where(iota((LANES, LANES), 0) <= iota((LANES, LANES), 1), 1.0, 0.0).astype(BF16)
    count = dot(start.astype(F32).astype(BF16), upper)
    rows, total = [], jnp.full((1, 1), -1.0, F32)
    for index in range(start.shape[0]):
        row = count[index : index + 1]
        rows.append(row + total)
        total = total + row[:, LANES - 1 :]
    return rows, total


def lead_mask(start):
    first = jnp.broadcast_to(start[0:1].astype(F32), (EDGE, LANES))
    before = jnp.where(iota((EDGE, LANES), 1) <= iota((EDGE, LANES), 0), first, 0.0)
    return jnp.where(jnp.sum(before, axis=1, keepdims=True) > 0.0, 0.0, 1.0)


def tail_mask(start):
    rows = start.shape[0]
    last = jnp.broadcast_to(start[rows - 1 : rows].astype(F32), (EDGE, LANES))
    after = jnp.where(iota((EDGE, LANES), 1) > iota((EDGE, LANES), 0) + (LANES - EDGE), last, 0.0)
    return jnp.where(jnp.sum(after, axis=1, keepdims=True) > 0.0, 0.0, 1.0)


def load_kernel(hidden_hbm, start_hbm, grad_hbm,
                back_ref, ahead_ref, hidden_ref, start_ref, rows_v, sem):
    pairs = [(start_hbm, start_ref), (hidden_hbm, hidden_ref)]
    copies = [pltpu.make_async_copy(*pair, sem.at[at]) for at, pair in enumerate(pairs)]
    for copy in copies:
        copy.start()
    bytes_, feats = hidden_ref.shape
    width = grad_hbm.shape[1]
    copies[0].wait()
    start = start_ref[...]
    last = jnp.sum(start) - 1
    group = pl.multiple_of((last // EDGE) * EDGE, EDGE)
    rows = pltpu.make_async_copy(grad_hbm.at[pl.ds(group, EDGE), :], rows_v, sem.at[2])
    rows.start()
    back_ref[:, feats:] = jnp.broadcast_to(lead_mask(start), (EDGE, LANES)).astype(BF16)
    ahead_ref[:EDGE, feats:] = jnp.broadcast_to(tail_mask(start), (EDGE, LANES)).astype(BF16)
    copies[1].wait()
    back_ref[:, :feats] = hidden_ref[:EDGE]
    ahead_ref[:EDGE, :feats] = hidden_ref[bytes_ - EDGE :]
    rows.wait()
    chosen = iota((EDGE, width), 0) == last - group
    row = jnp.sum(jnp.where(chosen, rows_v[...].astype(F32), 0.0), axis=0, keepdims=True)
    ahead_ref[EDGE:] = jnp.zeros((EDGE, feats + LANES), BF16)
    for at in range(width // feats):
        piece = row[:, at * feats : (at + 1) * feats]
        spread = jnp.where(iota((EDGE, feats), 0) == at, piece, 0.0)
        old = ahead_ref[EDGE:, :feats].astype(F32)
        ahead_ref[EDGE:, :feats] = (old + spread).astype(BF16)


def pool_kernel(hidden_ref, next_ref, start_ref, query_ref, low_ref, pooled_ref, denom_ref):
    bytes_, feats = hidden_ref.shape
    slots = low_ref.shape[0]
    query = row_of(query_ref)
    rows, last = segment_rows(start_ref[...])
    segment = jnp.concatenate(rows, axis=1).astype(jnp.int32)
    onehot = jnp.where(iota((slots, bytes_), 0) == segment, 1.0, 0.0).astype(BF16)
    hidden = hidden_ref[...].astype(F32)
    _, weight = scores(hidden, query)
    numer = dot_split(onehot, weight * hidden)
    denom = dot_split(onehot, weight)
    following = next_ref[:, :feats].astype(F32)
    mask = next_ref[:, feats : feats + 1].astype(F32)
    extra = scores(following, query)[1] * mask
    is_last = iota((slots, feats), 0) == last.astype(jnp.int32)
    denom = denom + jnp.where(is_last, jnp.sum(extra, axis=0, keepdims=True), 0.0)
    numer = numer + jnp.where(is_last, jnp.sum(extra * following, axis=0, keepdims=True), 0.0)
    live = denom > 0.0
    pooled = jnp.where(live, numer / jnp.where(live, denom, 1.0), 0.0)
    low_ref[...] = pooled.astype(BF16)
    pooled_ref[...] = pooled
    denom_ref[...] = denom


def spread_kernel(hidden_ref, prev_ref, start_ref, query_ref, pooled_ref, denom_ref,
                  onehot_ref, share_ref, delta_ref, slope_ref):
    bytes_, feats = hidden_ref.shape
    slots = pooled_ref.shape[0]
    query = row_of(query_ref)
    rows, _ = segment_rows(start_ref[...])
    columns = [jnp.transpose(jnp.broadcast_to(row, (LANES, LANES))) for row in rows]
    segment = jnp.concatenate(columns, axis=0).astype(jnp.int32)
    onehot = jnp.concatenate(
        [
            jnp.where(segment == iota((bytes_, LANES), 1) + offset, 1.0, 0.0).astype(BF16)
            for offset in range(0, slots, LANES)
        ],
        axis=1,
    )
    onehot_ref[...] = onehot
    hidden = hidden_ref[...].astype(F32)
    bent, weight = scores(hidden, query)
    before = prev_ref[:EDGE, :feats].astype(F32)
    part = scores(before, query)[1] * prev_ref[:EDGE, feats : feats + 1].astype(F32)
    lead = lead_mask(start_ref[...])
    own = weight[:EDGE] * lead
    first_denom = jnp.sum(part + own, axis=0, keepdims=True)
    first_numer = jnp.sum(part * before + own * hidden[:EDGE], axis=0, keepdims=True)
    full = first_denom > 0.0
    first_pooled = jnp.where(full, first_numer / jnp.where(full, first_denom, 1.0), 0.0)
    denom = dot_split(onehot, denom_ref[...])
    pooled = dot_split(onehot, pooled_ref[...])
    denom = jnp.concatenate([denom[:EDGE] + lead * first_denom, denom[EDGE:]], axis=0)
    pooled = jnp.concatenate([pooled[:EDGE] + lead * first_pooled, pooled[EDGE:]], axis=0)
    share = weight / denom
    share_ref[...] = share
    delta_ref[...] = hidden - pooled
    slope_ref[...] = share * (1.0 - bent * bent) * (inv_root * query)


def bytes_kernel(parts, *refs):
    recv_refs, (start_ref, onehot_ref, share_ref, delta_ref, slope_ref, out_ref) = (
        refs[:parts],
        refs[parts:],
    )
    slots = onehot_ref.shape[1]
    grad = recv_refs[0][...].astype(F32)
    for ref in recv_refs[1:]:
        grad = grad + ref[...].astype(F32)
    rows = dot_split(onehot_ref[...], grad[:slots])
    first = jnp.sum(grad[slots:], axis=0, keepdims=True)
    rows = jnp.concatenate([rows[:EDGE] + lead_mask(start_ref[...]) * first, rows[EDGE:]], axis=0)
    inner = head_sum(rows * delta_ref[...])
    out_ref[...] = (share_ref[...] * rows + slope_ref[...] * inner).astype(BF16)


def gather_parts(part_refs, full_ref):
    feats = part_refs[0].shape[1]
    place = lax.axis_index("mp")
    for index, ref in enumerate(part_refs):
        owner = pl.multiple_of((place ^ index) * feats, feats)
        full_ref[:, pl.ds(owner, feats)] = ref[...]


def outer_kernel(parts, scale, *refs):
    part_refs, grad_ref, out_refs = refs[:parts], refs[parts], refs[parts + 1 : -2]
    full_ref, terms_ref = refs[-2:]
    gather_parts(part_refs, full_ref)
    terms_ref[...] = dot(full_ref[...], grad_ref[...], ((0,), (0,))) * scale
    if len(out_refs) == 1:
        out_refs[0][...] = terms_ref[...].astype(out_refs[0].dtype)
        return
    place = lax.axis_index("seq")
    rows = out_refs[0].shape[0]
    for index, ref in enumerate(out_refs):
        owner = pl.multiple_of((place ^ index) * rows, rows)
        ref[...] = terms_ref[pl.ds(owner, rows), :].astype(ref.dtype)


def latent_kernel(parts, *refs):
    part_refs, (weight_ref, out_ref, full_ref) = refs[:parts], refs[parts:]
    gather_parts(part_refs, full_ref)
    out_ref[...] = dot(full_ref[...], weight_ref[...]).astype(BF16)


def partial_kernel(parts, grad_ref, prev_ref, *refs):
    piece_refs, out_refs, full_ref = refs[: -parts - 1], refs[-parts - 1 : -1], refs[-1]
    slots, width = grad_ref.shape
    feats = out_refs[0].shape[1]
    if len(piece_refs) == 1:
        full_ref[...] = piece_refs[0][...]
    else:
        rows = piece_refs[0].shape[0]
        spot = lax.axis_index("seq")
        for index, ref in enumerate(piece_refs):
            owner = pl.multiple_of((spot ^ index) * rows, rows)
            full_ref[pl.ds(owner, rows), :] = ref[...]
    last = prev_ref[EDGE:, :feats].astype(F32)
    row = jnp.concatenate([last[at : at + 1] for at in range(width // feats)], axis=1)
    row = jnp.where(iota((EDGE, width), 0) == 0, row, 0.0).astype(BF16)
    place = lax.axis_index("mp")
    for index, ref in enumerate(out_refs):
        owner = pl.multiple_of((place ^ index) * feats, feats)
        block = full_ref[pl.ds(owner, feats), :]
        ref[:slots] = dot(grad_ref[...], block, ((1,), (1,))).astype(BF16)
        ref[slots:] = dot(row, block, ((1,), (1,))).astype(BF16)


def call(kernel, out_shape, *args, flops=0, scratch=(), in_specs=None, limit=VMEM_LIMIT):
    if in_specs is None:
        in_specs = [pl.BlockSpec(memory_space=pltpu.VMEM)] * len(args)
    return pl.pallas_call(
        kernel,
        out_shape=out_shape,
        in_specs=in_specs,
        out_specs=jax.tree.map(lambda _: pl.BlockSpec(memory_space=pltpu.VMEM), out_shape),
        scratch_shapes=list(scratch),
        cost_estimate=pl.CostEstimate(flops=0, bytes_accessed=0, transcendentals=0),
        compiler_params=pltpu.CompilerParams(vmem_limit_bytes=limit),
    )(*args)


def shape(dims, dtype):
    return jax.ShapeDtypeStruct(dims, dtype)


VMEM = pl.BlockSpec(memory_space=pltpu.VMEM)
after = lax.optimization_barrier
HBM = pl.BlockSpec(memory_space=pltpu.HBM)


def shards(byte_hidden, patch_start, pool_query, in_weight, latent_grad):
    bytes_, feats = byte_hidden.shape
    slots, width = latent_grad.shape
    n_seq, n_mp = lax.axis_size("seq"), lax.axis_size("mp")
    latent_dim = feats * n_mp
    rows = latent_dim // n_seq
    staged = n_seq == 8

    def swap(value, step):
        return lax.ppermute(value, "mp", [(i, i ^ step) for i in range(n_mp)])

    def trade(value, step):
        return lax.ppermute(value, "seq", [(i, i ^ step) for i in range(n_seq)])

    arguments = (
        byte_hidden,
        patch_start.reshape(bytes_ // LANES, LANES),
        latent_grad,
    )
    query = pool_query.reshape(feats // LANES, LANES)
    back, ahead, byte_hidden, start = call(
        load_kernel,
        (
            shape((EDGE, feats + LANES), BF16),
            shape((2 * EDGE, feats + LANES), BF16),
            shape(byte_hidden.shape, BF16),
            shape(arguments[1].shape, jnp.int32),
        ),
        *arguments,
        in_specs=[HBM] * len(arguments),
        limit=VMEM_MOST,
        scratch=(
            pltpu.VMEM((EDGE, width), BF16),
            pltpu.SemaphoreType.DMA((len(arguments),)),
        ),
    )
    following = lax.ppermute(back, "seq", [(i, i - 1) for i in range(1, n_seq)])
    previous = lax.ppermute(ahead, "seq", [(i, i + 1) for i in range(n_seq - 1)])

    if staged:
        in_weight, _ = after((in_weight, back))
        pieces = [in_weight] + [None] * (n_seq - 1)
        for step in (1, 2, 4):
            pieces[step] = trade(in_weight, step)
        pieces[6] = trade(pieces[4], 2)
    else:
        pieces = [lax.all_gather(in_weight, "seq", axis=0, tiled=True)]

    low, pooled, denom = call(
        pool_kernel,
        (shape((slots, feats), BF16), shape((slots, feats), F32), shape((slots, feats), F32)),
        byte_hidden,
        following,
        start,
        query,
        flops=8 * bytes_ * slots * feats,
    )

    if staged:
        low, *pieces[1:3] = after((low, *pieces[1:3]))
        pieces[3] = trade(after((pieces[2], low))[0], 1)
    parts = [low]
    for step in reversed([1 << bit for bit in range(n_mp.bit_length() - 1)]):
        if staged and step == 1:
            parts[0], _ = after((parts[0], (pieces[4], pieces[3], previous)))
        parts = [part for held in parts for part in (held, swap(held, step))]
    onehot, share, delta, slope = call(
        spread_kernel,
        (shape((bytes_, slots), BF16),) + (shape((bytes_, feats), F32),) * 3,
        byte_hidden,
        previous,
        start,
        query,
        pooled,
        denom,
        flops=8 * bytes_ * slots * feats,
    )
    work = 2 * slots * width * latent_dim
    scale = 1.0 / math.sqrt(n_seq * slots)
    if staged:
        blocks = [shape((rows, width), BF16 if index % 2 else F32) for index in range(n_seq)]
    else:
        blocks = [shape((latent_dim, width), BF16)]
    terms = call(
        functools.partial(outer_kernel, n_mp, scale),
        tuple(blocks),
        *parts,
        latent_grad,
        flops=work,
        scratch=(pltpu.VMEM((slots, latent_dim), BF16), pltpu.VMEM((latent_dim, width), F32)),
    )
    if staged:
        fetched = {}
        fetched[7] = trade(terms[7], 1)
        pieces[5] = trade(pieces[4], 1)
        pieces[7] = trade(after((pieces[5], terms[0]))[0], 2)
        fetched[5] = trade(after((terms[5], fetched[7]))[0], 1)

    *partials, weight_full = call(
        functools.partial(partial_kernel, n_mp),
        (shape((slots + EDGE, feats), BF16),) * n_mp + (shape((latent_dim, width), BF16),),
        latent_grad,
        previous,
        *pieces,
        flops=work,
    )
    grads = [partials[0]] + [swap(partials[step], step) for step in range(1, n_mp)]

    if staged:
        fetched[6] = trade((terms[6] + fetched[7].astype(F32)).astype(BF16), 2)
        fetched[3] = trade(after((terms[3], weight_full, share, fetched[6]))[0], 1)
        pair = terms[4] + fetched[5].astype(F32) + fetched[6].astype(F32)
        fetched[4] = trade(pair.astype(BF16), 4)
        fetched[1] = trade(after((terms[1], fetched[5], grads[2]))[0], 1)
        fetched[2] = trade((terms[2] + fetched[3].astype(F32)).astype(BF16), 2)
        grad_weight = terms[0] + fetched[1].astype(F32)
        for step in (4, 2):
            grad_weight = grad_weight + fetched[step].astype(F32)
    else:
        received = lax.all_to_all(terms[0], "seq", split_axis=0, concat_axis=0, tiled=True)
        grad_weight = received.reshape(n_seq, rows, width).astype(F32).sum(0)

    latent = call(
        functools.partial(latent_kernel, n_mp),
        shape((slots, width), BF16),
        *parts,
        weight_full,
        flops=work,
        scratch=(pltpu.VMEM((slots, latent_dim), BF16),),
    )
    grad_bytes = call(
        functools.partial(bytes_kernel, n_mp),
        shape((bytes_, feats), BF16),
        *grads,
        start,
        onehot,
        share,
        delta,
        slope,
        flops=4 * bytes_ * slots * feats,
    )
    return latent, grad_weight, grad_bytes


def solution(mesh):
    in_specs = (P("seq", "mp"), P("seq"), P("mp"), P("seq", "mp"), P("seq", "mp"))
    out_specs = (P("seq", "mp"), P("seq", "mp"), P("seq", "mp"))
    return jax.shard_map(shards, mesh=mesh, in_specs=in_specs, out_specs=out_specs, check_vma=False)
```

```python
import functools
import math

import jax
import jax.numpy as jnp
from jax import lax
from jax.experimental import pallas as pl
from jax.experimental.pallas import tpu as pltpu
from jax.sharding import PartitionSpec as P

HEAD_DIM = 64
EDGE = 16
LANES = 128

soft_cap = 20.0
inv_root = 1.0 / math.sqrt(HEAD_DIM)
F32 = jnp.float32
BF16 = jnp.bfloat16
VMEM_LIMIT = 48 * 1024 * 1024
VMEM_MOST = 53 * 1024 * 1024


def iota(shape, dim):
    return lax.broadcasted_iota(jnp.int32, shape, dim)


def split(value):
    high = value.astype(BF16)
    return high, (value - high.astype(F32)).astype(BF16)


def dot(left, right, dims=((1,), (0,))):
    return lax.dot_general(left, right, (dims, ((), ())), preferred_element_type=F32)


def dot_split(left, value):
    high, low = split(value)
    return dot(left, high) + dot(left, low)


def head_sum(value):
    feats = value.shape[1]
    same = (iota((feats, feats), 0) // HEAD_DIM) == (iota((feats, feats), 1) // HEAD_DIM)
    block = jnp.where(same, 1.0, 0.0).astype(BF16)
    high, low = split(value)
    return dot(high, block) + dot(low, block)


def row_of(ref):
    value = ref[...].astype(F32)
    return jnp.concatenate([value[at : at + 1] for at in range(value.shape[0])], axis=1)


def scores(hidden, query):
    raw = head_sum(hidden * query) * inv_root
    bent = jnp.tanh(raw / soft_cap)
    return bent, jnp.exp(soft_cap * bent)


def segment_rows(start):
    upper = jnp.where(iota((LANES, LANES), 0) <= iota((LANES, LANES), 1), 1.0, 0.0).astype(BF16)
    count = dot(start.astype(F32).astype(BF16), upper)
    rows, total = [], jnp.full((1, 1), -1.0, F32)
    for index in range(start.shape[0]):
        row = count[index : index + 1]
        rows.append(row + total)
        total = total + row[:, LANES - 1 :]
    return rows, total


def lead_mask(start):
    first = jnp.broadcast_to(start[0:1].astype(F32), (EDGE, LANES))
    before = jnp.where(iota((EDGE, LANES), 1) <= iota((EDGE, LANES), 0), first, 0.0)
    return jnp.where(jnp.sum(before, axis=1, keepdims=True) > 0.0, 0.0, 1.0)


def tail_mask(start):
    rows = start.shape[0]
    last = jnp.broadcast_to(start[rows - 1 : rows].astype(F32), (EDGE, LANES))
    after = jnp.where(iota((EDGE, LANES), 1) > iota((EDGE, LANES), 0) + (LANES - EDGE), last, 0.0)
    return jnp.where(jnp.sum(after, axis=1, keepdims=True) > 0.0, 0.0, 1.0)


def load_kernel(hidden_hbm, start_hbm, grad_hbm,
                back_ref, ahead_ref, hidden_ref, start_ref, rows_v, sem):
    pairs = [(start_hbm, start_ref), (hidden_hbm, hidden_ref)]
    copies = [pltpu.make_async_copy(*pair, sem.at[at]) for at, pair in enumerate(pairs)]
    for copy in copies:
        copy.start()
    bytes_, feats = hidden_ref.shape
    width = grad_hbm.shape[1]
    copies[0].wait()
    start = start_ref[...]
    last = jnp.sum(start) - 1
    group = pl.multiple_of((last // EDGE) * EDGE, EDGE)
    rows = pltpu.make_async_copy(grad_hbm.at[pl.ds(group, EDGE), :], rows_v, sem.at[2])
    rows.start()
    back_ref[:, feats:] = jnp.broadcast_to(lead_mask(start), (EDGE, LANES)).astype(BF16)
    ahead_ref[:EDGE, feats:] = jnp.broadcast_to(tail_mask(start), (EDGE, LANES)).astype(BF16)
    copies[1].wait()
    back_ref[:, :feats] = hidden_ref[:EDGE]
    ahead_ref[:EDGE, :feats] = hidden_ref[bytes_ - EDGE :]
    rows.wait()
    chosen = iota((EDGE, width), 0) == last - group
    row = jnp.sum(jnp.where(chosen, rows_v[...].astype(F32), 0.0), axis=0, keepdims=True)
    ahead_ref[EDGE:] = jnp.zeros((EDGE, feats + LANES), BF16)
    for at in range(width // feats):
        piece = row[:, at * feats : (at + 1) * feats]
        spread = jnp.where(iota((EDGE, feats), 0) == at, piece, 0.0)
        old = ahead_ref[EDGE:, :feats].astype(F32)
        ahead_ref[EDGE:, :feats] = (old + spread).astype(BF16)


def pool_kernel(hidden_ref, next_ref, start_ref, query_ref, low_ref, pooled_ref, denom_ref):
    bytes_, feats = hidden_ref.shape
    slots = low_ref.shape[0]
    query = row_of(query_ref)
    rows, last = segment_rows(start_ref[...])
    segment = jnp.concatenate(rows, axis=1).astype(jnp.int32)
    onehot = jnp.where(iota((slots, bytes_), 0) == segment, 1.0, 0.0).astype(BF16)
    hidden = hidden_ref[...].astype(F32)
    _, weight = scores(hidden, query)
    numer = dot_split(onehot, weight * hidden)
    denom = dot_split(onehot, weight)
    following = next_ref[:, :feats].astype(F32)
    mask = next_ref[:, feats : feats + 1].astype(F32)
    extra = scores(following, query)[1] * mask
    is_last = iota((slots, feats), 0) == last.astype(jnp.int32)
    denom = denom + jnp.where(is_last, jnp.sum(extra, axis=0, keepdims=True), 0.0)
    numer = numer + jnp.where(is_last, jnp.sum(extra * following, axis=0, keepdims=True), 0.0)
    live = denom > 0.0
    pooled = jnp.where(live, numer / jnp.where(live, denom, 1.0), 0.0)
    low_ref[...] = pooled.astype(BF16)
    pooled_ref[...] = pooled
    denom_ref[...] = denom


def spread_kernel(hidden_ref, prev_ref, start_ref, query_ref, pooled_ref, denom_ref,
                  onehot_ref, share_ref, delta_ref, slope_ref):
    bytes_, feats = hidden_ref.shape
    slots = pooled_ref.shape[0]
    query = row_of(query_ref)
    rows, _ = segment_rows(start_ref[...])
    columns = [jnp.transpose(jnp.broadcast_to(row, (LANES, LANES))) for row in rows]
    segment = jnp.concatenate(columns, axis=0).astype(jnp.int32)
    onehot = jnp.concatenate(
        [
            jnp.where(segment == iota((bytes_, LANES), 1) + offset, 1.0, 0.0).astype(BF16)
            for offset in range(0, slots, LANES)
        ],
        axis=1,
    )
    onehot_ref[...] = onehot
    hidden = hidden_ref[...].astype(F32)
    bent, weight = scores(hidden, query)
    before = prev_ref[:EDGE, :feats].astype(F32)
    part = scores(before, query)[1] * prev_ref[:EDGE, feats : feats + 1].astype(F32)
    lead = lead_mask(start_ref[...])
    own = weight[:EDGE] * lead
    first_denom = jnp.sum(part + own, axis=0, keepdims=True)
    first_numer = jnp.sum(part * before + own * hidden[:EDGE], axis=0, keepdims=True)
    full = first_denom > 0.0
    first_pooled = jnp.where(full, first_numer / jnp.where(full, first_denom, 1.0), 0.0)
    denom = dot_split(onehot, denom_ref[...])
    pooled = dot_split(onehot, pooled_ref[...])
    denom = jnp.concatenate([denom[:EDGE] + lead * first_denom, denom[EDGE:]], axis=0)
    pooled = jnp.concatenate([pooled[:EDGE] + lead * first_pooled, pooled[EDGE:]], axis=0)
    share = weight / denom
    share_ref[...] = share
    delta_ref[...] = hidden - pooled
    slope_ref[...] = share * (1.0 - bent * bent) * (inv_root * query)


def bytes_kernel(parts, *refs):
    recv_refs, (start_ref, onehot_ref, share_ref, delta_ref, slope_ref, out_ref) = (
        refs[:parts],
        refs[parts:],
    )
    slots = onehot_ref.shape[1]
    grad = recv_refs[0][...].astype(F32)
    for ref in recv_refs[1:]:
        grad = grad + ref[...].astype(F32)
    rows = dot_split(onehot_ref[...], grad[:slots])
    first = jnp.sum(grad[slots:], axis=0, keepdims=True)
    rows = jnp.concatenate([rows[:EDGE] + lead_mask(start_ref[...]) * first, rows[EDGE:]], axis=0)
    inner = head_sum(rows * delta_ref[...])
    out_ref[...] = (share_ref[...] * rows + slope_ref[...] * inner).astype(BF16)


def gather_parts(part_refs, full_ref):
    feats = part_refs[0].shape[1]
    place = lax.axis_index("mp")
    for index, ref in enumerate(part_refs):
        owner = pl.multiple_of((place ^ index) * feats, feats)
        full_ref[:, pl.ds(owner, feats)] = ref[...]


def outer_kernel(parts, scale, *refs):
    part_refs, grad_ref, out_refs = refs[:parts], refs[parts], refs[parts + 1 : -2]
    full_ref, terms_ref = refs[-2:]
    gather_parts(part_refs, full_ref)
    terms_ref[...] = dot(full_ref[...], grad_ref[...], ((0,), (0,))) * scale
    if len(out_refs) == 1:
        out_refs[0][...] = terms_ref[...].astype(out_refs[0].dtype)
        return
    place = lax.axis_index("seq")
    rows = out_refs[0].shape[0]
    for index, ref in enumerate(out_refs):
        owner = pl.multiple_of((place ^ index) * rows, rows)
        ref[...] = terms_ref[pl.ds(owner, rows), :].astype(ref.dtype)


def latent_kernel(parts, *refs):
    part_refs, (weight_ref, out_ref, full_ref) = refs[:parts], refs[parts:]
    gather_parts(part_refs, full_ref)
    out_ref[...] = dot(full_ref[...], weight_ref[...]).astype(BF16)


def partial_kernel(parts, grad_ref, prev_ref, *refs):
    piece_refs, out_refs, full_ref = refs[: -parts - 1], refs[-parts - 1 : -1], refs[-1]
    slots, width = grad_ref.shape
    feats = out_refs[0].shape[1]
    if len(piece_refs) == 1:
        full_ref[...] = piece_refs[0][...]
    else:
        rows = piece_refs[0].shape[0]
        spot = lax.axis_index("seq")
        for index, ref in enumerate(piece_refs):
            owner = pl.multiple_of((spot ^ index) * rows, rows)
            full_ref[pl.ds(owner, rows), :] = ref[...]
    last = prev_ref[EDGE:, :feats].astype(F32)
    row = jnp.concatenate([last[at : at + 1] for at in range(width // feats)], axis=1)
    row = jnp.where(iota((EDGE, width), 0) == 0, row, 0.0).astype(BF16)
    place = lax.axis_index("mp")
    for index, ref in enumerate(out_refs):
        owner = pl.multiple_of((place ^ index) * feats, feats)
        block = full_ref[pl.ds(owner, feats), :]
        ref[:slots] = dot(grad_ref[...], block, ((1,), (1,))).astype(BF16)
        ref[slots:] = dot(row, block, ((1,), (1,))).astype(BF16)


def call(kernel, out_shape, *args, flops=0, scratch=(), in_specs=None, limit=VMEM_LIMIT):
    if in_specs is None:
        in_specs = [pl.BlockSpec(memory_space=pltpu.VMEM)] * len(args)
    return pl.pallas_call(
        kernel,
        out_shape=out_shape,
        in_specs=in_specs,
        out_specs=jax.tree.map(lambda _: pl.BlockSpec(memory_space=pltpu.VMEM), out_shape),
        scratch_shapes=list(scratch),
        cost_estimate=pl.CostEstimate(flops=0, bytes_accessed=0, transcendentals=0),
        compiler_params=pltpu.CompilerParams(vmem_limit_bytes=limit),
    )(*args)


def shape(dims, dtype):
    return jax.ShapeDtypeStruct(dims, dtype)


VMEM = pl.BlockSpec(memory_space=pltpu.VMEM)
after = lax.optimization_barrier
HBM = pl.BlockSpec(memory_space=pltpu.HBM)


def shards(byte_hidden, patch_start, pool_query, in_weight, latent_grad):
    bytes_, feats = byte_hidden.shape
    slots, width = latent_grad.shape
    n_seq, n_mp = lax.axis_size("seq"), lax.axis_size("mp")
    latent_dim = feats * n_mp
    rows = latent_dim // n_seq
    staged = n_seq == 8

    def swap(value, step):
        return lax.ppermute(value, "mp", [(i, i ^ step) for i in range(n_mp)])

    def trade(value, step):
        return lax.ppermute(value, "seq", [(i, i ^ step) for i in range(n_seq)])

    arguments = (
        byte_hidden,
        patch_start.reshape(bytes_ // LANES, LANES),
        latent_grad,
    )
    query = pool_query.reshape(feats // LANES, LANES)
    back, ahead, byte_hidden, start = call(
        load_kernel,
        (
            shape((EDGE, feats + LANES), BF16),
            shape((2 * EDGE, feats + LANES), BF16),
            shape(byte_hidden.shape, BF16),
            shape(arguments[1].shape, jnp.int32),
        ),
        *arguments,
        in_specs=[HBM] * len(arguments),
        limit=VMEM_MOST,
        scratch=(
            pltpu.VMEM((EDGE, width), BF16),
            pltpu.SemaphoreType.DMA((len(arguments),)),
        ),
    )
    following = lax.ppermute(back, "seq", [(i, i - 1) for i in range(1, n_seq)])
    previous = lax.ppermute(ahead, "seq", [(i, i + 1) for i in range(n_seq - 1)])

    if staged:
        in_weight, _ = after((in_weight, back))
        pieces = [in_weight] + [None] * (n_seq - 1)
        for step in (1, 2, 4):
            pieces[step] = trade(in_weight, step)
        pieces[6] = trade(pieces[4], 2)
    else:
        pieces = [lax.all_gather(in_weight, "seq", axis=0, tiled=True)]

    low, pooled, denom = call(
        pool_kernel,
        (shape((slots, feats), BF16), shape((slots, feats), F32), shape((slots, feats), F32)),
        byte_hidden,
        following,
        start,
        query,
        flops=8 * bytes_ * slots * feats,
    )

    if staged:
        low, *pieces[1:3] = after((low, *pieces[1:3]))
        pieces[3] = trade(after((pieces[2], low))[0], 1)
    parts = [low]
    for step in reversed([1 << bit for bit in range(n_mp.bit_length() - 1)]):
        if staged and step == 1:
            parts[0], _ = after((parts[0], (pieces[4], pieces[3], previous)))
        parts = [part for held in parts for part in (held, swap(held, step))]
    onehot, share, delta, slope = call(
        spread_kernel,
        (shape((bytes_, slots), BF16),) + (shape((bytes_, feats), F32),) * 3,
        byte_hidden,
        previous,
        start,
        query,
        pooled,
        denom,
        flops=8 * bytes_ * slots * feats,
    )
    work = 2 * slots * width * latent_dim
    scale = 1.0 / math.sqrt(n_seq * slots)
    if staged:
        blocks = [shape((rows, width), BF16 if index % 2 else F32) for index in range(n_seq)]
    else:
        blocks = [shape((latent_dim, width), BF16)]
    terms = call(
        functools.partial(outer_kernel, n_mp, scale),
        tuple(blocks),
        *parts,
        latent_grad,
        flops=work,
        scratch=(pltpu.VMEM((slots, latent_dim), BF16), pltpu.VMEM((latent_dim, width), F32)),
    )
    if staged:
        fetched = {}
        fetched[7] = trade(terms[7], 1)
        pieces[5] = trade(pieces[4], 1)
        pieces[7] = trade(after((pieces[5], terms[0]))[0], 2)
        fetched[5] = trade(after((terms[5], fetched[7]))[0], 1)

    *partials, weight_full = call(
        functools.partial(partial_kernel, n_mp),
        (shape((slots + EDGE, feats), BF16),) * n_mp + (shape((latent_dim, width), BF16),),
        latent_grad,
        previous,
        *pieces,
        flops=work,
    )
    grads = [partials[0]] + [swap(partials[step], step) for step in range(1, n_mp)]

    if staged:
        fetched[6] = trade((terms[6] + fetched[7].astype(F32)).astype(BF16), 2)
        fetched[3] = trade(after((terms[3], weight_full, fetched[6]))[0], 1)
        pair = terms[4] + fetched[5].astype(F32) + fetched[6].astype(F32)
        fetched[4] = trade(pair.astype(BF16), 4)
        fetched[1] = trade(after((terms[1], fetched[5], grads[2], share))[0], 1)
        fetched[2] = trade((terms[2] + fetched[3].astype(F32)).astype(BF16), 2)
        grad_weight = terms[0] + fetched[1].astype(F32)
        for step in (4, 2):
            grad_weight = grad_weight + fetched[step].astype(F32)
    else:
        received = lax.all_to_all(terms[0], "seq", split_axis=0, concat_axis=0, tiled=True)
        grad_weight = received.reshape(n_seq, rows, width).astype(F32).sum(0)

    latent = call(
        functools.partial(latent_kernel, n_mp),
        shape((slots, width), BF16),
        *parts,
        weight_full,
        flops=work,
        scratch=(pltpu.VMEM((slots, latent_dim), BF16),),
    )
    grad_bytes = call(
        functools.partial(bytes_kernel, n_mp),
        shape((bytes_, feats), BF16),
        *grads,
        start,
        onehot,
        share,
        delta,
        slope,
        flops=4 * bytes_ * slots * feats,
    )
    return latent, grad_weight, grad_bytes


def solution(mesh):
    in_specs = (P("seq", "mp"), P("seq"), P("mp"), P("seq", "mp"), P("seq", "mp"))
    out_specs = (P("seq", "mp"), P("seq", "mp"), P("seq", "mp"))
    return jax.shard_map(shards, mesh=mesh, in_specs=in_specs, out_specs=out_specs, check_vma=False)
```
